32 devices in a mesh: dp: 16 (over z, x, core), tensor: 2 (over y).
Axes of the slice: x: 2, y: 2, z: 4, core: 2. Of those that a mesh axis runs over, the one named last changes fastest.
Arguments:
- hidden_in: bfloat16 [8192, 1280], P('dp'), may hold values from -0.16699219 to 0.16699219
- query_weight: bfloat16 [1280, 1280], P(None, 'tensor'), may hold values from -0.15625 to 0.15625
- key_weight: bfloat16 [1280, 1280], P(None, 'tensor'), may hold values from -0.15625 to 0.15625
- value_weight: bfloat16 [1280, 1280], P(None, 'tensor'), may hold values from -0.15625 to 0.15625
- out_weight: bfloat16 [1280, 1280], P('tensor'), may hold values from -0.15625 to 0.15625
- up_weight: bfloat16 [1280, 5120], P(None, 'tensor'), may hold values from -0.15625 to 0.15625
- gate_weight: bfloat16 [1280, 5120], P(None, 'tensor'), may hold values from -0.15625 to 0.15625
- down_weight: bfloat16 [5120, 1280], P('tensor'), may hold values from -0.078125 to 0.078125
- head_scale: float32 [1280], P('tensor'), may hold values from 0.5 to 2
- attention_rate: float32 [1280], replicated, may hold values from 0.1 to 0.5
- up_scale: float32 [5120], P('tensor'), may hold values from 0.5 to 2
- gate_scale: float32 [5120], P('tensor'), may hold values from 0.5 to 2
- swiglu_rate: float32 [1280], replicated, may hold values from 0.1 to 0.5
- teacher: bfloat16 [2048, 1280], P('dp'), may hold values from -0.16699219 to 0.16699219
- valid_mask: int32 [2048], P('dp'), may hold values from 0 to 1, as said below
- group_ids: int32 [16], P('dp'), may hold values from 0 to 15, as said below
Outputs:
- hidden_out: float32 [8192, 1280], P('dp')
- loss: float32 [], replicated
- grad_hidden: float32 [8192, 1280], P(('dp', 'tensor'))
- grad_query: float32 [1280, 1280], P('dp', 'tensor')
- grad_key: float32 [1280, 1280], P('dp', 'tensor')
- grad_value: float32 [1280, 1280], P('dp', 'tensor')
- grad_out: float32 [1280, 1280], P('tensor', 'dp')
- grad_up: float32 [1280, 5120], P('dp', 'tensor')
- grad_gate: float32 [1280, 5120], P('dp', 'tensor')
- grad_down: float32 [5120, 1280], P('tensor', 'dp')
- grad_head_scale: float32 [1280], P('tensor')
- grad_attention_rate: float32 [1280], replicated
- grad_up_scale: float32 [5120], P('tensor')
- grad_gate_scale: float32 [5120], P('tensor')
- grad_swiglu_rate: float32 [1280], replicated
The draws below stay inside these ranges and needn't reach their ends.
Inputs may be any that keep to these rules, and one draw needn't show every extreme that they name: `group_ids`: entry j is j // 1 or that number with its lowest bit flipped; the first entry, the last entry and entry 8 are the latter. `valid_mask`: the first token of every continuation is valid.
All inputs are finite; a program needn't handle non-finite values.
Results may differ from the reference program's by a relative error of at most 0.015.
Values may be sent and summed in bfloat16 or wider, within the bound.
No kernel may reach another device: no remote copies, remote signals or barrier semaphores. Data moves between devices by JAX's collectives and lax.ppermute only.
A program may use at most 256 MiB of HBM per device.

```python
import math
import jax
import jax.numpy as jnp
from jax import lax

D = 1280
HEADS = 20
HD = 64
FF = 5120
P_SIZE = 384
L = 128
CONT = 1
ROWS = 512
TOKENS = 8192
CTOKENS = 2048
N_DP = 16


def draw_group_ids(key, part):
    key = jax.random.fold_in(key, 11)
    count_all = N_DP * CONT
    index = jnp.arange(count_all, dtype=jnp.int32)
    store = index // CONT
    partner = store + 1 - 2 * (store % 2)
    picked = jax.random.randint(key, (count_all,), 0, 2, dtype=jnp.int32)
    forced = (index == 0) | (index == count_all - 1) | (index == count_all // 2)
    picked = jnp.where(forced, 1, picked)
    return jnp.where(picked == 1, partner, store).astype(jnp.int32)


def draw_valid_mask(key, part):
    key = jax.random.fold_in(key, 23)
    total = N_DP * CONT * L
    index = jnp.arange(total, dtype=jnp.int32)
    store = index // (CONT * L)
    position = index % L
    limit = 300 + 600 * store // max(N_DP - 1, 1)
    score = jax.random.randint(key, (total,), 0, 1000, dtype=jnp.int32)
    return jnp.where((score < limit) | (position == 0), 1, 0).astype(jnp.int32)


def block_scale(rng, shape, shards, low, largest):
    def one(dim, parts):
        heights = jax.random.uniform(jax.random.fold_in(jax.random.fold_in(rng, 6), dim), (parts,), jnp.float32, low / len(shards), largest / len(shards))
        return jnp.repeat(jnp.exp(heights), shape[dim] // parts).reshape((-1,) + (1,) * (len(shape) - dim - 1))

    factor_of = one(*shards[0])
    for cut in shards[1:]:
        factor_of = factor_of * one(*cut)
    return factor_of


def normal_values(rng, shape, width, most, cuts=(), kind=jnp.bfloat16):
    loudness = block_scale(rng, shape, cuts, -0.22, 0.18) if cuts else 1.0
    values = jax.random.normal(rng, shape, jnp.float32) * width * loudness
    return jnp.minimum(jnp.maximum(values, -most), most).astype(kind)


def setup_inputs(seed: int = 0) -> dict:
    arg_keys = jax.random.split(jax.random.key(seed), 17)
    return {
        "hidden_in": normal_values(arg_keys[0], (TOKENS, D), (D ** -0.5), 0.16699219, ((0, 16),)),
        "query_weight": normal_values(arg_keys[1], (D, D), D ** -0.5, 0.15625, ((1, 2),)),
        "key_weight": normal_values(arg_keys[2], (D, D), D ** -0.5, 0.15625, ((1, 2),)),
        "value_weight": normal_values(arg_keys[3], (D, D), D ** -0.5, 0.15625, ((1, 2),)),
        "out_weight": normal_values(arg_keys[4], (D, D), D ** -0.5, 0.15625, ((0, 2),)),
        "up_weight": normal_values(arg_keys[5], (D, FF), D ** -0.5, 0.15625, ((1, 2),)),
        "gate_weight": normal_values(arg_keys[6], (D, FF), D ** -0.5, 0.15625, ((1, 2),)),
        "down_weight": normal_values(arg_keys[7], (FF, D), FF ** -0.5, 0.078125, ((0, 2),)),
        "head_scale": jnp.clip(jnp.exp(math.log(2.0) - 1.3862944 * jax.random.uniform(arg_keys[8], (D,), jnp.float32) ** block_scale(arg_keys[8], (D,), ((0, 2),), -0.2, 0.2)), 0.5, 2.0),
        "attention_rate": jnp.clip(jax.random.uniform(arg_keys[9], (D,), jnp.float32, 0.1, 0.5), 0.1, 0.5),
        "up_scale": jnp.clip(jnp.exp(math.log(2.0) - 1.3862944 * jax.random.uniform(arg_keys[10], (FF,), jnp.float32) ** block_scale(arg_keys[10], (FF,), ((0, 2),), -0.2, 0.2)), 0.5, 2.0),
        "gate_scale": jnp.clip(jnp.exp(math.log(2.0) - 1.3862944 * jax.random.uniform(arg_keys[11], (FF,), jnp.float32) ** block_scale(arg_keys[11], (FF,), ((0, 2),), -0.2, 0.2)), 0.5, 2.0),
        "swiglu_rate": jnp.clip(jax.random.uniform(arg_keys[12], (D,), jnp.float32, 0.1, 0.5), 0.1, 0.5),
        "teacher": normal_values(arg_keys[13], (CTOKENS, D), (D ** -0.5), 0.16699219, ((0, 16),)),
        "valid_mask": draw_valid_mask(jax.random.fold_in(arg_keys[16], 71), 0),
        "group_ids": draw_group_ids(jax.random.fold_in(arg_keys[16], 71), 0),
    }


@jax.custom_vjp
def low(v):
    return lax.optimization_barrier(v.astype(jnp.bfloat16)).astype(jnp.float32)

@jax.custom_vjp
def low_back(v):
    return v

def low_keep(v):
    return (low(v), None)

def low_pass(kept, grad):
    return (grad,)

def back_keep(v):
    return (v, None)

def back_low(kept, grad):
    return (low(grad),)
low.defvjp(low_keep, low_pass)
low_back.defvjp(back_keep, back_low)
epsilon = 1e-06
exact_prec = lax.Precision.HIGHEST

def unit_rows(values):
    return values * lax.rsqrt(lax.optimization_barrier(jnp.sum(values * values, axis=-1, keepdims=True)) + epsilon)

def matmul(left, right):
    return jnp.dot(left, right, precision=exact_prec, preferred_element_type=jnp.float32)

def visible(rows, own_flags):
    keys = jnp.arange(2 * P_SIZE + CONT * L, dtype=jnp.int32)[None, :]
    rows = rows[:, None]
    in_prompt = rows < P_SIZE
    cont_row = jnp.maximum(rows - P_SIZE, 0) // L
    spot_row = jnp.maximum(rows - P_SIZE, 0) % L
    slots = jnp.arange(CONT, dtype=jnp.int32)[None, :]
    own_row = jnp.any((cont_row == slots) & own_flags[None, :], axis=1, keepdims=True)
    cont_key = jnp.maximum(keys - 2 * P_SIZE, 0) // L
    spot_key = jnp.maximum(keys - 2 * P_SIZE, 0) % L
    prompt_part = in_prompt & (keys <= rows)
    own_part = ~in_prompt & own_row & (keys < P_SIZE)
    other_part = ~in_prompt & ~own_row & (keys >= P_SIZE) & (keys < 2 * P_SIZE)
    cont_part = ~in_prompt & (keys >= 2 * P_SIZE) & (cont_key == cont_row) & (spot_key <= spot_row)
    return prompt_part | own_part | other_part | cont_part

def forward(xin, wq, wk, wv, wo, wu, wg, wd, sqk, rate_att, s_up, s_gate, rate_mlp, group_ids):
    total_rows = xin.shape[0]
    query_raw = low_back(matmul(xin, wq)).reshape(total_rows, HEADS, HD)
    key_raw = low_back(matmul(xin, wk)).reshape(total_rows, HEADS, HD)
    values = low(low_back(matmul(xin, wv))).reshape(N_DP, ROWS, HEADS, HD)
    scale_heads = sqk.reshape(HEADS, HD)
    queries = low(unit_rows(query_raw) * scale_heads).reshape(N_DP, ROWS, HEADS, HD)
    keys_all = low(unit_rows(key_raw) * scale_heads).reshape(N_DP, ROWS, HEADS, HD)

    def store_attention(store):
        partner = store + 1 - 2 * (store % 2)
        keys = jnp.concatenate([keys_all[store, :P_SIZE], keys_all[partner, :P_SIZE], keys_all[store, P_SIZE:]], 0)
        vals = jnp.concatenate([values[store, :P_SIZE], values[partner, :P_SIZE], values[store, P_SIZE:]], 0)
        own_flags = lax.dynamic_slice(group_ids, (store * CONT,), (CONT,)) == store
        scores = low_back(8.0 * jnp.einsum('qhe,khe->hqk', queries[store], keys, precision=exact_prec))
        mask = visible(jnp.arange(ROWS, dtype=jnp.int32), own_flags)
        scores = jnp.where(mask[None], scores, -1e+30)
        probs = low(jax.nn.softmax(scores, axis=-1))
        return jnp.einsum('hqk,khe->qhe', probs, vals, precision=exact_prec)
    mixed = lax.map(jax.checkpoint(store_attention), jnp.arange(N_DP, dtype=jnp.int32))
    attended = low(low_back(mixed.reshape(total_rows, D)))
    attn_val = low_back(matmul(attended, wo))
    hidden_one = unit_rows(xin + rate_att * (unit_rows(attn_val) - xin))
    one_low = low(hidden_one)
    up_val = low_back(matmul(one_low, wu))
    gate_val = low_back(matmul(one_low, wg))
    gate_arg = s_gate * math.sqrt(D) * gate_val
    inner = low(low_back(s_up * up_val * jax.nn.silu(gate_arg)))
    ffn_val = low_back(matmul(inner, wd))
    return unit_rows(hidden_one + rate_mlp * (unit_rows(ffn_val) - hidden_one))

def reference(hidden_in, query_weight, key_weight, value_weight, out_weight, up_weight, gate_weight, down_weight, head_scale, attention_rate, up_scale, gate_scale, swiglu_rate, teacher, valid_mask, group_ids):
    inputs = tuple((item.astype(jnp.float32) for item in (hidden_in, query_weight, key_weight, value_weight, out_weight, up_weight, gate_weight, down_weight, head_scale, attention_rate, up_scale, gate_scale, swiglu_rate)))
    teacher_f = teacher.astype(jnp.float32)
    valid_f = valid_mask.astype(jnp.float32)
    count = jnp.sum(valid_f)
    total_cont = N_DP * CONT * L

    def objective(xin, wq, wk, wv, wo, wu, wg, wd, sqk, rate_att, s_up, s_gate, rate_mlp):
        result = forward(xin, wq, wk, wv, wo, wu, wg, wd, sqk, rate_att, s_up, s_gate, rate_mlp, group_ids)
        tail = result.reshape(N_DP, ROWS, D)[:, P_SIZE:].reshape(total_cont, D)
        diff = tail - teacher_f
        total = jnp.sum(valid_f * lax.optimization_barrier(jnp.sum(diff * diff, axis=1)))
        return (total_cont * total / count, result)
    loss, pullback, result = jax.vjp(objective, *inputs, has_aux=True)
    grads = pullback(jnp.ones((), jnp.float32))
    return (result, loss, grads[0], grads[1], grads[2], grads[3], grads[4], grads[5], grads[6], grads[7], grads[8], grads[9], grads[10], grads[11], grads[12])
```

```python
import functools
import math

import jax
import jax.numpy as jnp
from jax import lax
from jax.experimental import pallas as pl
from jax.experimental.pallas import tpu as pltpu
from jax.sharding import PartitionSpec as P

D = 1280
HD = 64
P_SIZE = 384
L = 128
PAIR = 2 * HD
EPS = 1e-06
ROOT = math.sqrt(D)
BF = jnp.bfloat16
F32 = jnp.float32


def swap(value, axis, bit):
    count = lax.axis_size(axis)
    return lax.ppermute(value, axis, [(i, i ^ bit) for i in range(count)])


def settle(value):
    return lax.optimization_barrier(value)


def pair_sum(part):
    mine = settle(part.astype(BF))
    return mine.astype(F32) + swap(mine, "tensor", 1).astype(F32)


def sum_all(value):
    bit = 1
    while bit < lax.axis_size("dp"):
        value = value + swap(value, "dp", bit)
        bit *= 2
    return value


def take(value, index, axis):
    return lax.dynamic_index_in_dim(value, index, axis, keepdims=False)


def fold(value, axis, bit):
    mine = (lax.axis_index("dp") // bit) % 2
    sent = take(value, 1 - mine, axis).astype(BF)
    return take(value, mine, axis).astype(F32) + swap(sent, "dp", bit).astype(F32)


def scatter_sum(grad):
    count = lax.axis_size("dp")
    rows, width = grad.shape
    far = count // 4
    if far > 4:
        return lax.psum_scatter(grad, "dp", scatter_dimension=0, tiled=True)
    value = grad.reshape(far, 2, 2, rows // count, width)
    value = fold(value, 2, 1)
    value = fold(value, 1, 2)
    place = lax.axis_index("dp") // 4
    total = take(value, place, 0)
    low = value.astype(BF)
    for step in range(1, far):
        sent = take(low, (place + step) % far, 0)
        got = lax.ppermute(sent, "dp", [(i, (i + 4 * step) % count) for i in range(count)])
        total = total + got.astype(F32)
    return total


def inverse_norm(values):
    return lax.rsqrt(jnp.sum(values * values, axis=-1, keepdims=True) + EPS)


def norm_back(grad, unit, inverse):
    return inverse * (grad - unit * jnp.sum(grad * unit, axis=-1, keepdims=True))


def head_sums(values):
    rows = lax.broadcasted_iota(jnp.int32, (PAIR, PAIR), 0) // HD
    cols = lax.broadcasted_iota(jnp.int32, (PAIR, PAIR), 1) // HD
    ones = jnp.where(rows == cols, 1.0, 0.0).astype(BF)
    high = values.astype(BF)
    low = (values - high.astype(F32)).astype(BF)
    return jnp.dot(high, ones, preferred_element_type=F32) + jnp.dot(
        low, ones, preferred_element_type=F32
    )


def project_kernel(has_query, *refs):
    if has_query:
        x_ref, wq_ref, wk_ref, wv_ref, scale_ref, q_ref, k_ref, v_ref, qr_ref, kr_ref = refs
    else:
        x_ref, wk_ref, wv_ref, scale_ref, k_ref, v_ref, kr_ref = refs
    x = x_ref[...]

    def normed(weight_ref, raw_ref, out_ref):
        raw = jnp.dot(x, weight_ref[...], preferred_element_type=F32)
        raw_ref[...] = raw
        for start in range(0, raw.shape[1], PAIR):
            part = raw[:, start : start + PAIR]
            unit = part * lax.rsqrt(head_sums(part * part) + EPS)
            out_ref[:, start : start + PAIR] = (
                unit * scale_ref[:, start : start + PAIR]
            ).astype(BF)

    normed(wk_ref, kr_ref, k_ref)
    v_ref[...] = jnp.dot(x, wv_ref[...], preferred_element_type=F32).astype(BF)
    if has_query:
        normed(wq_ref, qr_ref, q_ref)


def project(x, weights, scale):
    rows, width = x.shape[0], scale.shape[1]
    has_query = len(weights) == 3
    low = jax.ShapeDtypeStruct((rows, width), BF)
    full = jax.ShapeDtypeStruct((rows, width), F32)
    outs = (low, low, low, full, full) if has_query else (low, low, full)
    return pl.pallas_call(
        functools.partial(project_kernel, has_query),
        out_shape=outs,
        compiler_params=pltpu.CompilerParams(vmem_limit_bytes=40 * 2**20),
        cost_estimate=pl.CostEstimate(
            flops=2 * rows * D * width * len(weights),
            bytes_accessed=2 * D * width * len(weights) + 2 * rows * D + 14 * rows * width,
            transcendentals=0,
        ),
    )(x, *weights, scale)


def halves(value):
    first = lax.broadcasted_iota(jnp.int32, value.shape, 1) < HD
    zero = jnp.zeros_like(value)
    return jnp.concatenate([jnp.where(first, value, zero), jnp.where(first, zero, value)], 0)


def merge(value):
    rows = value.shape[0] // 2
    first = lax.broadcasted_iota(jnp.int32, (rows, PAIR), 1) < HD
    return jnp.where(first, value[:rows], value[rows:])


def weights_of(queries, keys, offset):
    scores = 8.0 * lax.dot_general(
        queries, keys, (((1,), (1,)), ((), ())), preferred_element_type=F32
    )
    rows = queries.shape[0] // 2
    row = lax.broadcasted_iota(jnp.int32, scores.shape, 0)
    row = jnp.where(row >= rows, row - rows, row)
    col = lax.broadcasted_iota(jnp.int32, scores.shape, 1)
    expo = jnp.where(col <= row + offset, jnp.exp(scores), 0.0)
    return expo * (1.0 / jnp.sum(expo, axis=1, keepdims=True))


def attend_kernel(offset, q_ref, k_ref, v_ref, out_ref):
    for start in range(0, q_ref.shape[1], PAIR):
        cols = slice(start, start + PAIR)
        probs = weights_of(halves(q_ref[:, cols]), k_ref[:, cols], offset).astype(BF)
        out = jnp.dot(probs, v_ref[:, cols], preferred_element_type=F32)
        out_ref[:, cols] = merge(out).astype(BF)


def attend(queries, keys, values, offset):
    rows, width = queries.shape
    count = keys.shape[0]
    return pl.pallas_call(
        functools.partial(attend_kernel, offset),
        out_shape=jax.ShapeDtypeStruct((rows, width), BF),
        compiler_params=pltpu.CompilerParams(vmem_limit_bytes=40 * 2**20),
        cost_estimate=pl.CostEstimate(
            flops=8 * rows * count * width,
            bytes_accessed=4 * (rows + count) * width,
            transcendentals=rows * count * width // HD,
        ),
    )(queries, keys, values)


def attend_back_kernel(
    offset, q_ref, k_ref, v_ref, d_ref, qr_ref, kr_ref, scale_ref, dq_ref, dk_ref, dv_ref, ds_ref
):
    def raw_back(grad, raw, scale):
        inverse = lax.rsqrt(head_sums(raw * raw) + EPS)
        unit = raw * inverse
        scaled = grad * scale
        back = inverse * (scaled - unit * head_sums(scaled * unit))
        return back.astype(BF), jnp.sum(grad * unit, axis=0, keepdims=True)

    for start in range(0, q_ref.shape[1], PAIR):
        cols = slice(start, start + PAIR)
        queries = halves(q_ref[:, cols])
        keys, values = k_ref[:, cols], v_ref[:, cols]
        grads = halves(d_ref[:, cols])
        scale = scale_ref[:, cols]
        probs = weights_of(queries, keys, offset)
        d_probs = lax.dot_general(
            grads, values, (((1,), (1,)), ((), ())), preferred_element_type=F32
        )
        delta = jnp.sum(d_probs * probs, axis=1, keepdims=True)
        d_scores = (probs * (d_probs - delta)).astype(BF)
        d_query = 8.0 * merge(jnp.dot(d_scores, keys, preferred_element_type=F32))
        d_keys = 8.0 * lax.dot_general(
            d_scores, queries, (((0,), (0,)), ((), ())), preferred_element_type=F32
        )
        dv_ref[:, cols] = lax.dot_general(
            probs.astype(BF), grads, (((0,), (0,)), ((), ())), preferred_element_type=F32
        ).astype(BF)
        dq_ref[:, cols], by_query = raw_back(d_query, qr_ref[:, cols], scale)
        dk_ref[:, cols], by_key = raw_back(d_keys, kr_ref[:, cols], scale)
        ds_ref[:, cols] = by_query + by_key


def attend_back(queries, keys, values, grads, query_raw, key_raw, scale, offset):
    rows, width = queries.shape
    count = keys.shape[0]
    return pl.pallas_call(
        functools.partial(attend_back_kernel, offset),
        out_shape=(
            jax.ShapeDtypeStruct((rows, width), BF),
            jax.ShapeDtypeStruct((count, width), BF),
            jax.ShapeDtypeStruct((count, width), BF),
            jax.ShapeDtypeStruct((1, width), F32),
        ),
        compiler_params=pltpu.CompilerParams(vmem_limit_bytes=40 * 2**20),
        cost_estimate=pl.CostEstimate(
            flops=20 * rows * count * width,
            bytes_accessed=12 * (rows + count) * width,
            transcendentals=rows * count * width // HD,
        ),
    )(queries, keys, values, grads, query_raw, key_raw, scale)


def dot(left, right):
    return jnp.dot(left, right, preferred_element_type=F32)


def dot_nt(left, right):
    return lax.dot_general(left, right, (((1,), (1,)), ((), ())), preferred_element_type=F32)


def dot_tn(left, right):
    return lax.dot_general(left, right, (((0,), (0,)), ((), ())), preferred_element_type=F32)


def swiglu(low, up_weight, gate_weight, up_scale, gate_scale):
    up_val = dot(low, up_weight)
    gate_val = dot(low, gate_weight)
    arg = gate_scale * ROOT * gate_val
    sigma = jax.nn.sigmoid(arg)
    swish = arg * sigma
    return up_val, gate_val, arg, sigma, swish, (up_scale * up_val * swish).astype(BF)


def swiglu_back(d_inner, parts, up_scale, gate_scale):
    up_val, gate_val, arg, sigma, swish, inner = parts
    d_up = (d_inner * up_scale * swish).astype(BF)
    d_arg = d_inner * up_scale * up_val * sigma * (1.0 + arg * (1.0 - sigma))
    d_gate = (d_arg * gate_scale * ROOT).astype(BF)
    return d_up, d_arg, d_gate


def mix(old, sums, rate):
    inverse_in = inverse_norm(sums)
    unit_in = sums * inverse_in
    mixed = old + rate * (unit_in - old)
    inverse_out = inverse_norm(mixed)
    return mixed * inverse_out, unit_in, inverse_in, inverse_out


def local(
    hidden_in,
    query_weight,
    key_weight,
    value_weight,
    out_weight,
    up_weight,
    gate_weight,
    down_weight,
    head_scale,
    attention_rate,
    up_scale,
    gate_scale,
    swiglu_rate,
    teacher,
    valid_mask,
    group_ids,
):
    count_dp = lax.axis_size("dp")
    me = lax.axis_index("dp")
    side = lax.axis_index("tensor")
    local_width = query_weight.shape[1]
    own = group_ids[0] == me
    valid_f = valid_mask.astype(F32)
    scale = head_scale.reshape(1, local_width)

    valid_count = sum_all(jnp.sum(valid_f, keepdims=True))[0]
    x_prompt, x_cont = hidden_in[:P_SIZE], hidden_in[P_SIZE:]
    x_other = swap(x_prompt, "dp", 1)
    q_all, k_all, v_all, q_raw, k_raw = project(
        hidden_in, (query_weight, key_weight, value_weight), scale
    )
    k_other, v_other, k_raw_other = project(x_other, (key_weight, value_weight), scale)

    def seen(mine, other):
        return jnp.concatenate([jnp.where(own, mine[:P_SIZE], other), mine[P_SIZE:]], 0)

    x_seen = seen(hidden_in, x_other)
    k_seen = seen(k_all, k_other)
    v_seen = seen(v_all, v_other)
    k_raw_seen = seen(k_raw, k_raw_other)
    q_cont = q_all[P_SIZE:]

    att = attend(q_cont, k_seen, v_seen, P_SIZE)
    x_cont_f = x_cont.astype(F32)
    attn_sum = pair_sum(dot(att, out_weight))
    one, attn_unit, attn_inv, one_inv = mix(x_cont_f, attn_sum, attention_rate)
    one_b = one.astype(BF)
    parts = swiglu(one_b, up_weight, gate_weight, up_scale, gate_scale)
    up_val, gate_val, arg, sigma, swish, inner = parts
    ffn_sum = pair_sum(dot(inner, down_weight))
    out, ffn_unit, ffn_inv, two_inv = mix(one, ffn_sum, swiglu_rate)
    diff = out - teacher.astype(F32)
    local_loss = jnp.sum(valid_f * jnp.sum(diff * diff, axis=1), keepdims=True)
    total_cont = count_dp * valid_mask.shape[0]
    factor = total_cont / valid_count
    grad_two = 2.0 * factor * valid_f[:, None] * diff
    dmix_two = norm_back(grad_two, out, two_inv)
    rate_mlp_grad = jnp.sum(dmix_two * (ffn_unit - one), axis=0)
    d_ffn = norm_back(dmix_two * swiglu_rate, ffn_unit, ffn_inv).astype(BF)
    d_inner = dot_nt(d_ffn, down_weight)
    d_up, d_arg, d_gate = swiglu_back(d_inner, parts, up_scale, gate_scale)
    up_scale_grad = jnp.sum(d_inner * up_val * swish, axis=0)
    gate_scale_grad = jnp.sum(d_arg * ROOT * gate_val, axis=0)
    d_one = (1.0 - swiglu_rate) * dmix_two + pair_sum(
        dot_nt(d_up, up_weight) + dot_nt(d_gate, gate_weight)
    )
    dmix_one = norm_back(d_one, one, one_inv)
    rate_att_grad = jnp.sum(dmix_one * (attn_unit - x_cont_f), axis=0)
    d_attn = norm_back(dmix_one * attention_rate, attn_unit, attn_inv).astype(BF)
    d_att = dot_nt(d_attn, out_weight).astype(BF)
    out_grad = scatter_sum(dot_tn(d_attn, att)).T
    d_query, d_key, d_value, head_grad = attend_back(
        q_cont, k_seen, v_seen, d_att, q_raw[P_SIZE:], k_raw_seen, scale, P_SIZE
    )
    value_grad = scatter_sum(dot_tn(x_seen, d_value))
    key_grad = scatter_sum(dot_tn(x_seen, d_key))
    query_grad = scatter_sum(dot_tn(x_cont, d_query))

    far = count_dp // 4
    if far <= 4:
        group = D // far
        start = (me // 4) * group

        def gathered(value):
            got = [value]
            for step in range(1, far):
                pairs = [(i, (i + 4 * step) % count_dp) for i in range(count_dp)]
                got.append(lax.ppermute(value, "dp", pairs))
            return jnp.concatenate(got, 0)

        ones = gathered(one_b)
        d_ffns = gathered(d_ffn)
        g_parts = swiglu(ones, up_weight, gate_weight, up_scale, gate_scale)
        g_up, g_arg, g_gate = swiglu_back(
            dot_nt(d_ffns, down_weight), g_parts, up_scale, gate_scale
        )
        ones_part = lax.dynamic_slice_in_dim(ones, start, group, 1)
        d_ffns_part = lax.dynamic_slice_in_dim(d_ffns, start, group, 1)

        def folded(grad):
            grad = grad.reshape(2, 2, group // 4, grad.shape[1])
            return fold(fold(grad, 1, 1), 0, 2)

        up_grad = folded(dot_tn(ones_part, g_up))
        gate_grad = folded(dot_tn(ones_part, g_gate))
        down_grad = folded(dot_tn(d_ffns_part, g_parts[5])).T
    else:
        up_grad = scatter_sum(dot_tn(one_b, d_up))
        gate_grad = scatter_sum(dot_tn(one_b, d_gate))
        down_grad = scatter_sum(dot_tn(d_ffn, inner)).T

    d_rows = (
        dot_nt(d_key, key_weight) + dot_nt(d_value, value_weight)
    )
    d_rows = jnp.concatenate(
        [d_rows[:P_SIZE], d_rows[P_SIZE:] + dot_nt(d_query, query_weight)], 0
    )
    share = d_rows.shape[0] // 2
    d_low = settle(d_rows.astype(BF)).reshape(2, share, D)
    d_share = take(d_low, side, 0).astype(F32) + swap(
        take(d_low, 1 - side, 0), "tensor", 1
    ).astype(F32)
    row = side * share + jnp.arange(share, dtype=jnp.int32)[:, None]
    is_prompt = row < P_SIZE
    kept = jnp.where(is_prompt & ~own, 0.0, d_share)
    sent = jnp.where(is_prompt & ~own, d_share, 0.0)
    residual = jnp.concatenate(
        [jnp.zeros((P_SIZE, D), F32), dmix_one * (1.0 - attention_rate)], 0
    )
    residual = lax.dynamic_slice_in_dim(residual, side * share, share, 0)
    grad_hidden = residual + kept + swap(sent.astype(BF), "dp", 1).astype(F32)

    att_p = attend(q_all[:P_SIZE], k_all[:P_SIZE], v_all[:P_SIZE], 0)
    attn_sum_p = pair_sum(dot(att_p, out_weight))
    one_p = mix(x_prompt.astype(F32), attn_sum_p, attention_rate)[0]
    inner_p = swiglu(one_p.astype(BF), up_weight, gate_weight, up_scale, gate_scale)[5]
    ffn_sum_p = pair_sum(dot(inner_p, down_weight))
    out_p = mix(one_p, ffn_sum_p, swiglu_rate)[0]
    hidden_out = jnp.concatenate([out_p, out], 0)

    middle = (up_scale_grad, gate_scale_grad, rate_mlp_grad, local_loss)
    middle = sum_all(jnp.concatenate(middle))
    last = sum_all(jnp.concatenate([rate_att_grad, head_grad[0]]))
    units = up_weight.shape[1]
    loss = total_cont * middle[2 * units + D] / valid_count
    return (
        hidden_out,
        loss,
        grad_hidden,
        query_grad,
        key_grad,
        value_grad,
        out_grad,
        up_grad,
        gate_grad,
        down_grad,
        last[D:],
        last[:D],
        middle[:units],
        middle[units : 2 * units],
        middle[2 * units : 2 * units + D],
    )


def solution(mesh):
    placed = (
        P("dp", None),
        P(None, "tensor"),
        P(None, "tensor"),
        P(None, "tensor"),
        P("tensor", None),
        P(None, "tensor"),
        P(None, "tensor"),
        P("tensor", None),
        P("tensor"),
        P(),
        P("tensor"),
        P("tensor"),
        P(),
        P("dp", None),
        P("dp"),
        P("dp"),
    )
    return jax.shard_map(
        local,
        mesh=mesh,
        in_specs=placed,
        out_specs=(
            P("dp", None),
            P(),
            P(("dp", "tensor"), None),
            P("dp", "tensor"),
            P("dp", "tensor"),
            P("dp", "tensor"),
            P("tensor", "dp"),
            P("dp", "tensor"),
            P("dp", "tensor"),
            P("tensor", "dp"),
            P("tensor"),
            P(),
            P("tensor"),
            P("tensor"),
            P(),
        ),
        check_vma=False,
    )
```

```python
import functools
import math

import jax
import jax.numpy as jnp
from jax import lax
from jax.experimental import pallas as pl
from jax.experimental.pallas import tpu as pltpu
from jax.sharding import PartitionSpec as P

D = 1280
HD = 64
P_SIZE = 384
L = 128
PAIR = 2 * HD
EPS = 1e-06
ROOT = math.sqrt(D)
BF = jnp.bfloat16
F32 = jnp.float32
MIB = 2**20
GAINS = 16
OWN, CORE, PLACE_X, PLACE_FAR, SIDE = range(5)


def swap(value, axis, bit):
    count = lax.axis_size(axis)
    return lax.ppermute(value, axis, [(i, i ^ bit) for i in range(count)])


def sum_all(value):
    bit = 1
    while bit < lax.axis_size("dp"):
        value = value + swap(value, "dp", bit)
        bit *= 2
    return value


def dot(left, right):
    return jnp.dot(left, right, preferred_element_type=F32)


def dot_nt(left, right):
    return lax.dot_general(left, right, (((1,), (1,)), ((), ())), preferred_element_type=F32)


def dot_tn(left, right):
    return lax.dot_general(left, right, (((0,), (0,)), ((), ())), preferred_element_type=F32)


def inverse_norm(values):
    return lax.rsqrt(jnp.sum(values * values, axis=-1, keepdims=True) + EPS)


def norm_back(grad, unit, inverse):
    return inverse * (grad - unit * jnp.sum(grad * unit, axis=-1, keepdims=True))


def mix(old, mine, other, rate):
    sums = mine.astype(F32) + other.astype(F32)
    inverse_in = inverse_norm(sums)
    unit_in = sums * inverse_in
    mixed = old + rate * (unit_in - old)
    inverse_out = inverse_norm(mixed)
    return mixed * inverse_out, unit_in, inverse_in, inverse_out


def call(kernel, outs, ins, flops, scratch=(), vmem=40, smem=0):
    moved = sum(math.prod(v.shape) * v.dtype.itemsize for v in (*ins, *outs))
    return pl.pallas_call(
        kernel,
        out_shape=tuple(outs),
        in_specs=[pl.BlockSpec(memory_space=pltpu.SMEM)] * smem
        + [pl.BlockSpec(memory_space=pltpu.VMEM)] * (len(ins) - smem),
        out_specs=tuple(pl.BlockSpec(memory_space=pltpu.VMEM) for _ in outs),
        scratch_shapes=list(scratch),
        compiler_params=pltpu.CompilerParams(vmem_limit_bytes=vmem * MIB),
        cost_estimate=pl.CostEstimate(flops=flops, bytes_accessed=moved, transcendentals=0),
    )(*ins)


def shape(rows, cols, kind):
    return jax.ShapeDtypeStruct((rows, cols), kind)


def head_sums(values):
    rows = lax.broadcasted_iota(jnp.int32, (PAIR, PAIR), 0) // HD
    cols = lax.broadcasted_iota(jnp.int32, (PAIR, PAIR), 1) // HD
    ones = jnp.where(rows == cols, 1.0, 0.0).astype(BF)
    high = values.astype(BF)
    low = (values - high.astype(F32)).astype(BF)
    return dot(high, ones) + dot(low, ones)


def unit_heads(raw):
    inverse = lax.rsqrt(head_sums(raw * raw) + EPS)
    return raw * inverse, inverse


def halves(value):
    first = lax.broadcasted_iota(jnp.int32, value.shape, 1) < HD
    zero = jnp.zeros_like(value)
    return jnp.concatenate([jnp.where(first, value, zero), jnp.where(first, zero, value)], 0)


def merge(value):
    rows = value.shape[0] // 2
    first = lax.broadcasted_iota(jnp.int32, (rows, PAIR), 1) < HD
    return jnp.where(first, value[:rows], value[rows:])


def weights_of(queries, keys, offset):
    scores = 8.0 * dot_nt(queries, keys)
    rows = queries.shape[0] // 2
    row = lax.broadcasted_iota(jnp.int32, scores.shape, 0)
    row = jnp.where(row >= rows, row - rows, row)
    col = lax.broadcasted_iota(jnp.int32, scores.shape, 1)
    expo = jnp.where(col <= row + offset, jnp.exp(scores), 0.0)
    return expo * (1.0 / jnp.sum(expo, axis=1, keepdims=True))


def attention_body(x, offset, wq_ref, wk_ref, wv_ref, wo_ref, scale_ref, outs):
    att_ref, part_ref, v_ref, qr_ref, kr_ref = outs
    kr_ref[...] = dot(x, wk_ref[...])
    v_ref[...] = dot(x, wv_ref[...]).astype(BF)
    qr_ref[...] = dot(x[offset:], wq_ref[...])
    for start in range(0, wq_ref.shape[1], PAIR):
        cols = slice(start, start + PAIR)
        scale = scale_ref[:, cols]
        keys = (unit_heads(kr_ref[:, cols])[0] * scale).astype(BF)
        queries = (unit_heads(qr_ref[:, cols])[0] * scale).astype(BF)
        probs = weights_of(halves(queries), keys, offset).astype(BF)
        att_ref[:, cols] = merge(dot(probs, v_ref[:, cols])).astype(BF)
    part_ref[...] = dot(att_ref[...], wo_ref[...]).astype(BF)


def seen_rows(info_ref, hidden_ref, other_ref):
    own = info_ref[OWN] == 1
    prompt = jnp.where(own, hidden_ref[:P_SIZE], other_ref[...])
    return jnp.concatenate([prompt, hidden_ref[P_SIZE:]], 0)


def cont_kernel(info_ref, hidden_ref, other_ref, wq_ref, wk_ref, wv_ref, wo_ref, scale_ref, *outs):
    x = seen_rows(info_ref, hidden_ref, other_ref)
    attention_body(x, P_SIZE, wq_ref, wk_ref, wv_ref, wo_ref, scale_ref, outs)


def prompt_kernel(hidden_ref, wq_ref, wk_ref, wv_ref, wo_ref, scale_ref, part_ref, *scratch):
    x = hidden_ref[:P_SIZE]
    att_ref, v_ref, qr_ref, kr_ref = scratch
    attention_body(
        x, 0, wq_ref, wk_ref, wv_ref, wo_ref, scale_ref, (att_ref, part_ref, v_ref, qr_ref, kr_ref)
    )


def cont_attention(info, hidden, other, weights, scale):
    rows, width = hidden.shape[0], scale.shape[1]
    outs = (
        shape(L, width, BF),
        shape(L, D, BF),
        shape(rows, width, BF),
        shape(L, width, F32),
        shape(rows, width, F32),
    )
    flops = 4 * rows * D * width + 4 * L * D * width + 8 * L * rows * width
    return call(cont_kernel, outs, (info, hidden, other, *weights, scale), flops, smem=1)


def prompt_attention(hidden, weights, scale):
    width = scale.shape[1]
    scratch = [
        pltpu.VMEM((P_SIZE, width), BF),
        pltpu.VMEM((P_SIZE, width), BF),
        pltpu.VMEM((P_SIZE, width), F32),
        pltpu.VMEM((P_SIZE, width), F32),
    ]
    flops = 8 * P_SIZE * D * width + 8 * P_SIZE * P_SIZE * width
    return call(
        prompt_kernel, (shape(P_SIZE, D, BF),), (hidden, *weights, scale), flops, scratch
    )[0]


def swiglu(low, up_weight, gate_weight, up_scale, gate_scale):
    return swiglu_of(dot(low, up_weight), dot(low, gate_weight), up_scale, gate_scale)


def swiglu_of(up_val, gate_val, up_scale, gate_scale):
    arg = gate_scale * ROOT * gate_val
    sigma = 1.0 / (1.0 + jnp.exp(-arg))
    swish = arg * sigma
    return up_val, gate_val, arg, sigma, swish


def swiglu_back(d_inner, parts, up_scale, gate_scale):
    up_val, gate_val, arg, sigma, swish = parts
    d_up = d_inner * up_scale * swish
    d_arg = d_inner * up_scale * up_val * sigma * (1.0 + arg * (1.0 - sigma))
    return d_up.astype(BF), d_arg, (d_arg * gate_scale * ROOT).astype(BF)


def ffn_kernel(save, mine, other, x, rate, up_w, gate_w, down_w, up_s, gate_s, *rest):
    if save:
        one_ref, part_ref, low_ref, up_ref, gate_ref, acc = rest
    else:
        one_ref, part_ref, low_ref, acc = rest
    step = pl.program_id(0)

    @pl.when(step == 0)
    def _():
        one = mix(x[...].astype(F32), mine[...], other[...], rate[...])[0]
        one_ref[...] = one
        low_ref[...] = one.astype(BF)
        acc[...] = jnp.zeros_like(acc)

    parts = swiglu(low_ref[...], up_w[...], gate_w[...], up_s[...], gate_s[...])
    if save:
        up_ref[...] = parts[0]
        gate_ref[...] = parts[1]
    inner = (up_s[...] * parts[0] * parts[4]).astype(BF)
    acc[...] += dot(inner, down_w[...])

    @pl.when(step == pl.num_programs(0) - 1)
    def _():
        part_ref[...] = acc[...].astype(BF)


def whole(rows, cols, row_block=0):
    return pl.BlockSpec((rows, cols), lambda j: (row_block, 0))


def tiles(rows, tile):
    return pl.BlockSpec((rows, tile), lambda j: (0, j))


def swiglu_specs(tile):
    return [
        tiles(D, tile),
        tiles(D, tile),
        pl.BlockSpec((tile, D), lambda j: (j, 0)),
        tiles(1, tile),
        tiles(1, tile),
    ]


def ffn(save, mine, other, hidden, rate, weights, tile=512):
    rows = mine.shape[0]
    units = weights[0].shape[1]
    outs = [shape(rows, D, F32), shape(rows, D, BF)]
    out_specs = [whole(rows, D), whole(rows, D)]
    scratch = [pltpu.VMEM((rows, D), F32)]
    if save:
        outs += [shape(rows, D, BF), shape(rows, units, F32), shape(rows, units, F32)]
        out_specs += [whole(rows, D), tiles(rows, tile), tiles(rows, tile)]
    else:
        scratch = [pltpu.VMEM((rows, D), BF)] + scratch
    return pl.pallas_call(
        functools.partial(ffn_kernel, save),
        grid=(units // tile,),
        out_shape=tuple(outs),
        in_specs=[
            whole(rows, D),
            whole(rows, D),
            whole(rows, D, P_SIZE // rows if save else 0),
            whole(1, D),
            *swiglu_specs(tile),
        ],
        out_specs=tuple(out_specs),
        scratch_shapes=scratch,
        compiler_params=pltpu.CompilerParams(
            vmem_limit_bytes=40 * MIB, dimension_semantics=("arbitrary",)
        ),
        cost_estimate=pl.CostEstimate(
            flops=6 * rows * D * units,
            bytes_accessed=6 * D * units + 12 * rows * D + 8 * rows * units,
            transcendentals=rows * units,
        ),
    )(mine, other, hidden, rate, *weights)


def ffn_back_kernel(
    mine,
    other,
    one,
    rate,
    teacher,
    valid,
    up_v,
    gate_v,
    up_w,
    gate_w,
    down_w,
    up_s,
    gate_s,
    out_ref,
    low_ref,
    dmix_ref,
    rate_ref,
    loss_ref,
    up_ref,
    gate_ref,
    part_ref,
    acc,
):
    step = pl.program_id(0)

    @pl.when(step == 0)
    def _():
        old = one[...]
        out, unit, inverse_in, inverse_out = mix(old, mine[...], other[...], rate[...])
        out_ref[...] = out
        diff = out - teacher[...].astype(F32)
        weighted = valid[...] * diff
        by_row = jnp.sum(weighted * diff, axis=1, keepdims=True)
        loss_ref[...] = jnp.sum(by_row, axis=0, keepdims=True)
        dmix = norm_back(2.0 * weighted, out, inverse_out)
        dmix_ref[...] = dmix
        rate_ref[...] = jnp.sum(dmix * (unit - old), axis=0, keepdims=True)
        low_ref[...] = norm_back(dmix * rate[...], unit, inverse_in).astype(BF)
        acc[...] = jnp.zeros_like(acc)

    d_inner = dot_nt(low_ref[...], down_w[...])
    parts = swiglu_of(up_v[...], gate_v[...], up_s[...], gate_s[...])
    d_up, d_arg, d_gate = swiglu_back(d_inner, parts, up_s[...], gate_s[...])
    up_ref[...] = jnp.sum(d_inner * parts[0] * parts[4], axis=0, keepdims=True)
    gate_ref[...] = jnp.sum(d_arg * ROOT * parts[1], axis=0, keepdims=True)
    acc[...] += dot_nt(d_up, up_w[...]) + dot_nt(d_gate, gate_w[...])

    @pl.when(step == pl.num_programs(0) - 1)
    def _():
        part_ref[...] = acc[...].astype(BF)


def ffn_back(mine, other, one, rate, teacher, valid, up_val, gate_val, weights, tile=512):
    rows = mine.shape[0]
    units = weights[0].shape[1]
    return pl.pallas_call(
        ffn_back_kernel,
        grid=(units // tile,),
        out_shape=(
            shape(rows, D, F32),
            shape(rows, D, BF),
            shape(rows, D, F32),
            shape(1, D, F32),
            shape(1, 1, F32),
            shape(1, units, F32),
            shape(1, units, F32),
            shape(rows, D, BF),
        ),
        in_specs=[
            whole(rows, D),
            whole(rows, D),
            whole(rows, D),
            whole(1, D),
            whole(rows, D),
            whole(rows, 1),
            tiles(rows, tile),
            tiles(rows, tile),
            *swiglu_specs(tile),
        ],
        out_specs=(
            whole(rows, D),
            whole(rows, D),
            whole(rows, D),
            whole(1, D),
            whole(1, 1),
            tiles(1, tile),
            tiles(1, tile),
            whole(rows, D),
        ),
        scratch_shapes=[pltpu.VMEM((rows, D), F32)],
        compiler_params=pltpu.CompilerParams(
            vmem_limit_bytes=40 * MIB, dimension_semantics=("arbitrary",)
        ),
        cost_estimate=pl.CostEstimate(
            flops=6 * rows * D * units,
            bytes_accessed=6 * D * units + 24 * rows * D + 8 * rows * units,
            transcendentals=rows * units,
        ),
    )(mine, other, one, rate, teacher, valid, up_val, gate_val, *weights)


def split_blocks(blocks, first, send_ref, keep_ref, start):
    size = blocks[0].shape[0]
    for j in range(0, len(blocks), 2):
        rows = slice(start + j // 2 * size, start + (j // 2 + 1) * size)
        even, odd = blocks[j], blocks[j + 1]
        send_ref[rows] = jnp.where(first, odd, even)
        keep_ref[rows] = jnp.where(first, even, odd)


def ffn_grad_kernel(split, info, ones, d_ffns, ones_t, d_ffns_t, *rest):
    up_w, gate_w, down_w, up_s, gate_s = rest[:5]
    parts = swiglu(ones[...], up_w[...], gate_w[...], up_s[...], gate_s[...])
    d_inner = dot_nt(d_ffns[...], down_w[...])
    d_up, _, d_gate = swiglu_back(d_inner, parts, up_s[...], gate_s[...])
    inner = (up_s[...] * parts[0] * parts[4]).astype(BF)
    pairs = ((ones_t, d_up), (ones_t, d_gate), (d_ffns_t, inner))
    for i, (left, right) in enumerate(pairs):
        grad = dot(left[...], right)
        if split:
            size = grad.shape[0] // 4
            grad = grad.astype(BF)
            blocks = [grad[j * size : (j + 1) * size] for j in range(4)]
            split_blocks(blocks, info[CORE] == 0, rest[5], rest[6], i * 2 * size)
        else:
            rest[5 + i][...] = grad


def ffn_grad(split, info, ones, d_ffns, ones_t, d_ffns_t, weights, tile=256):
    rows, group = ones.shape[0], ones_t.shape[0]
    units = weights[0].shape[1]
    if split:
        outs = [shape(3 * group // 2, units, BF)] * 2
    else:
        outs = [shape(group, units, F32)] * 3
    return pl.pallas_call(
        functools.partial(ffn_grad_kernel, split),
        grid=(units // tile,),
        out_shape=tuple(outs),
        in_specs=[
            pl.BlockSpec(memory_space=pltpu.SMEM),
            whole(rows, D),
            whole(rows, D),
            whole(group, rows),
            whole(group, rows),
            *swiglu_specs(tile),
        ],
        out_specs=tuple(tiles(out.shape[0], tile) for out in outs),
        compiler_params=pltpu.CompilerParams(
            vmem_limit_bytes=40 * MIB, dimension_semantics=("arbitrary",)
        ),
        cost_estimate=pl.CostEstimate(
            flops=6 * rows * (D + group) * units,
            bytes_accessed=6 * D * units + 4 * rows * D + 6 * group * units,
            transcendentals=rows * units,
        ),
    )(info, ones, d_ffns, ones_t, d_ffns_t, *weights)


def attention_back_kernel(split, *refs):
    info, hidden, other_x, d_mine, d_other, dmix_two, one, a_mine, a_other = refs[:9]
    rate_two, rate_one, att, wo, v_ref, qr_ref, kr_ref, scale_ref = refs[9:17]
    mlp_grad, up_grad, gate_grad, loss, count = refs[17:22]
    dq_ref, dk_ref, dv_ref, residual_ref = refs[22:26]
    gains, d_att = refs[-2:]
    outs = refs[26:-2]
    width = scale_ref.shape[1]
    x = seen_rows(info, hidden, other_x)
    x_cont = hidden[P_SIZE:]
    old = x_cont.astype(F32)
    _, unit_in, inverse_in, inverse_out = mix(old, a_mine[...], a_other[...], rate_one[...])
    d_one = d_mine[...].astype(F32) + d_other[...].astype(F32)
    d_one = d_one + (1.0 - rate_two[...]) * dmix_two[...]
    dmix = norm_back(d_one, one[...], inverse_out)
    residual_ref[...] = dmix * (1.0 - rate_one[...])
    att_grad = jnp.sum(dmix * (unit_in - old), axis=0, keepdims=True)
    d_attn = norm_back(dmix * rate_one[...], unit_in, inverse_in).astype(BF)
    d_att[...] = dot_nt(d_attn, wo[...]).astype(BF)

    gains[...] = jnp.zeros_like(gains)
    place = 0
    for value in (mlp_grad[...], att_grad, up_grad[...], gate_grad[...]):
        for start in range(0, value.shape[1], width):
            gains[place : place + 1] = value[:, start : start + width]
            place += 1

    def raw_back(grad, unit, inverse, scale):
        scaled = grad * scale
        back = inverse * (scaled - unit * head_sums(scaled * unit))
        return back.astype(BF), jnp.sum(grad * unit, axis=0, keepdims=True)

    for start in range(0, width, PAIR):
        cols = slice(start, start + PAIR)
        scale = scale_ref[:, cols]
        q_unit, q_inverse = unit_heads(qr_ref[:, cols])
        k_unit, k_inverse = unit_heads(kr_ref[:, cols])
        queries = halves((q_unit * scale).astype(BF))
        keys = (k_unit * scale).astype(BF)
        grads = halves(d_att[:, cols])
        probs = weights_of(queries, keys, P_SIZE)
        d_probs = dot_nt(grads, v_ref[:, cols])
        delta = jnp.sum(d_probs * probs, axis=1, keepdims=True)
        d_scores = (probs * (d_probs - delta)).astype(BF)
        d_query = 8.0 * merge(dot(d_scores, keys))
        d_keys = 8.0 * dot_tn(d_scores, queries)
        dv_ref[:, cols] = dot_tn(probs.astype(BF), grads).astype(BF)
        dq_ref[:, cols], by_query = raw_back(d_query, q_unit, q_inverse, scale)
        dk_ref[:, cols], by_key = raw_back(d_keys, k_unit, k_inverse, scale)
        gains[place : place + 1, cols] = by_query + by_key

    col = lax.broadcasted_iota(jnp.int32, (1, width), 1)
    last = jnp.zeros((1, width), F32)
    for i, value in enumerate((loss[...], count[...])):
        high = value.astype(BF).astype(F32)
        last = jnp.where(col == 2 * i, high, last)
        last = jnp.where(col == 2 * i + 1, value - high, last)
    gains[place + 1 : place + 2] = last

    products = ((x, dv_ref[...]), (x, dk_ref[...]), (x_cont, dq_ref[...]), (d_attn, att[...]))
    for i, (left, right) in enumerate(products):
        grad = dot_tn(left, right)
        if split:
            size = grad.shape[0] // 16
            grad = grad.astype(BF)
            blocks = [grad[j * size : (j + 1) * size] for j in range(16)]
            split_blocks(blocks, info[CORE] == 0, outs[0], outs[1], i * 8 * size)
        else:
            outs[i][...] = grad
    if split:
        low = gains[...].astype(BF)
        for ref in outs:
            ref[4 * D // 2 :] = low
    else:
        outs[4][...] = gains[...]


def attention_back(split, ins, width, rows):
    outs = [shape(L, width, BF), shape(rows, width, BF), shape(rows, width, BF), shape(L, D, F32)]
    if split:
        outs += [shape(2 * D + GAINS, width, BF)] * 2
    else:
        outs += [shape(D, width, F32)] * 4 + [shape(GAINS, width, F32)]
    scratch = [pltpu.VMEM((GAINS, width), F32), pltpu.VMEM((L, width), BF)]
    flops = 20 * L * rows * width + 4 * (rows + L) * D * width + 4 * L * D * width
    return call(
        functools.partial(attention_back_kernel, split), outs, ins, flops, scratch, smem=1
    )


def fold_x_kernel(matrices, info, keep, got, send_ref, keep_ref):
    size = keep.shape[0] // (matrices * 8)
    size -= size % 16
    first = info[PLACE_X] == 0
    total = (keep[...].astype(F32) + got[...].astype(F32)).astype(BF)
    for m in range(matrices):
        start = m * 8 * size
        blocks = [total[start + j * size : start + (j + 1) * size] for j in range(8)]
        split_blocks(blocks, first, send_ref, keep_ref, m * 4 * size)
    for ref in (send_ref, keep_ref):
        ref[matrices * 4 * size :] = total[matrices * 8 * size :]


def fold_far_kernel(matrices, far, info, keep, got, *outs):
    size = (keep.shape[0] - GAINS) // (matrices * far)
    total = (keep[...].astype(F32) + got[...].astype(F32)).astype(BF)
    for step in range(far):
        place = (info[PLACE_FAR] + step) % far
        for m in range(matrices):
            block = total[m * far * size : (m * far + 1) * size]
            for j in range(1, far):
                start = (m * far + j) * size
                block = jnp.where(place == j, total[start : start + size], block)
            outs[step][m * size : (m + 1) * size] = block
        outs[step][matrices * size :] = total[matrices * far * size :]


def finish_kernel(far, tokens, info, *refs):
    parts, outs = refs[:far], refs[far:]
    size = (parts[0].shape[0] - GAINS) // 4
    gains = [part[4 * size :].astype(F32) for part in parts]
    total = jnp.zeros_like(gains[0])
    for j in range(far):
        for step in range(far):
            here = (info[PLACE_FAR] + far - step) % far == j
            total = total + jnp.where(here, gains[step], 0.0)
    outs[4][...] = total
    count = total[13:14, 2:3] + total[13:14, 3:4]
    factor = tokens / count
    outs[5][...] = factor
    for m in range(4):
        grad = parts[0][m * size : (m + 1) * size].astype(F32)
        for part in parts[1:]:
            grad = grad + part[m * size : (m + 1) * size].astype(F32)
        grad = grad * factor
        outs[m][...] = grad.T if m == 3 else grad


def finish_units_kernel(keep, got, factor, up_ref, gate_ref, down_ref):
    total = (keep[...].astype(F32) + got[...].astype(F32)) * factor[...]
    size = total.shape[0] // 3
    up_ref[...] = total[:size]
    gate_ref[...] = total[size : 2 * size]
    down_ref[...] = total[2 * size :].T


def fold_units_kernel(info, keep, got, send_ref, keep_ref):
    size = keep.shape[0] // 6
    total = (keep[...].astype(F32) + got[...].astype(F32)).astype(BF)
    blocks = [total[j * size : (j + 1) * size] for j in range(6)]
    split_blocks(blocks, info[PLACE_X] == 0, send_ref, keep_ref, 0)


def rows_kernel(info, dq, dk, dv, wq, wk, wv, send_ref, keep_ref):
    half = send_ref.shape[0]
    prompt = dot_nt(dk[...], wk[...]) + dot_nt(dv[...], wv[...])
    top = prompt[:half].astype(BF)
    low = jnp.concatenate(
        [prompt[half:P_SIZE], prompt[P_SIZE:] + dot_nt(dq[...], wq[...])], 0
    ).astype(BF)
    first = info[SIDE] == 0
    send_ref[...] = jnp.where(first, low, top)
    keep_ref[...] = jnp.where(first, top, low)


def share_kernel(info, keep, got, residual, kept_ref, sent_ref):
    half = keep.shape[0]
    total = keep[...].astype(F32) + got[...].astype(F32)
    row = lax.broadcasted_iota(jnp.int32, (half, 1), 0) + info[SIDE] * half
    away = (row < P_SIZE) & (info[OWN] == 0)
    sent_ref[...] = jnp.where(away, total, 0.0).astype(BF)
    kept_ref[...] = jnp.where(away, 0.0, total)
    kept_ref[half - L :] += jnp.where(info[SIDE] == 1, residual[...], 0.0)


def last_mix_kernel(mine, other, one, rate, out, result):
    step = pl.program_id(0)
    last = pl.num_programs(0) - 1

    @pl.when(step < last)
    def _():
        result[...] = mix(one[...], mine[...], other[...], rate[...])[0]

    @pl.when(step == last)
    def _():
        result[...] = out[...]


def last_mix(mine, other, one, rate, out):
    steps = P_SIZE // L
    block = pl.BlockSpec((L, D), lambda i: (jnp.minimum(i, steps - 1), 0))
    return pl.pallas_call(
        last_mix_kernel,
        grid=(steps + 1,),
        out_shape=shape(P_SIZE + L, D, F32),
        in_specs=[block, block, block, whole(1, D), whole(L, D)],
        out_specs=pl.BlockSpec((L, D), lambda i: (i, 0)),
        compiler_params=pltpu.CompilerParams(
            vmem_limit_bytes=32 * MIB, dimension_semantics=("arbitrary",)
        ),
        cost_estimate=pl.CostEstimate(
            flops=20 * P_SIZE * D, bytes_accessed=14 * P_SIZE * D, transcendentals=0
        ),
    )(mine, other, one, rate, out)


def local(
    hidden_in,
    query_weight,
    key_weight,
    value_weight,
    out_weight,
    up_weight,
    gate_weight,
    down_weight,
    head_scale,
    attention_rate,
    up_scale,
    gate_scale,
    swiglu_rate,
    teacher,
    valid_mask,
    group_ids,
):
    count_dp = lax.axis_size("dp")
    far = count_dp // 4
    split = far <= 4
    me = lax.axis_index("dp")
    rows = hidden_in.shape[0]
    width = query_weight.shape[1]
    units = up_weight.shape[1]
    scale = head_scale.reshape(1, width)
    rate_one = attention_rate.reshape(1, D)
    rate_two = swiglu_rate.reshape(1, D)
    valid = valid_mask.astype(F32)
    own = (group_ids[0] == me).astype(jnp.int32)
    info = jnp.stack([own, me % 2, me // 2 % 2, me // 4, lax.axis_index("tensor")])
    info = info.astype(jnp.int32)
    qkvo = (query_weight, key_weight, value_weight, out_weight)
    ffn_weights = (
        up_weight,
        gate_weight,
        down_weight,
        up_scale.reshape(1, units),
        gate_scale.reshape(1, units),
    )

    other_x = swap(hidden_in[:P_SIZE], "dp", 1)
    att, a_mine, values, query_raw, key_raw = cont_attention(
        info, hidden_in, other_x, qkvo, scale
    )
    a_other = swap(a_mine, "tensor", 1)
    one, m_mine, one_low, up_val, gate_val = ffn(
        True, a_mine, a_other, hidden_in, rate_one, ffn_weights
    )
    m_other = swap(m_mine, "tensor", 1)
    out, d_ffn, dmix_two, mlp_grad, local_loss, up_scale_grad, gate_scale_grad, d_mine = ffn_back(
        m_mine,
        m_other,
        one,
        rate_two,
        teacher,
        valid.reshape(L, 1),
        up_val,
        gate_val,
        ffn_weights,
    )
    d_other = swap(d_mine, "tensor", 1)
    back = attention_back(
        split,
        (
            info,
            hidden_in,
            other_x,
            d_mine,
            d_other,
            dmix_two,
            one,
            a_mine,
            a_other,
            rate_two,
            rate_one,
            att,
            out_weight,
            values,
            query_raw,
            key_raw,
            scale,
            mlp_grad,
            up_scale_grad,
            gate_scale_grad,
            local_loss,
            jnp.sum(valid).reshape(1, 1),
        ),
        width,
        rows,
    )
    d_query, d_key, d_value, residual = back[:4]

    p_mine = prompt_attention(hidden_in, qkvo, scale)
    p_other = swap(p_mine, "tensor", 1)
    one_p, mp_mine = ffn(False, p_mine, p_other, hidden_in, rate_one, ffn_weights)
    mp_other = swap(mp_mine, "tensor", 1)
    hidden_out = last_mix(mp_mine, mp_other, one_p, rate_two, out)

    total_cont = count_dp * valid_mask.shape[0]
    if split:
        send, keep = back[4:]
        got = swap(send, "dp", 1)
        half = shape(D + GAINS, width, BF)
        send, keep = call(
            functools.partial(fold_x_kernel, 4), (half, half), (info, keep, got), 0, smem=1
        )
        got = swap(send, "dp", 2)
        parts = call(
            functools.partial(fold_far_kernel, 4, far),
            [shape(D // far + GAINS, width, BF)] * far,
            (info, keep, got),
            0,
            smem=1,
        )
        arrived = [parts[0]]
        for step in range(1, far):
            pairs = [(i, (i + 4 * step) % count_dp) for i in range(count_dp)]
            arrived.append(lax.ppermute(parts[step], "dp", pairs))
        mine = D // count_dp
        value_grad, key_grad, query_grad, out_grad, gains, factor = call(
            functools.partial(finish_kernel, far, total_cont),
            [shape(mine, width, F32)] * 3
            + [shape(width, mine, F32), shape(GAINS, width, F32), shape(1, 1, F32)],
            (info, *arrived),
            0,
            smem=1,
        )
        group = D // far
        start = me // 4 * group
        lanes = [[i * 4 + j for i in range(far)] for j in range(4)]
        ones = lax.all_gather(one_low, "dp", axis=0, tiled=True, axis_index_groups=lanes)
        d_ffns = lax.all_gather(d_ffn, "dp", axis=0, tiled=True, axis_index_groups=lanes)
        ones_t = lax.dynamic_slice_in_dim(ones, start, group, 1).T
        d_ffns_t = lax.dynamic_slice_in_dim(d_ffns, start, group, 1).T
        send, keep = ffn_grad(True, info, ones, d_ffns, ones_t, d_ffns_t, ffn_weights)
        got = swap(send, "dp", 1)
        half = shape(3 * group // 4, units, BF)
        send, keep = call(fold_units_kernel, (half, half), (info, keep, got), 0, smem=1)
        got = swap(send, "dp", 2)
        up_grad, gate_grad, down_grad = call(
            finish_units_kernel,
            (shape(mine, units, F32), shape(mine, units, F32), shape(units, mine, F32)),
            (keep, got, factor),
            0,
        )
    else:
        gains = sum_all(back[8])
        factor = total_cont / (gains[13:14, 2:3] + gains[13:14, 3:4])

        def scattered(grad):
            return factor * lax.psum_scatter(grad, "dp", scatter_dimension=0, tiled=True)

        value_grad, key_grad, query_grad = (scattered(grad) for grad in back[4:7])
        out_grad = scattered(back[7]).T
        up_grad, gate_grad, down_grad = (
            scattered(grad)
            for grad in ffn_grad(
                False, info, one_low, d_ffn, one_low.T, d_ffn.T, ffn_weights
            )
        )
        down_grad = down_grad.T

    half = shape(rows // 2, D, BF)
    send, keep = call(
        rows_kernel,
        (half, half),
        (info, d_query, d_key, d_value, query_weight, key_weight, value_weight),
        6 * rows * D * width,
        smem=1,
    )
    got = swap(send, "tensor", 1)
    kept, sent = call(
        share_kernel, (shape(rows // 2, D, F32), half), (info, keep, got, residual), 0, smem=1
    )
    grad_hidden = factor * (kept + swap(sent, "dp", 1).astype(F32))

    loss = factor[0, 0] * (gains[13, 0] + gains[13, 1])
    gains = gains * factor
    flat = gains[:13].reshape(-1)
    return (
        hidden_out,
        loss,
        grad_hidden,
        query_grad,
        key_grad,
        value_grad,
        out_grad,
        up_grad,
        gate_grad,
        down_grad,
        gains[12],
        flat[D : 2 * D],
        flat[2 * D : 2 * D + units],
        flat[2 * D + units : 2 * D + 2 * units],
        flat[:D],
    )


def solution(mesh):
    placed = (
        P("dp", None),
        P(None, "tensor"),
        P(None, "tensor"),
        P(None, "tensor"),
        P("tensor", None),
        P(None, "tensor"),
        P(None, "tensor"),
        P("tensor", None),
        P("tensor"),
        P(),
        P("tensor"),
        P("tensor"),
        P(),
        P("dp", None),
        P("dp"),
        P("dp"),
    )
    return jax.shard_map(
        local,
        mesh=mesh,
        in_specs=placed,
        out_specs=(
            P("dp", None),
            P(),
            P(("dp", "tensor"), None),
            P("dp", "tensor"),
            P("dp", "tensor"),
            P("dp", "tensor"),
            P("tensor", "dp"),
            P("dp", "tensor"),
            P("dp", "tensor"),
            P("tensor", "dp"),
            P("tensor"),
            P(),
            P("tensor"),
            P("tensor"),
            P(),
        ),
        check_vma=False,
    )
```

```python
import functools
import math

import jax
import jax.numpy as jnp
from jax import lax
from jax.experimental import pallas as pl
from jax.experimental.pallas import tpu as pltpu
from jax.sharding import PartitionSpec as P

D = 1280
HD = 64
P_SIZE = 384
L = 128
PAIR = 2 * HD
EPS = 1e-06
ROOT = math.sqrt(D)
BF = jnp.bfloat16
F32 = jnp.float32
MIB = 2**20
GAINS = 16
OWN, CORE, PLACE_X, PLACE_FAR, SIDE = range(5)


def swap(value, axis, bit):
    count = lax.axis_size(axis)
    return lax.ppermute(value, axis, [(i, i ^ bit) for i in range(count)])


def sum_all(value):
    bit = 1
    while bit < lax.axis_size("dp"):
        value = value + swap(value, "dp", bit)
        bit *= 2
    return value


def dot(left, right):
    return jnp.dot(left, right, preferred_element_type=F32)


def dot_nt(left, right):
    return lax.dot_general(left, right, (((1,), (1,)), ((), ())), preferred_element_type=F32)


def dot_tn(left, right):
    return lax.dot_general(left, right, (((0,), (0,)), ((), ())), preferred_element_type=F32)


def inverse_norm(values):
    return lax.rsqrt(jnp.sum(values * values, axis=-1, keepdims=True) + EPS)


def norm_back(grad, unit, inverse):
    return inverse * (grad - unit * jnp.sum(grad * unit, axis=-1, keepdims=True))


def mix(old, sums, rate):
    inverse_in = inverse_norm(sums)
    unit_in = sums * inverse_in
    mixed = old + rate * (unit_in - old)
    inverse_out = inverse_norm(mixed)
    return mixed * inverse_out, unit_in, inverse_in, inverse_out


def both(mine, other):
    return mine.astype(F32) + other.astype(F32)


class Line:
    def __init__(self, last=None):
        self.last = last

    def call(
        self, kernel, outs, ins, *, flops=0, scratch=(), vmem=12, smem=0, away=(), loose=(), sent=(), aliases=()
    ):
        moved = sum(math.prod(v.shape) * v.dtype.itemsize for v in (*ins, *outs))
        count = len(ins)
        places = [pltpu.SMEM] * smem + [pltpu.VMEM] * (count - smem)
        ins = list(ins)
        for i in loose:
            places[i] = pl.ANY
        for i in away:
            places[i] = pl.ANY
            ins[i] = pltpu.with_memory_space_constraint(ins[i], pltpu.HBM)
        out_places = [pl.ANY if i in sent else pltpu.VMEM for i in range(len(outs))]
        body = kernel
        if self.last is not None:
            places.append(pl.ANY)
            ins.append(self.last)

            def body(*refs):
                kernel(*refs[:count], *refs[count + 1 :])

        done = pl.pallas_call(
            body,
            out_shape=tuple(outs),
            in_specs=[pl.BlockSpec(memory_space=place) for place in places],
            out_specs=tuple(pl.BlockSpec(memory_space=place) for place in out_places),
            scratch_shapes=list(scratch),
            input_output_aliases=dict(aliases),
            compiler_params=pltpu.CompilerParams(vmem_limit_bytes=vmem * MIB),
            cost_estimate=pl.CostEstimate(flops=flops, bytes_accessed=moved, transcendentals=0),
        )(*ins)
        self.last = done[0]
        return done


def halves_of(values):
    half = len(values) // 2
    return values[:half], values[half:]


def section(usual, work, *ins):
    shapes = jax.eval_shape(work, *ins)
    return lax.cond(
        usual, work, lambda *_: jax.tree.map(lambda v: jnp.zeros(v.shape, v.dtype), shapes), *ins
    )


class Copies:
    def __init__(self, sems):
        self.sems, self.copies = sems, []

    def start(self, source, target):
        copy = pltpu.make_async_copy(source, target, self.sems.at[len(self.copies)])
        copy.start()
        self.copies.append(copy)
        return copy

    def wait(self):
        for copy in self.copies:
            copy.wait()


class Tiles:
    def __init__(self, come, groups, ahead=2):
        self.come, self.groups, self.ahead, self.going = come, groups, ahead, []
        for _ in range(ahead):
            self.more()

    def more(self):
        if len(self.going) < len(self.groups):
            group = self.groups[len(self.going)]
            self.going.append([self.come.start(source, target) for source, target in group])

    def wait(self, i):
        for copy in self.going[i]:
            copy.wait()
        self.more()


def distant(rows, cols, kind):
    return pltpu.HBM((rows, cols), kind)


def vmem(rows, cols, kind):
    return pltpu.VMEM((rows, cols), kind)


def sems(count):
    return pltpu.SemaphoreType.DMA((count,))


def near(rows, cols, kind):
    return pltpu.VMEM((rows, cols), kind)


def fetch(pairs, sems):
    copies = [pltpu.make_async_copy(a, b, sems.at[i]) for i, (a, b) in enumerate(pairs)]
    for copy in copies:
        copy.start()
    return copies


def shape(rows, cols, kind):
    return jax.ShapeDtypeStruct((rows, cols), kind)


def head_sums(values):
    rows = lax.broadcasted_iota(jnp.int32, (PAIR, PAIR), 0) // HD
    cols = lax.broadcasted_iota(jnp.int32, (PAIR, PAIR), 1) // HD
    ones = jnp.where(rows == cols, 1.0, 0.0).astype(BF)
    high = values.astype(BF)
    low = (values - high.astype(F32)).astype(BF)
    return dot(high, ones) + dot(low, ones)


def unit_heads(raw):
    inverse = lax.rsqrt(head_sums(raw * raw) + EPS)
    return raw * inverse, inverse


def halves(value):
    first = lax.broadcasted_iota(jnp.int32, value.shape, 1) < HD
    zero = jnp.zeros_like(value)
    return jnp.concatenate([jnp.where(first, value, zero), jnp.where(first, zero, value)], 0)


def merge(value):
    rows = value.shape[0] // 2
    first = lax.broadcasted_iota(jnp.int32, (rows, PAIR), 1) < HD
    return jnp.where(first, value[:rows], value[rows:])


def weights_of(queries, keys, offset):
    scores = 8.0 * dot_nt(queries, keys)
    rows = queries.shape[0] // 2
    row = lax.broadcasted_iota(jnp.int32, scores.shape, 0)
    row = jnp.where(row >= rows, row - rows, row)
    col = lax.broadcasted_iota(jnp.int32, scores.shape, 1)
    expo = jnp.where(col <= row + offset, jnp.exp(scores), 0.0)
    return expo * (1.0 / jnp.sum(expo, axis=1, keepdims=True))


def attention_body(x, offset, weights, scale_ref, refs, arrived, ready):
    wq_ref, wk_ref, wv_ref, wo_ref = weights
    att_ref, part_ref, v_ref, qr_ref, kr_ref = refs
    arrived(0)
    kr_ref[...] = dot(x, wk_ref[...])
    ready(0)
    arrived(1)
    v_ref[...] = dot(x, wv_ref[...]).astype(BF)
    ready(1)
    arrived(2)
    qr_ref[...] = dot(x[offset:], wq_ref[...])
    ready(2)
    for start in range(0, wq_ref.shape[1], PAIR):
        cols = slice(start, start + PAIR)
        scale = scale_ref[:, cols]
        keys = (unit_heads(kr_ref[:, cols])[0] * scale).astype(BF)
        queries = (unit_heads(qr_ref[:, cols])[0] * scale).astype(BF)
        probs = weights_of(halves(queries), keys, offset).astype(BF)
        att_ref[:, cols] = merge(dot(probs, v_ref[:, cols])).astype(BF)
    ready(3)
    arrived(3)
    part_ref[...] = dot(att_ref[...], wo_ref[...]).astype(BF)


def cont_kernel(info, hidden, other, wq, wk, wv, wo, scale, *refs):
    part, att_far, x_far, v_far, qr_far, kr_far, wq_near, wk_near, wv_near, wo_near = refs[:10]
    own_x, other_x, x_ref, att, v_ref, qr, kr, in_sems, out_sems = refs[10:]
    come, go = Copies(in_sems), Copies(out_sems)
    arrive = Tiles(
        come,
        (
            ((hidden, own_x), (other.at[:P_SIZE], other_x)),
            ((wk, wk_near),),
            ((wv, wv_near),),
            ((wq, wq_near),),
            ((wo, wo_near),),
        ),
    )
    arrive.wait(0)
    x_ref[:P_SIZE] = jnp.where(info[OWN] == 1, own_x[:P_SIZE], other_x[...])
    x_ref[P_SIZE:] = own_x[P_SIZE:]
    go.start(x_ref, x_far)
    results = ((kr, kr_far), (v_ref, v_far), (qr, qr_far), (att, att_far))
    attention_body(
        x_ref[...],
        P_SIZE,
        (wq_near, wk_near, wv_near, wo_near),
        scale,
        (att, part, v_ref, qr, kr),
        lambda i: arrive.wait(1 + i),
        lambda i: go.start(*results[i]),
    )
    go.wait()


def cont_attention(line, info, hidden, other, weights, scale):
    rows, width = hidden.shape[0], scale.shape[1]
    outs = [
        shape(L, D, BF),
        distant(L, width, BF),
        distant(rows, D, BF),
        distant(rows, width, BF),
        distant(L, width, F32),
        distant(rows, width, F32),
    ] + [near(*weight.shape, BF) for weight in weights]
    scratch = [
        vmem(rows, D, BF),
        vmem(P_SIZE, D, BF),
        vmem(rows, D, BF),
        vmem(L, width, BF),
        vmem(rows, width, BF),
        vmem(L, width, F32),
        vmem(rows, width, F32),
        sems(6),
        sems(5),
    ]
    flops = 4 * rows * D * width + 4 * L * D * width + 8 * L * rows * width
    return line.call(
        cont_kernel,
        outs,
        (info, hidden, other, *weights, scale),
        flops=flops,
        scratch=scratch,
        vmem=28,
        smem=1,
        away=(1, 3, 4, 5, 6),
        loose=(2,),
        sent=range(1, 6),
    )


def prompt_kernel(hidden, wq, wk, wv, wo, scale, up, gate, down, *refs):
    part, up_near, gate_near, down_near, x_ref, att, v_ref, qr, kr, in_sems = refs
    come = Copies(in_sems)
    come.start(hidden.at[:P_SIZE], x_ref)
    for source, target in ((up, up_near), (gate, gate_near), (down, down_near)):
        come.start(source, target)
    come.copies[0].wait()
    attention_body(
        x_ref[...],
        0,
        (wq, wk, wv, wo),
        scale,
        (att, part, v_ref, qr, kr),
        lambda i: None,
        lambda i: None,
    )
    for copy in come.copies[1:]:
        copy.wait()


def prompt_attention(line, hidden, weights, scale, later):
    width = scale.shape[1]
    scratch = [
        vmem(P_SIZE, D, BF),
        vmem(P_SIZE, width, BF),
        vmem(P_SIZE, width, BF),
        vmem(P_SIZE, width, F32),
        vmem(P_SIZE, width, F32),
        sems(4),
    ]
    outs = [shape(P_SIZE, D, BF)] + [near(*weight.shape, BF) for weight in later]
    flops = 8 * P_SIZE * D * width + 8 * P_SIZE * P_SIZE * width
    ins = (hidden, *weights, scale, *later)
    return line.call(
        prompt_kernel, outs, ins, flops=flops, scratch=scratch, vmem=13, away=(0, 6, 7, 8)
    )


def swiglu_of(up_val, gate_val, up_scale, gate_scale):
    half = (gate_scale * (0.5 * ROOT)) * gate_val
    more = jnp.tanh(half) + 1.0
    swish = half * more
    return (up_scale * up_val * swish).astype(BF), 0.5 * more, swish


def swiglu_back(d_inner, up_val, sigma, swish, up_scale, gate_scale):
    scaled = d_inner * up_scale
    d_arg = scaled * up_val * (sigma + swish * (1.0 - sigma))
    return (scaled * swish).astype(BF), d_arg, (d_arg * (gate_scale * ROOT)).astype(BF)


def unit_tiles(units, tile):
    return [slice(start, start + tile) for start in range(0, units, tile)]


def ffn_kernel(mine, other, hidden, rate, up_w, gate_w, down_w, up_s, gate_s, *refs):
    part, low_ref, up_ref, gate_ref, one_ref, sums_far, one_far = refs[:7]
    sums_ref, inner_ref, x_ref, in_sems, out_sems = refs[7:]
    come, go = Copies(in_sems), Copies(out_sems)
    come.start(hidden.at[P_SIZE:], x_ref)
    sums = both(mine[...], other[...])
    sums_ref[...] = sums
    go.start(sums_ref, sums_far)
    come.wait()
    one = mix(x_ref[...].astype(F32), sums, rate[...])[0]
    one_ref[...] = one
    go.start(one_ref, one_far)
    low = one.astype(BF)
    low_ref[...] = low
    for cols in unit_tiles(up_w.shape[1], 512):
        up_val, gate_val = dot(low, up_w[:, cols]), dot(low, gate_w[:, cols])
        up_ref[:, cols] = up_val
        gate_ref[:, cols] = gate_val
        inner_ref[:, cols] = swiglu_of(up_val, gate_val, up_s[:, cols], gate_s[:, cols])[0]
    part[...] = dot(inner_ref[...], down_w[...]).astype(BF)
    go.wait()


def ffn(line, mine, other, hidden, rate, weights):
    units = weights[0].shape[1]
    outs = [
        shape(L, D, BF),
        shape(L, D, BF),
        near(L, units, F32),
        near(L, units, F32),
        near(L, D, F32),
        distant(L, D, F32),
        distant(L, D, F32),
    ]
    scratch = [vmem(L, D, F32), vmem(L, units, BF), vmem(L, D, BF), sems(1), sems(2)]
    ins = (mine, other, hidden, rate, *weights)
    flops = 6 * L * D * units
    return line.call(
        ffn_kernel, outs, ins, flops=flops, scratch=scratch, away=(2,), sent=(5, 6)
    )


def prompt_ffn_kernel(mine, other, hidden, rate, up_far, gate_far, down_far, up_s, gate_s, *refs):
    one_ref, part, inner_ref, x_ref, up_w, gate_w, down_w, in_sems = refs
    tiles = unit_tiles(up_w.shape[1], 512)
    groups = [((hidden.at[:P_SIZE], x_ref),)]
    for cols in tiles:
        groups.append(
            (
                (up_far.at[:, cols], up_w.at[:, cols]),
                (gate_far.at[:, cols], gate_w.at[:, cols]),
                (down_far.at[cols], down_w.at[cols]),
            )
        )
    arrive = Tiles(Copies(in_sems), groups, 3)
    arrive.wait(0)
    one = mix(x_ref[...].astype(F32), both(mine[...], other[...]), rate[...])[0]
    one_ref[...] = one
    low = one.astype(BF)
    for i, cols in enumerate(tiles):
        arrive.wait(1 + i)
        up_val, gate_val = dot(low, up_w[:, cols]), dot(low, gate_w[:, cols])
        inner_ref[:, cols] = swiglu_of(up_val, gate_val, up_s[:, cols], gate_s[:, cols])[0]
    part[...] = dot(inner_ref[...], down_w[...]).astype(BF)


def weight_scratch(weights):
    return [vmem(*weight.shape, BF) for weight in weights[:3]]


def prompt_ffn(line, mine, other, hidden, rate, weights):
    units = weights[0].shape[1]
    scratch = [
        vmem(P_SIZE, units, BF),
        vmem(P_SIZE, D, BF),
        *weight_scratch(weights),
        sems(1 + 3 * units // 512),
    ]
    ins = (mine, other, hidden, rate, *weights)
    outs = (distant(P_SIZE, D, F32), shape(P_SIZE, D, BF))
    flops = 6 * P_SIZE * D * units
    return line.call(
        prompt_ffn_kernel, outs, ins, flops=flops, scratch=scratch, vmem=38, away=(2, 4, 5, 6)
    )


def ffn_back_kernel(mine, other, one, rate, teacher, valid, up_v, gate_v, *refs):
    up_w, gate_w, down_w, up_s, gate_s = refs[:5]
    part, low_ref, out_ref, dmix_ref, gains, d_up_ref, d_gate_ref = refs[5:]
    tiles = unit_tiles(up_w.shape[1], 512)
    row = lax.broadcasted_iota(jnp.int32, (L, L), 0)
    col = lax.broadcasted_iota(jnp.int32, (L, L), 1)
    counted = jnp.sum(jnp.where(row == col, valid[...].astype(F32), 0.0), axis=1, keepdims=True)
    old = one[...]
    out, unit, inverse_in, inverse_out = mix(old, both(mine[...], other[...]), rate[...])
    out_ref[...] = out
    diff = out - teacher[...].astype(F32)
    weighted = counted * diff
    by_row = jnp.sum(weighted * diff, axis=1, keepdims=True)
    dmix = norm_back(2.0 * weighted, out, inverse_out)
    dmix_ref[...] = dmix
    low = norm_back(dmix * rate[...], unit, inverse_in).astype(BF)
    low_ref[...] = low

    width = gains.shape[1]
    gains[...] = jnp.zeros_like(gains)

    def put(place, value):
        for start in range(0, value.shape[1], width):
            gains[place : place + 1] = value[:, start : start + width]
            place += 1

    put(0, jnp.sum(dmix * (unit - old), axis=0, keepdims=True))
    lane = lax.broadcasted_iota(jnp.int32, (1, width), 1)
    last = jnp.zeros((1, width), F32)
    for i, value in enumerate((by_row, counted)):
        value = jnp.sum(value, axis=0, keepdims=True)
        high = value.astype(BF).astype(F32)
        last = jnp.where(lane == 2 * i, high, last)
        last = jnp.where(lane == 2 * i + 1, value - high, last)
    put(13, last)
    for cols in tiles:
        d_inner = dot_nt(low, down_w[cols])
        up_val, gate_val = up_v[:, cols], gate_v[:, cols]
        _, sigma, swish = swiglu_of(up_val, gate_val, up_s[:, cols], gate_s[:, cols])
        d_up, d_arg, d_gate = swiglu_back(
            d_inner, up_val, sigma, swish, up_s[:, cols], gate_s[:, cols]
        )
        d_up_ref[:, cols] = d_up
        d_gate_ref[:, cols] = d_gate
        for place, value in ((4, d_inner * up_val * swish), (8, d_arg * ROOT * gate_val)):
            total = jnp.sum(value, axis=0, keepdims=True)
            done = cols.start
            while done < cols.stop:
                step = min(cols.stop, (done // width + 1) * width) - done
                left, at = done - cols.start, done % width
                gains[place + done // width : place + done // width + 1, at : at + step] = total[
                    :, left : left + step
                ]
                done += step
    total = dot_nt(d_up_ref[...], up_w[...]) + dot_nt(d_gate_ref[...], gate_w[...])
    part[...] = total.astype(BF)


def ffn_back(line, mine, other, one, rate, teacher, valid, up_val, gate_val, weights, width):
    units = weights[0].shape[1]
    outs = (
        distant(L, D, BF),
        distant(L, D, BF),
        distant(L, D, F32),
        distant(L, D, F32),
        distant(GAINS, width, F32),
    )
    scratch = [vmem(L, units, BF), vmem(L, units, BF)]
    ins = (mine, other, one, rate, teacher, valid, up_val, gate_val, *weights)
    flops = 6 * L * D * units
    return line.call(ffn_back_kernel, outs, ins, flops=flops, scratch=scratch)


def split_blocks(blocks, first, send_ref, keep_ref, start):
    size = blocks[0].shape[0]
    for j in range(0, len(blocks), 2):
        rows = slice(start + j // 2 * size, start + (j // 2 + 1) * size)
        even, odd = blocks[j], blocks[j + 1]
        send_ref[rows] = jnp.where(first, odd, even)
        keep_ref[rows] = jnp.where(first, even, odd)


def collect_kernel(far, info, *refs):
    parts, (ones_far, ones_t_far, ones, ones_t, in_sems, out_sems) = refs[:far], refs[far:]
    rows = parts[0].shape[0]
    come, go = Copies(in_sems), Copies(out_sems)
    for k, part in enumerate(parts):
        come.start(part, ones.at[pl.ds((info[PLACE_FAR] ^ k) * rows, rows)])
    come.wait()
    go.start(ones, ones_far)
    turn_part(far, info, ones, ones_t)
    go.start(ones_t, ones_t_far)
    go.wait()


def collect(line, info, parts):
    far, rows = len(parts), len(parts) * parts[0].shape[0]
    outs = (distant(rows, D, BF), distant(D // far, rows, BF))
    scratch = [vmem(rows, D, BF), vmem(D // far, rows, BF), sems(far), sems(2)]
    return line.call(
        functools.partial(collect_kernel, far),
        outs,
        (info, *parts),
        scratch=scratch,
        vmem=6,
        smem=1,
        loose=range(1, 1 + far),
        sent=(0, 1),
    )


def unit_factors_kernel(ones_far, up_far, gate_far, up_s, gate_s, *refs):
    far, (ones, up_w, gate_w), kept, (in_sems, out_sems) = refs[:3], refs[3:6], refs[6:9], refs[9:]
    go = Copies(out_sems)
    tiles = unit_tiles(up_w.shape[1], 512)
    groups = [((ones_far, ones),)]
    for cols in tiles:
        groups.append(
            ((up_far.at[:, cols], up_w.at[:, cols]), (gate_far.at[:, cols], gate_w.at[:, cols]))
        )
    arrive = Tiles(Copies(in_sems), groups, 3)
    arrive.wait(0)
    for i, cols in enumerate(tiles):
        arrive.wait(1 + i)
        up_scale, gate_scale = up_s[:, cols], gate_s[:, cols]
        up_val, gate_val = dot(ones[...], up_w[:, cols]), dot(ones[...], gate_w[:, cols])
        inner, sigma, swish = swiglu_of(up_val, gate_val, up_scale, gate_scale)
        kept[0][:, cols] = inner
        kept[1][:, cols] = (up_scale * swish).astype(BF)
        slope = sigma + swish * (1.0 - sigma)
        kept[2][:, cols] = (up_scale * (gate_scale * ROOT) * up_val * slope).astype(BF)
        for source, target in zip(kept, far):
            go.start(source.at[:, cols], target.at[:, cols])
    go.wait()


def turn_part(far, info, source, target):
    group = target.shape[0]
    for j in range(far):

        @pl.when(info[PLACE_FAR] == j)
        def _(j=j):
            target[...] = source[:, j * group : (j + 1) * group].T


def unit_factors(line, ones, weights):
    rows, units = ones.shape[0], weights[0].shape[1]
    outs = [distant(rows, units, BF)] * 3
    scratch = [vmem(rows, D, BF), vmem(D, units, BF), vmem(D, units, BF)]
    scratch += [vmem(rows, units, BF)] * 3 + [sems(1 + 2 * units // 512), sems(3 * units // 512)]
    return line.call(
        unit_factors_kernel,
        outs,
        (ones, weights[0], weights[1], weights[3], weights[4]),
        flops=4 * rows * D * units,
        scratch=scratch,
        vmem=36,
        away=(0, 1, 2),
        sent=(0, 1, 2),
    )


def ffn_grad_kernel(far, info, *refs):
    parts, (ones_t_far, down_far), refs = refs[:far], refs[far : far + 2], refs[far + 2 :]
    factors_far, (send, keep), refs = refs[:3], refs[3:5], refs[5:]
    ones_t, d_ffns, d_ffns_t, down_w, *factors, in_sems = refs
    rows = parts[0].shape[0]
    tiles = unit_tiles(down_w.shape[0], 512)
    first = [
        (part, d_ffns.at[pl.ds((info[PLACE_FAR] ^ k) * rows, rows)]) for k, part in enumerate(parts)
    ]
    groups = [[*first, (ones_t_far, ones_t)]]
    for cols in tiles:
        group = [(down_far.at[cols], down_w.at[cols])]
        group += [(a.at[:, cols], b.at[:, cols]) for a, b in zip(factors_far, factors)]
        groups.append(group)
    arrive = Tiles(Copies(in_sems), groups, 3)
    arrive.wait(0)
    turn_part(far, info, d_ffns, d_ffns_t)
    size = ones_t.shape[0] // 4
    for i, cols in enumerate(tiles):
        arrive.wait(1 + i)
        d_inner = dot_nt(d_ffns[...], down_w[cols])
        inner, to_up, to_gate = (factor[:, cols] for factor in factors)
        d_up = (d_inner * to_up.astype(F32)).astype(BF)
        d_gate = (d_inner * to_gate.astype(F32)).astype(BF)
        for k, (left, right) in enumerate(((ones_t, d_up), (ones_t, d_gate), (d_ffns_t, inner))):
            grad = dot(left[...], right).astype(BF)
            blocks = [grad[j * size : (j + 1) * size] for j in range(4)]
            split_blocks(blocks, info[CORE] == 0, send.at[:, cols], keep.at[:, cols], k * 2 * size)


def ffn_grad(line, info, parts, down_weight, ones_t, factors):
    far, units = len(parts), down_weight.shape[0]
    rows, group = far * parts[0].shape[0], D // far
    outs = [distant(3 * group // 2, units, BF)] * 2
    scratch = [vmem(group, rows, BF), vmem(rows, D, BF), vmem(group, rows, BF), vmem(units, D, BF)]
    scratch += [vmem(rows, units, BF)] * 3 + [sems(far + 1 + 4 * units // 512)]
    return line.call(
        functools.partial(ffn_grad_kernel, far),
        outs,
        (info, *parts, ones_t, down_weight, *factors),
        flops=2 * rows * (D + 3 * group) * units,
        scratch=scratch,
        vmem=36,
        smem=1,
        loose=range(1, 1 + far),
        away=range(1 + far, 6 + far),
    )


def plain_unit_grads(low, d_ffn, weights):
    up_w, gate_w, down_w, up_s, gate_s = weights
    up_val = dot(low, up_w)
    inner, sigma, swish = swiglu_of(up_val, dot(low, gate_w), up_s, gate_s)
    d_up, _, d_gate = swiglu_back(dot_nt(d_ffn, down_w), up_val, sigma, swish, up_s, gate_s)
    return dot_tn(low, d_up), dot_tn(low, d_gate), dot_tn(d_ffn, inner)


def turn_kernel(source, result):
    result[...] = source[...].T


def turn(line, value):
    rows, cols = value.shape
    value = pltpu.with_memory_space_constraint(value, pltpu.HBM)
    return line.call(turn_kernel, (distant(cols, rows, value.dtype),), (value,))[0]


def give(split, info, products, outs):
    for i, (left, right) in enumerate(products):
        grad = dot(left, right[...]).astype(BF)
        if split:
            size = D // 16
            blocks = [grad[j * size : (j + 1) * size] for j in range(16)]
            split_blocks(blocks, info[CORE] == 0, outs[0], outs[1], i * 8 * size)
        else:
            outs[i][...] = grad


BACK_INPUTS = (
    ("d_mine", BF),
    ("dmix_two", F32),
    ("one", F32),
    ("sums", F32),
    ("x_cont", BF),
    ("wo", BF),
    ("kr", F32),
    ("qr", F32),
    ("v", BF),
    ("gains", F32),
    ("x_t", BF),
    ("att", BF),
)


def attention_back_kernel(split, info, _, d_other, rate_two, rate_one, scale_ref, *refs):
    count = len(BACK_INPUTS)
    far, outs, held = refs[:count], refs[count : -count - 7], refs[-count - 6 : -6]
    d_att, dq_ref, dk_ref, dv_ref, in_sems, out_sems = refs[-6:]
    come, go = Copies(in_sems), Copies(out_sems)
    ref = {}
    arrived = {}
    pairs = {}
    for (name, _), source, target in zip(BACK_INPUTS, far, held):
        ref[name] = target
        pairs[name] = (source.at[P_SIZE:] if name == "x_cont" else source, target)

    def begin(*names):
        for name in names:
            arrived[name] = come.start(*pairs[name]).wait

    begin("d_mine", "dmix_two", "one", "sums", "x_cont", "wo")
    outs, (dq_far, dk_far, dv_far, residual_ref, gains_out) = outs[:-5], outs[-5:]

    for name in ("d_mine", "dmix_two", "one", "sums", "x_cont"):
        arrived[name]()
    begin("gains", "kr", "qr", "v", "att", "x_t")
    old = ref["x_cont"][...].astype(F32)
    _, unit_in, inverse_in, inverse_out = mix(old, ref["sums"][...], rate_one[...])
    d_one = both(ref["d_mine"][...], d_other[...])
    d_one = d_one + (1.0 - rate_two[...]) * ref["dmix_two"][...]
    dmix = norm_back(d_one, ref["one"][...], inverse_out)
    residual_ref[...] = dmix * (1.0 - rate_one[...])
    att_grad = jnp.sum(dmix * (unit_in - old), axis=0, keepdims=True)
    d_attn = norm_back(dmix * rate_one[...], unit_in, inverse_in).astype(BF)
    arrived["wo"]()
    d_att[...] = dot_nt(d_attn, ref["wo"][...]).astype(BF)

    gains = ref["gains"]
    width = scale_ref.shape[1]
    arrived["gains"]()
    for i in range(D // width):
        gains[2 + i : 3 + i] = att_grad[:, i * width : (i + 1) * width]

    def raw_back(grad, unit, inverse, scale):
        scaled = grad * scale
        back = inverse * (scaled - unit * head_sums(scaled * unit))
        return back.astype(BF), jnp.sum(grad * unit, axis=0, keepdims=True)

    for name in ("kr", "qr", "v"):
        arrived[name]()
    for start in range(0, width, PAIR):
        cols = slice(start, start + PAIR)
        scale = scale_ref[:, cols]
        q_unit, q_inverse = unit_heads(ref["qr"][:, cols])
        k_unit, k_inverse = unit_heads(ref["kr"][:, cols])
        queries = halves((q_unit * scale).astype(BF))
        keys = (k_unit * scale).astype(BF)
        grads = halves(d_att[:, cols])
        probs = weights_of(queries, keys, P_SIZE)
        d_probs = dot_nt(grads, ref["v"][:, cols])
        delta = jnp.sum(d_probs * probs, axis=1, keepdims=True)
        d_scores = (probs * (d_probs - delta)).astype(BF)
        d_query = 8.0 * merge(dot(d_scores, keys))
        d_keys = 8.0 * dot_tn(d_scores, queries)
        dv_ref[:, cols] = dot_tn(probs.astype(BF), grads).astype(BF)
        dq_ref[:, cols], by_query = raw_back(d_query, q_unit, q_inverse, scale)
        dk_ref[:, cols], by_key = raw_back(d_keys, k_unit, k_inverse, scale)
        gains[12:13, cols] = by_query + by_key
    for source, target in ((dq_ref, dq_far), (dk_ref, dk_far), (dv_ref, dv_far)):
        go.start(source, target)

    arrived["x_t"]()
    arrived["att"]()
    x_t = ref["x_t"]
    products = (
        (x_t[...], dv_ref),
        (x_t[...], dk_ref),
        (x_t[:, P_SIZE:], dq_ref),
        (d_attn.T, ref["att"]),
    )
    give(split, info, products, outs)
    gains_out[...] = gains[...]
    if split:
        for out in outs:
            out[2 * D :] = gains[...].astype(BF)
    go.wait()


def attention_back(line, split, info, passed, d_other, rate_two, rate_one, scale, ins):
    width = scale.shape[1]
    rows = ins["v"].shape[0]
    outs = [shape(2 * D + GAINS, width, BF)] * 2 if split else [shape(D, width, BF)] * 4
    first = len(outs)
    outs += [distant(L, width, BF), distant(rows, width, BF), distant(rows, width, BF)]
    outs += [distant(L, D, F32), shape(GAINS, width, F32), shape(*passed.shape, BF)]
    scratch = []
    for name, kind in BACK_INPUTS:
        scratch.append(vmem(L if name == "x_cont" else ins[name].shape[0], ins[name].shape[1], kind))
    scratch += [vmem(L, width, BF), vmem(L, width, BF), vmem(rows, width, BF), vmem(rows, width, BF)]
    scratch += [sems(len(BACK_INPUTS)), sems(3)]
    flops = 20 * L * rows * width + 4 * (rows + L) * D * width + 4 * L * D * width
    return line.call(
        functools.partial(attention_back_kernel, split),
        outs,
        (info, passed, d_other, rate_two, rate_one, scale, *(ins[name] for name, _ in BACK_INPUTS)),
        flops=flops,
        scratch=scratch,
        vmem=38,
        smem=1,
        away=range(6, 6 + len(BACK_INPUTS)),
        loose=(1,),
        sent=(first, first + 1, first + 2, first + 5),
        aliases={1: first + 5},
    )


def fold_core_kernel(info, keep, got, *outs):
    size = D // 16
    total = (keep[...].astype(F32) + got[...].astype(F32)).astype(BF)
    for m in range(4):
        start = m * 8 * size
        blocks = [total[start + j * size : start + (j + 1) * size] for j in range(8)]
        send, kept = outs[:2] if m < 2 else outs[2:]
        split_blocks(blocks, info[PLACE_X] == 0, send, kept, m % 2 * 4 * size)
    for ref in outs[:2]:
        ref[8 * size :] = total[32 * size :]


def fold_kernel(matrices, count, bit, info, keep, got, send, kept):
    size = D // 16
    low = info[PLACE_FAR] // bit % 2 == 0
    total = (keep[...].astype(F32) + got[...].astype(F32)).astype(BF)
    half = count // 2
    for m in range(matrices):
        first = total[m * count * size : (m * count + half) * size]
        second = total[(m * count + half) * size : (m + 1) * count * size]
        rows = slice(m * half * size, (m + 1) * half * size)
        send[rows] = jnp.where(low, second, first)
        kept[rows] = jnp.where(low, first, second)
    if keep.shape[0] > matrices * count * size:
        for ref in (send, kept):
            ref[matrices * half * size :] = total[matrices * count * size :]


def finish_kernel(tokens, keep_a, got_a, keep_b, got_b, *outs):
    value, key, query, out, mlp, att, up, gate, head, loss, factor_ref = outs
    size = value.shape[0]
    first = keep_a[...].astype(F32) + got_a[...].astype(F32)
    second = keep_b[...].astype(F32) + got_b[...].astype(F32)
    total = first[2 * size :]
    factor = tokens / (total[13:14, 2:3] + total[13:14, 3:4])
    factor_ref[...] = factor
    loss[...] = factor * (total[13:14, 0:1] + total[13:14, 1:2])
    total = total * factor
    width = total.shape[1]
    place = 0
    for ref in (mlp, att, up, gate, head):
        for start in range(0, ref.shape[1], width):
            ref[:, start : start + width] = total[place : place + 1]
            place += 1
    value[...] = first[:size] * factor
    key[...] = first[size : 2 * size] * factor
    query[...] = second[:size] * factor
    out[...] = second[size:] * factor


def fold_units_kernel(info, keep, got, *outs):
    size = keep.shape[0] // 6
    total = (keep[...].astype(F32) + got[...].astype(F32)).astype(BF)
    for m in range(3):
        blocks = [total[j * size : (j + 1) * size] for j in (2 * m, 2 * m + 1)]
        split_blocks(blocks, info[PLACE_X] == 0, outs[m], outs[3 + m], 0)


def finish_units_kernel(factor, *refs):
    for keep, got, result in zip(refs[:3], refs[3:6], refs[6:]):
        result[...] = (keep[...].astype(F32) + got[...].astype(F32)) * factor[...]


def rows_kernel(info, dq, dk, dv, wq_far, wk_far, wv_far, send_ref, keep_ref, wq, wk, wv, in_sems):
    come = Copies(in_sems)
    for source, target in ((wk_far, wk), (wv_far, wv), (wq_far, wq)):
        come.start(source, target)
    half = send_ref.shape[0]
    come.copies[0].wait()
    prompt = dot_nt(dk[...], wk[...])
    come.copies[1].wait()
    prompt = prompt + dot_nt(dv[...], wv[...])
    come.copies[2].wait()
    top = prompt[:half].astype(BF)
    low = jnp.concatenate(
        [prompt[half:P_SIZE], prompt[P_SIZE:] + dot_nt(dq[...], wq[...])], 0
    ).astype(BF)
    first = info[SIDE] == 0
    send_ref[...] = jnp.where(first, low, top)
    keep_ref[...] = jnp.where(first, top, low)


def share_kernel(info, keep, got, residual, kept_ref, sent_ref):
    half = keep.shape[0]
    total = keep[...].astype(F32) + got[...].astype(F32)
    row = lax.broadcasted_iota(jnp.int32, (half, 1), 0) + info[SIDE] * half
    away = (row < P_SIZE) & (info[OWN] == 0)
    sent_ref[...] = jnp.where(away, total, 0.0).astype(BF)
    kept_ref[...] = jnp.where(away, 0.0, total)
    kept_ref[half - L :] += jnp.where(info[SIDE] == 1, residual[...], 0.0)


def last_share_kernel(kept, got, factor, result):
    result[...] = (kept[...] + got[...].astype(F32)) * factor[...]


def last_mix_kernel(mine, other, one, rate, out, result):
    result[:P_SIZE] = mix(one[...], both(mine[...], other[...]), rate[...])[0]
    result[P_SIZE:] = out[...]


def local(
    hidden_in,
    query_weight,
    key_weight,
    value_weight,
    out_weight,
    up_weight,
    gate_weight,
    down_weight,
    head_scale,
    attention_rate,
    up_scale,
    gate_scale,
    swiglu_rate,
    teacher,
    valid_mask,
    group_ids,
):
    count_dp = lax.axis_size("dp")
    far = count_dp // 4
    split = far == 4
    me = lax.axis_index("dp")
    rows = hidden_in.shape[0]
    width = query_weight.shape[1]
    units = up_weight.shape[1]
    scale = head_scale.reshape(1, width)
    rate_one = attention_rate.reshape(1, D)
    rate_two = swiglu_rate.reshape(1, D)
    own = (group_ids[0] == me).astype(jnp.int32)
    info = jnp.stack([own, me % 2, me // 2 % 2, me // 4, lax.axis_index("tensor")])
    info = info.astype(jnp.int32)
    qkvo = (query_weight, key_weight, value_weight, out_weight)
    ffn_weights = (
        up_weight,
        gate_weight,
        down_weight,
        up_scale.reshape(1, units),
        gate_scale.reshape(1, units),
    )

    line = Line()

    other_x = swap(hidden_in, "dp", 1)
    a_mine, att, x_seen, values, query_raw, key_raw, *qkvo_near = cont_attention(
        line, info, hidden_in, other_x, qkvo, scale
    )
    a_other = swap(a_mine, "tensor", 1)
    p_mine, *ffn_near = prompt_attention(line, hidden_in, qkvo_near, scale, ffn_weights[:3])
    ffn_near = (*ffn_near, *ffn_weights[3:])
    m_mine, one_low, up_val, gate_val, one_near, attn_sums, one = ffn(
        line, a_mine, a_other, hidden_in, rate_one, ffn_near
    )
    m_other = swap(m_mine, "tensor", 1)
    x_seen_t = turn(line, x_seen)
    d_mine, d_ffn, out, dmix_two, gains = ffn_back(
        line,
        m_mine,
        m_other,
        one_near,
        rate_two,
        teacher,
        valid_mask.reshape(1, L),
        up_val,
        gate_val,
        ffn_near,
        width,
    )
    total_cont = count_dp * valid_mask.shape[0]
    mine = D // count_dp
    usual = group_ids[0] >= 0
    half_rows = shape(rows // 2, D, BF)

    d_other = swap(d_mine, "tensor", 1)
    if split:
        ones = [one_low]
        bit = 4
        while bit < count_dp:
            ones += [swap(part, "dp", bit) for part in ones]
            bit *= 2
        ones, ones_t = collect(line, info, ones)
    *first, d_query, d_key, d_value, residual, gains, p_mine = attention_back(
        line,
        split,
        info,
        p_mine,
        d_other,
        rate_two,
        rate_one,
        scale,
        {
            "d_mine": d_mine,
            "dmix_two": dmix_two,
            "one": one,
            "sums": attn_sums,
            "x_cont": hidden_in,
            "wo": out_weight,
            "kr": key_raw,
            "qr": query_raw,
            "v": values,
            "gains": gains,
            "x_t": x_seen_t,
            "att": att,
        },
    )

    p_other = swap(p_mine, "tensor", 1)

    def fold(line, send, keep, count, bit):
        more = keep.shape[0] - 2 * count * mine
        return line.call(
            functools.partial(fold_kernel, 2, count, bit),
            [shape(count * mine + more, width, BF)] * 2,
            (info, keep, send),
            smem=1,
        )

    def rows_step(info, first, d_query, d_key, d_value, ones):
        inner = Line()
        if split:
            got = swap(first[0], "dp", 1)
        rows_pair = inner.call(
            rows_kernel,
            (half_rows, half_rows),
            (info, d_query, d_key, d_value, query_weight, key_weight, value_weight),
            flops=6 * rows * D * width,
            scratch=[vmem(D, width, BF)] * 3 + [sems(3)],
            vmem=22,
            smem=1,
            away=(4, 5, 6),
        )
        if not split:
            return first, rows_pair, ()
        send_a, keep_a, send_b, keep_b = inner.call(
            fold_core_kernel,
            [shape(D // 2 + GAINS, width, BF)] * 2 + [shape(D // 2, width, BF)] * 2,
            (info, first[1], got),
            smem=1,
        )
        got_a = swap(send_a, "dp", 2)
        factors = unit_factors(inner, ones, ffn_weights)
        send_a, keep_a = fold(inner, got_a, keep_a, 4, 2)
        return (send_a, keep_a, send_b, keep_b), rows_pair, factors

    if not split:
        ones = one_low
    first, (rows_sent, kept), factors = section(
        usual, rows_step, info, first, d_query, d_key, d_value, ones
    )
    line.last = kept
    share = swap(rows_sent, "tensor", 1)
    if split:
        send_a, keep_a, send_b, keep_b = first
        got_a, got_b = swap(send_a, "dp", 8), swap(send_b, "dp", 2)
        d_ffns = [d_ffn] + [swap(d_ffn, "dp", 4 * k) for k in range(1, far)]
        u_send, u_keep = ffn_grad(line, info, d_ffns, down_weight, ones_t, factors)
    else:
        u_send = u_keep = None

    def share_step(info, before, share_keep, share, residual, u_send, u_keep):
        inner = Line(before)
        if split:
            got = swap(u_send, "dp", 1)
        kept, sent = inner.call(
            share_kernel,
            (distant(rows // 2, D, F32), half_rows),
            (info, share_keep, share, residual),
            smem=1,
        )
        if split:
            u_send, u_keep = halves_of(
                inner.call(
                    fold_units_kernel, (shape(mine, units, BF),) * 6, (info, u_keep, got), smem=1
                )
            )
        return kept, sent, u_send, u_keep

    kept, sent, u_send, u_keep = section(
        usual, share_step, info, line.last, kept, share, residual, u_send, u_keep
    )
    line.last = kept
    share = swap(sent, "dp", 1)
    if split:
        u_got = [swap(part, "dp", 2) for part in u_send]
        send_b, keep_b = fold(line, got_b, keep_b, 4, 2)
        got_b = swap(send_b, "dp", 8)
    one_p, mp_mine = prompt_ffn(line, p_mine, p_other, hidden_in, rate_one, ffn_weights)
    mp_other = swap(mp_mine, "tensor", 1)
    if split:
        send_a, keep_a = fold(line, got_a, keep_a, 2, 1)
        got_a = swap(send_a, "dp", 4)
        send_b, keep_b = fold(line, got_b, keep_b, 2, 1)
        got_b = swap(send_b, "dp", 4)
        *grads, mlp, att_rate, up_g, gate_g, head, loss, factor = line.call(
            functools.partial(finish_kernel, total_cont),
            [distant(mine, width, F32)] * 4
            + [shape(1, n, F32) for n in (D, D, units, units, width, 1, 1)],
            (keep_a, got_a, keep_b, got_b),
        )
        value_grad, key_grad, query_grad, out_grad = grads
    else:
        total = sum_all(gains)
        factor = total_cont / (total[13:14, 2:3] + total[13:14, 3:4])
        loss = factor * (total[13:14, 0:1] + total[13:14, 1:2])
        flat = (total * factor).reshape(-1)
        mlp, att_rate, up_g, gate_g, head = (
            flat[start : start + size]
            for start, size in (
                (0, D),
                (D, D),
                (2 * D, units),
                (2 * D + units, units),
                (2 * D + 2 * units, width),
            )
        )

        def scattered(grad):
            grad = grad.astype(F32)
            return factor * lax.psum_scatter(grad, "dp", scatter_dimension=0, tiled=True)

        value_grad, key_grad, query_grad, out_grad = (scattered(grad) for grad in first)
        up_grad, gate_grad, down_grad = (
            scattered(grad) for grad in plain_unit_grads(one_low, d_ffn, ffn_weights)
        )
    grad_hidden = line.call(last_share_kernel, (distant(rows // 2, D, F32),), (kept, share, factor))[0]
    hidden_out = line.call(
        last_mix_kernel,
        (distant(rows, D, F32),),
        (mp_mine, mp_other, one_p, rate_two, out),
    )[0]
    if split:
        up_grad, gate_grad, down_grad = line.call(
            finish_units_kernel, (distant(mine, units, F32),) * 3, (factor, *u_keep, *u_got)
        )
    return (
        hidden_out,
        loss[0, 0],
        grad_hidden,
        query_grad,
        key_grad,
        value_grad,
        out_grad.T,
        up_grad,
        gate_grad,
        down_grad.T,
        head.reshape(-1),
        att_rate.reshape(-1),
        up_g.reshape(-1),
        gate_g.reshape(-1),
        mlp.reshape(-1),
    )


def solution(mesh):
    placed = (
        P("dp", None),
        P(None, "tensor"),
        P(None, "tensor"),
        P(None, "tensor"),
        P("tensor", None),
        P(None, "tensor"),
        P(None, "tensor"),
        P("tensor", None),
        P("tensor"),
        P(),
        P("tensor"),
        P("tensor"),
        P(),
        P("dp", None),
        P("dp"),
        P("dp"),
    )
    return jax.shard_map(
        local,
        mesh=mesh,
        in_specs=placed,
        out_specs=(
            P("dp", None),
            P(),
            P(("dp", "tensor"), None),
            P("dp", "tensor"),
            P("dp", "tensor"),
            P("dp", "tensor"),
            P("tensor", "dp"),
            P("dp", "tensor"),
            P("dp", "tensor"),
            P("tensor", "dp"),
            P("tensor"),
            P(),
            P("tensor"),
            P("tensor"),
            P(),
        ),
        check_vma=False,
    )
```

```python
import functools
import math

import jax
import jax.numpy as jnp
from jax import lax
from jax.experimental import pallas as pl
from jax.experimental.pallas import tpu as pltpu
from jax.sharding import PartitionSpec as P

D = 1280
HD = 64
P_SIZE = 384
L = 128
PAIR = 2 * HD
EPS = 1e-06
ROOT = math.sqrt(D)
BF = jnp.bfloat16
F32 = jnp.float32
MIB = 2**20
GAINS = 16
OWN, CORE, PLACE_X, PLACE_FAR, SIDE = range(5)


def swap(value, axis, bit):
    count = lax.axis_size(axis)
    return lax.ppermute(value, axis, [(i, i ^ bit) for i in range(count)])


def sum_all(value):
    bit = 1
    while bit < lax.axis_size("dp"):
        value = value + swap(value, "dp", bit)
        bit *= 2
    return value


def dot(left, right):
    return jnp.dot(left, right, preferred_element_type=F32)


def dot_nt(left, right):
    return lax.dot_general(left, right, (((1,), (1,)), ((), ())), preferred_element_type=F32)


def dot_tn(left, right):
    return lax.dot_general(left, right, (((0,), (0,)), ((), ())), preferred_element_type=F32)


def inverse_norm(values):
    return lax.rsqrt(jnp.sum(values * values, axis=-1, keepdims=True) + EPS)


def norm_back(grad, unit, inverse):
    return inverse * (grad - unit * jnp.sum(grad * unit, axis=-1, keepdims=True))


def mix(old, sums, rate):
    inverse_in = inverse_norm(sums)
    unit_in = sums * inverse_in
    mixed = old + rate * (unit_in - old)
    inverse_out = inverse_norm(mixed)
    return mixed * inverse_out, unit_in, inverse_in, inverse_out


def both(mine, other):
    return mine.astype(F32) + other.astype(F32)


class Line:
    def __init__(self, last=None):
        self.last = last

    def call(
        self, kernel, outs, ins, *, flops=0, scratch=(), vmem=12, smem=0, away=(), held=(), loose=(), sent=(), aliases=()
    ):
        moved = sum(math.prod(v.shape) * v.dtype.itemsize for v in (*ins, *outs))
        count, results = len(ins), len(outs)
        places = [pltpu.SMEM] * smem + [pltpu.VMEM] * (count - smem)
        ins = list(ins)
        for i in (*loose, *away):
            places[i] = pl.ANY
        for i in (*held, *away):
            ins[i] = pltpu.with_memory_space_constraint(ins[i], pltpu.HBM)
        out_places = [pl.ANY if i in sent else pltpu.VMEM for i in range(results)] + [pl.ANY]
        if self.last is not None:
            places.append(pl.ANY)
            ins.append(pltpu.with_memory_space_constraint(self.last, pltpu.HBM))
        first = len(ins)

        def body(*refs):
            kernel(*refs[:count], *refs[first : first + results], *refs[first + results + 1 :])

        *done, self.last = pl.pallas_call(
            body,
            out_shape=(*outs, distant(8, 128, F32)),
            in_specs=[pl.BlockSpec(memory_space=place) for place in places],
            out_specs=tuple(pl.BlockSpec(memory_space=place) for place in out_places),
            scratch_shapes=list(scratch),
            input_output_aliases=dict(aliases),
            compiler_params=pltpu.CompilerParams(vmem_limit_bytes=vmem * MIB),
            cost_estimate=pl.CostEstimate(flops=flops, bytes_accessed=moved, transcendentals=0),
        )(*ins)
        return done


def section(usual, work, *ins):
    shapes = jax.eval_shape(work, *ins)
    return lax.cond(
        usual, work, lambda *_: jax.tree.map(lambda v: jnp.zeros(v.shape, v.dtype), shapes), *ins
    )


class Copies:
    def __init__(self, sems):
        self.sems, self.copies = sems, []

    def start(self, source, target):
        copy = pltpu.make_async_copy(source, target, self.sems.at[len(self.copies)])
        copy.start()
        self.copies.append(copy)
        return copy

    def wait(self):
        for copy in self.copies:
            copy.wait()


class Tiles:
    def __init__(self, come, groups, ahead=2):
        self.come, self.groups, self.ahead, self.going = come, groups, ahead, []
        for _ in range(ahead):
            self.more()

    def more(self):
        if len(self.going) < len(self.groups):
            group = self.groups[len(self.going)]
            self.going.append([self.come.start(source, target) for source, target in group])

    def wait(self, i):
        for copy in self.going[i]:
            copy.wait()
        self.more()


def distant(rows, cols, kind):
    return pltpu.HBM((rows, cols), kind)


def vmem(rows, cols, kind):
    return pltpu.VMEM((rows, cols), kind)


def sems(count):
    return pltpu.SemaphoreType.DMA((count,))


def near(rows, cols, kind):
    return pltpu.VMEM((rows, cols), kind)


def fetch(pairs, sems):
    copies = [pltpu.make_async_copy(a, b, sems.at[i]) for i, (a, b) in enumerate(pairs)]
    for copy in copies:
        copy.start()
    return copies


def shape(rows, cols, kind):
    return jax.ShapeDtypeStruct((rows, cols), kind)


def head_sums(values):
    rows = lax.broadcasted_iota(jnp.int32, (PAIR, PAIR), 0) // HD
    cols = lax.broadcasted_iota(jnp.int32, (PAIR, PAIR), 1) // HD
    ones = jnp.where(rows == cols, 1.0, 0.0).astype(BF)
    high = values.astype(BF)
    low = (values - high.astype(F32)).astype(BF)
    return dot(high, ones) + dot(low, ones)


def unit_heads(raw):
    inverse = lax.rsqrt(head_sums(raw * raw) + EPS)
    return raw * inverse, inverse


def halves(value):
    first = lax.broadcasted_iota(jnp.int32, value.shape, 1) < HD
    zero = jnp.zeros_like(value)
    return jnp.concatenate([jnp.where(first, value, zero), jnp.where(first, zero, value)], 0)


def merge(value):
    rows = value.shape[0] // 2
    first = lax.broadcasted_iota(jnp.int32, (rows, PAIR), 1) < HD
    return jnp.where(first, value[:rows], value[rows:])


def weights_of(queries, keys, offset):
    scores = 8.0 * dot_nt(queries, keys)
    rows = queries.shape[0] // 2
    row = lax.broadcasted_iota(jnp.int32, scores.shape, 0)
    row = jnp.where(row >= rows, row - rows, row)
    col = lax.broadcasted_iota(jnp.int32, scores.shape, 1)
    expo = jnp.where(col <= row + offset, jnp.exp(scores), 0.0)
    return expo * (1.0 / jnp.sum(expo, axis=1, keepdims=True))


def attention_body(x, offset, weights, scale_ref, refs, arrived, ready):
    wq_ref, wk_ref, wv_ref, wo_ref = weights
    att_ref, part_ref, v_ref, qr_ref, kr_ref = refs
    arrived(0)
    kr_ref[...] = dot(x, wk_ref[...])
    ready(0)
    arrived(1)
    v_ref[...] = dot(x, wv_ref[...]).astype(BF)
    ready(1)
    arrived(2)
    qr_ref[...] = dot(x[offset:], wq_ref[...])
    ready(2)
    for start in range(0, wq_ref.shape[1], PAIR):
        cols = slice(start, start + PAIR)
        scale = scale_ref[:, cols]
        keys = (unit_heads(kr_ref[:, cols])[0] * scale).astype(BF)
        queries = (unit_heads(qr_ref[:, cols])[0] * scale).astype(BF)
        probs = weights_of(halves(queries), keys, offset).astype(BF)
        att_ref[:, cols] = merge(dot(probs, v_ref[:, cols])).astype(BF)
    ready(3)
    arrived(3)
    part_ref[...] = dot(att_ref[...], wo_ref[...]).astype(BF)


def cont_kernel(info, hidden, other, wq, wk, wv, wo, scale, *refs):
    part, att_far, x_far, v_far, qr_far, kr_far, wq_near, wk_near, wv_near, wo_near = refs[:10]
    own_x, other_x, x_ref, att, v_ref, qr, kr, in_sems, out_sems = refs[10:]
    come, go = Copies(in_sems), Copies(out_sems)
    arrive = Tiles(
        come,
        (
            ((hidden, own_x), (other.at[:P_SIZE], other_x)),
            ((wk, wk_near),),
            ((wv, wv_near),),
            ((wq, wq_near),),
            ((wo, wo_near),),
        ),
    )
    arrive.wait(0)
    x_ref[:P_SIZE] = jnp.where(info[OWN] == 1, own_x[:P_SIZE], other_x[...])
    x_ref[P_SIZE:] = own_x[P_SIZE:]
    go.start(x_ref, x_far)
    results = ((kr, kr_far), (v_ref, v_far), (qr, qr_far), (att, att_far))
    attention_body(
        x_ref[...],
        P_SIZE,
        (wq_near, wk_near, wv_near, wo_near),
        scale,
        (att, part, v_ref, qr, kr),
        lambda i: arrive.wait(1 + i),
        lambda i: go.start(*results[i]),
    )
    go.wait()


def cont_attention(line, info, hidden, other, weights, scale):
    rows, width = hidden.shape[0], scale.shape[1]
    outs = [
        shape(L, D, BF),
        distant(L, width, BF),
        distant(rows, D, BF),
        distant(rows, width, BF),
        distant(L, width, F32),
        distant(rows, width, F32),
    ] + [near(*weight.shape, BF) for weight in weights]
    scratch = [
        vmem(rows, D, BF),
        vmem(P_SIZE, D, BF),
        vmem(rows, D, BF),
        vmem(L, width, BF),
        vmem(rows, width, BF),
        vmem(L, width, F32),
        vmem(rows, width, F32),
        sems(6),
        sems(5),
    ]
    flops = 4 * rows * D * width + 4 * L * D * width + 8 * L * rows * width
    return line.call(
        cont_kernel,
        outs,
        (info, hidden, other, *weights, scale),
        flops=flops,
        scratch=scratch,
        vmem=28,
        smem=1,
        away=(1, 3, 4, 5, 6),
        loose=(2,),
        sent=range(1, 6),
    )


def prompt_kernel(hidden, wq, wk, wv, wo, scale, up, gate, down, *refs):
    part, up_near, gate_near, down_near, x_ref, att, v_ref, qr, kr, in_sems = refs
    come = Copies(in_sems)
    come.start(hidden.at[:P_SIZE], x_ref)
    for source, target in ((up, up_near), (gate, gate_near), (down, down_near)):
        come.start(source, target)
    come.copies[0].wait()
    attention_body(
        x_ref[...],
        0,
        (wq, wk, wv, wo),
        scale,
        (att, part, v_ref, qr, kr),
        lambda i: None,
        lambda i: None,
    )
    for copy in come.copies[1:]:
        copy.wait()


def prompt_attention(line, hidden, weights, scale, later):
    width = scale.shape[1]
    scratch = [
        vmem(P_SIZE, D, BF),
        vmem(P_SIZE, width, BF),
        vmem(P_SIZE, width, BF),
        vmem(P_SIZE, width, F32),
        vmem(P_SIZE, width, F32),
        sems(4),
    ]
    outs = [shape(P_SIZE, D, BF)] + [near(*weight.shape, BF) for weight in later]
    flops = 8 * P_SIZE * D * width + 8 * P_SIZE * P_SIZE * width
    ins = (hidden, *weights, scale, *later)
    return line.call(
        prompt_kernel, outs, ins, flops=flops, scratch=scratch, vmem=13, away=(0, 6, 7, 8)
    )


def swiglu_of(up_val, gate_val, up_scale, gate_scale):
    half = (gate_scale * (0.5 * ROOT)) * gate_val
    more = jnp.tanh(half) + 1.0
    swish = half * more
    return (up_scale * up_val * swish).astype(BF), 0.5 * more, swish


def swiglu_back(d_inner, up_val, sigma, swish, up_scale, gate_scale):
    scaled = d_inner * up_scale
    d_arg = scaled * up_val * (sigma + swish * (1.0 - sigma))
    return (scaled * swish).astype(BF), d_arg, (d_arg * (gate_scale * ROOT)).astype(BF)


def unit_tiles(units, tile):
    return [slice(start, start + tile) for start in range(0, units, tile)]


def ffn_kernel(mine, other, hidden, rate, up_w, gate_w, down_w, up_s, gate_s, *refs):
    part, low_ref, up_ref, gate_ref, one_ref, sums_far, one_far = refs[:7]
    sums_ref, inner_ref, x_ref, in_sems, out_sems = refs[7:]
    come, go = Copies(in_sems), Copies(out_sems)
    come.start(hidden.at[P_SIZE:], x_ref)
    sums = both(mine[...], other[...])
    sums_ref[...] = sums
    go.start(sums_ref, sums_far)
    come.wait()
    one = mix(x_ref[...].astype(F32), sums, rate[...])[0]
    one_ref[...] = one
    go.start(one_ref, one_far)
    low = one.astype(BF)
    low_ref[...] = low
    for cols in unit_tiles(up_w.shape[1], 512):
        up_val, gate_val = dot(low, up_w[:, cols]), dot(low, gate_w[:, cols])
        up_ref[:, cols] = up_val
        gate_ref[:, cols] = gate_val
        inner_ref[:, cols] = swiglu_of(up_val, gate_val, up_s[:, cols], gate_s[:, cols])[0]
    part[...] = dot(inner_ref[...], down_w[...]).astype(BF)
    go.wait()


def ffn(line, mine, other, hidden, rate, weights):
    units = weights[0].shape[1]
    outs = [
        shape(L, D, BF),
        shape(L, D, BF),
        near(L, units, F32),
        near(L, units, F32),
        near(L, D, F32),
        distant(L, D, F32),
        distant(L, D, F32),
    ]
    scratch = [vmem(L, D, F32), vmem(L, units, BF), vmem(L, D, BF), sems(1), sems(2)]
    ins = (mine, other, hidden, rate, *weights)
    flops = 6 * L * D * units
    return line.call(
        ffn_kernel, outs, ins, flops=flops, scratch=scratch, away=(2,), sent=(5, 6)
    )


def prompt_ffn_kernel(mine, other, hidden, rate, up_far, gate_far, down_far, up_s, gate_s, *refs):
    one_ref, *parts, inner_ref, x_ref, up_w, gate_w, down_w, in_sems = refs
    tiles = unit_tiles(up_w.shape[1], 512)
    groups = [((hidden.at[:P_SIZE], x_ref),)]
    for cols in tiles:
        groups.append(
            (
                (up_far.at[:, cols], up_w.at[:, cols]),
                (gate_far.at[:, cols], gate_w.at[:, cols]),
                (down_far.at[cols], down_w.at[cols]),
            )
        )
    arrive = Tiles(Copies(in_sems), groups, 3)
    arrive.wait(0)
    one = mix(x_ref[...].astype(F32), both(mine[...], other[...]), rate[...])[0]
    one_ref[...] = one
    low = one.astype(BF)
    for i, cols in enumerate(tiles):
        arrive.wait(1 + i)
        up_val, gate_val = dot(low, up_w[:, cols]), dot(low, gate_w[:, cols])
        inner_ref[:, cols] = swiglu_of(up_val, gate_val, up_s[:, cols], gate_s[:, cols])[0]
    total = dot(inner_ref[...], down_w[...]).astype(BF)
    for i, part in enumerate(parts):
        part[...] = total[i * part.shape[0] : (i + 1) * part.shape[0]]


def weight_scratch(weights):
    return [vmem(*weight.shape, BF) for weight in weights[:3]]


def prompt_ffn(line, mine, other, hidden, rate, weights):
    units = weights[0].shape[1]
    scratch = [
        vmem(P_SIZE, units, BF),
        vmem(P_SIZE, D, BF),
        *weight_scratch(weights),
        sems(1 + 3 * units // 512),
    ]
    ins = (mine, other, hidden, rate, *weights)
    outs = (distant(P_SIZE, D, F32), shape(P_SIZE // 2, D, BF), shape(P_SIZE // 2, D, BF))
    flops = 6 * P_SIZE * D * units
    return line.call(
        prompt_ffn_kernel, outs, ins, flops=flops, scratch=scratch, vmem=38, away=(2, 4, 5, 6)
    )


def ffn_back_kernel(mine, other, one, rate, teacher, valid, up_v, gate_v, *refs):
    up_w, gate_w, down_w, up_s, gate_s = refs[:5]
    part, low_ref, out_ref, dmix_ref, gains, d_up_ref, d_gate_ref = refs[5:]
    tiles = unit_tiles(up_w.shape[1], 512)
    row = lax.broadcasted_iota(jnp.int32, (L, L), 0)
    col = lax.broadcasted_iota(jnp.int32, (L, L), 1)
    counted = jnp.sum(jnp.where(row == col, valid[...].astype(F32), 0.0), axis=1, keepdims=True)
    old = one[...]
    out, unit, inverse_in, inverse_out = mix(old, both(mine[...], other[...]), rate[...])
    out_ref[...] = out
    diff = out - teacher[...].astype(F32)
    weighted = counted * diff
    by_row = jnp.sum(weighted * diff, axis=1, keepdims=True)
    dmix = norm_back(2.0 * weighted, out, inverse_out)
    dmix_ref[...] = dmix
    low = norm_back(dmix * rate[...], unit, inverse_in).astype(BF)
    low_ref[...] = low

    width = gains.shape[1]
    gains[...] = jnp.zeros_like(gains)

    def put(place, value):
        for start in range(0, value.shape[1], width):
            gains[place : place + 1] = value[:, start : start + width]
            place += 1

    put(0, jnp.sum(dmix * (unit - old), axis=0, keepdims=True))
    lane = lax.broadcasted_iota(jnp.int32, (1, width), 1)
    last = jnp.zeros((1, width), F32)
    for i, value in enumerate((by_row, counted)):
        value = jnp.sum(value, axis=0, keepdims=True)
        high = value.astype(BF).astype(F32)
        last = jnp.where(lane == 2 * i, high, last)
        last = jnp.where(lane == 2 * i + 1, value - high, last)
    put(13, last)
    for cols in tiles:
        d_inner = dot_nt(low, down_w[cols])
        up_val, gate_val = up_v[:, cols], gate_v[:, cols]
        _, sigma, swish = swiglu_of(up_val, gate_val, up_s[:, cols], gate_s[:, cols])
        d_up, d_arg, d_gate = swiglu_back(
            d_inner, up_val, sigma, swish, up_s[:, cols], gate_s[:, cols]
        )
        d_up_ref[:, cols] = d_up
        d_gate_ref[:, cols] = d_gate
        for place, value in ((4, d_inner * up_val * swish), (8, d_arg * ROOT * gate_val)):
            total = jnp.sum(value, axis=0, keepdims=True)
            done = cols.start
            while done < cols.stop:
                step = min(cols.stop, (done // width + 1) * width) - done
                left, at = done - cols.start, done % width
                gains[place + done // width : place + done // width + 1, at : at + step] = total[
                    :, left : left + step
                ]
                done += step
    total = dot_nt(d_up_ref[...], up_w[...]) + dot_nt(d_gate_ref[...], gate_w[...])
    part[...] = total.astype(BF)


def ffn_back(line, mine, other, one, rate, teacher, valid, up_val, gate_val, weights, width):
    units = weights[0].shape[1]
    outs = (
        distant(L, D, BF),
        distant(L, D, BF),
        distant(L, D, F32),
        distant(L, D, F32),
        distant(GAINS, width, F32),
    )
    scratch = [vmem(L, units, BF), vmem(L, units, BF)]
    ins = (mine, other, one, rate, teacher, valid, up_val, gate_val, *weights)
    flops = 6 * L * D * units
    return line.call(ffn_back_kernel, outs, ins, flops=flops, scratch=scratch)


def split_blocks(blocks, first, send_ref, keep_ref, start):
    size = blocks[0].shape[0]
    for j in range(0, len(blocks), 2):
        rows = slice(start + j // 2 * size, start + (j // 2 + 1) * size)
        even, odd = blocks[j], blocks[j + 1]
        send_ref[rows] = jnp.where(first, odd, even)
        keep_ref[rows] = jnp.where(first, even, odd)


def collect_kernel(far, info, *refs):
    parts, (ones_far, ones_t_far, ones, ones_t, in_sems, out_sems) = refs[:far], refs[far:]
    rows = parts[0].shape[0]
    come, go = Copies(in_sems), Copies(out_sems)
    for k, part in enumerate(parts):
        come.start(part, ones.at[pl.ds((info[PLACE_FAR] ^ k) * rows, rows)])
    come.wait()
    go.start(ones, ones_far)
    turn_part(far, info, ones, ones_t)
    go.start(ones_t, ones_t_far)
    go.wait()


def collect(line, info, parts):
    far, rows = len(parts), len(parts) * parts[0].shape[0]
    outs = (distant(rows, D, BF), distant(D // far, rows, BF))
    scratch = [vmem(rows, D, BF), vmem(D // far, rows, BF), sems(far), sems(2)]
    return line.call(
        functools.partial(collect_kernel, far),
        outs,
        (info, *parts),
        scratch=scratch,
        vmem=6,
        smem=1,
        loose=range(1, 1 + far),
        sent=(0, 1),
    )


def unit_factors_kernel(ones_far, up_far, gate_far, up_s, gate_s, *refs):
    far, (ones, up_w, gate_w), kept, (in_sems, out_sems) = refs[:3], refs[3:6], refs[6:9], refs[9:]
    go = Copies(out_sems)
    tiles = unit_tiles(up_w.shape[1], 512)
    groups = [((ones_far, ones),)]
    for cols in tiles:
        groups.append(
            ((up_far.at[:, cols], up_w.at[:, cols]), (gate_far.at[:, cols], gate_w.at[:, cols]))
        )
    arrive = Tiles(Copies(in_sems), groups, 3)
    arrive.wait(0)
    for i, cols in enumerate(tiles):
        arrive.wait(1 + i)
        up_scale, gate_scale = up_s[:, cols], gate_s[:, cols]
        up_val, gate_val = dot(ones[...], up_w[:, cols]), dot(ones[...], gate_w[:, cols])
        inner, sigma, swish = swiglu_of(up_val, gate_val, up_scale, gate_scale)
        kept[0][:, cols] = inner
        kept[1][:, cols] = (up_scale * swish).astype(BF)
        slope = sigma + swish * (1.0 - sigma)
        kept[2][:, cols] = (up_scale * (gate_scale * ROOT) * up_val * slope).astype(BF)
        for source, target in zip(kept, far):
            go.start(source.at[:, cols], target.at[:, cols])
    go.wait()


def turn_part(far, info, source, target):
    group = target.shape[0]
    for j in range(far):

        @pl.when(info[PLACE_FAR] == j)
        def _(j=j):
            target[...] = source[:, j * group : (j + 1) * group].T


def unit_factors(line, ones, weights):
    rows, units = ones.shape[0], weights[0].shape[1]
    outs = [distant(rows, units, BF)] * 3
    scratch = [vmem(rows, D, BF), vmem(D, units, BF), vmem(D, units, BF)]
    scratch += [vmem(rows, units, BF)] * 3 + [sems(1 + 2 * units // 512), sems(3 * units // 512)]
    return line.call(
        unit_factors_kernel,
        outs,
        (ones, weights[0], weights[1], weights[3], weights[4]),
        flops=4 * rows * D * units,
        scratch=scratch,
        vmem=36,
        away=(0, 1, 2),
        sent=(0, 1, 2),
    )


def ffn_grad_kernel(far, info, *refs):
    parts, (ones_t_far, down_far), refs = refs[:far], refs[far : far + 2], refs[far + 2 :]
    factors_far, (send, keep), refs = refs[:3], refs[3:5], refs[5:]
    ones_t, d_ffns, d_ffns_t, down_w, *factors, in_sems = refs
    rows = parts[0].shape[0]
    tiles = unit_tiles(down_w.shape[0], 512)
    first = [
        (part, d_ffns.at[pl.ds((info[PLACE_FAR] ^ k) * rows, rows)]) for k, part in enumerate(parts)
    ]
    groups = [[*first, (ones_t_far, ones_t)]]
    for cols in tiles:
        group = [(down_far.at[cols], down_w.at[cols])]
        group += [(a.at[:, cols], b.at[:, cols]) for a, b in zip(factors_far, factors)]
        groups.append(group)
    arrive = Tiles(Copies(in_sems), groups, 3)
    arrive.wait(0)
    turn_part(far, info, d_ffns, d_ffns_t)
    size = ones_t.shape[0] // 4
    for i, cols in enumerate(tiles):
        arrive.wait(1 + i)
        d_inner = dot_nt(d_ffns[...], down_w[cols])
        inner, to_up, to_gate = (factor[:, cols] for factor in factors)
        d_up = (d_inner * to_up.astype(F32)).astype(BF)
        d_gate = (d_inner * to_gate.astype(F32)).astype(BF)
        for k, (left, right) in enumerate(((ones_t, d_up), (ones_t, d_gate), (d_ffns_t, inner))):
            grad = dot(left[...], right).astype(BF)
            blocks = [grad[j * size : (j + 1) * size] for j in range(4)]
            split_blocks(blocks, info[CORE] == 0, send.at[:, cols], keep.at[:, cols], k * 2 * size)


def ffn_grad(line, info, parts, down_weight, ones_t, factors):
    far, units = len(parts), down_weight.shape[0]
    rows, group = far * parts[0].shape[0], D // far
    outs = [distant(3 * group // 2, units, BF)] * 2
    scratch = [vmem(group, rows, BF), vmem(rows, D, BF), vmem(group, rows, BF), vmem(units, D, BF)]
    scratch += [vmem(rows, units, BF)] * 3 + [sems(far + 1 + 4 * units // 512)]
    return line.call(
        functools.partial(ffn_grad_kernel, far),
        outs,
        (info, *parts, ones_t, down_weight, *factors),
        flops=2 * rows * (D + 3 * group) * units,
        scratch=scratch,
        vmem=36,
        smem=1,
        loose=range(1, 1 + far),
        away=range(1 + far, 6 + far),
    )


def plain_unit_grads(low, d_ffn, weights):
    up_w, gate_w, down_w, up_s, gate_s = weights
    up_val = dot(low, up_w)
    inner, sigma, swish = swiglu_of(up_val, dot(low, gate_w), up_s, gate_s)
    d_up, _, d_gate = swiglu_back(dot_nt(d_ffn, down_w), up_val, sigma, swish, up_s, gate_s)
    return dot_tn(low, d_up), dot_tn(low, d_gate), dot_tn(d_ffn, inner)


def turn_kernel(source, result):
    result[...] = source[...].T


def turn(line, value):
    rows, cols = value.shape
    value = pltpu.with_memory_space_constraint(value, pltpu.HBM)
    return line.call(turn_kernel, (distant(cols, rows, value.dtype),), (value,))[0]


def give(split, info, products, outs, done=lambda rows: None):
    for i, (left, right) in enumerate(products):
        grad = dot(left, right[...]).astype(BF)
        if split:
            size = D // 16
            blocks = [grad[j * size : (j + 1) * size] for j in range(16)]
            split_blocks(blocks, info[CORE] == 0, outs[0], outs[1], i * 8 * size)
            done(slice(i * 8 * size, (i + 1) * 8 * size))
        else:
            outs[i][...] = grad


BACK_INPUTS = (
    ("d_mine", BF),
    ("dmix_two", F32),
    ("one", F32),
    ("sums", F32),
    ("x_cont", BF),
    ("wo", BF),
    ("kr", F32),
    ("qr", F32),
    ("v", BF),
    ("gains", F32),
    ("x_t", BF),
    ("att", BF),
)


def attention_back_kernel(split, info, _, d_other, rate_two, rate_one, scale_ref, *refs):
    count = len(BACK_INPUTS)
    made = 2 if split else 4
    far, outs = refs[:count], refs[count : count + made]
    dq_far, dk_far, dv_far, residual_far, gains_out, _ = refs[count + made : count + made + 6]
    held, refs = refs[count + made + 6 : -9], refs[-9:]
    d_att, dq_ref, dk_ref, dv_ref, residual_ref, send_ref, keep_ref, in_sems, out_sems = refs
    come, go = Copies(in_sems), Copies(out_sems)
    ref = {}
    arrived = {}
    pairs = {}
    for (name, _), source, target in zip(BACK_INPUTS, far, held):
        ref[name] = target
        pairs[name] = (source.at[P_SIZE:] if name == "x_cont" else source, target)

    def begin(*names):
        for name in names:
            arrived[name] = come.start(*pairs[name]).wait

    begin("d_mine", "dmix_two", "one", "sums", "x_cont", "wo")

    for name in ("d_mine", "dmix_two", "one", "sums", "x_cont"):
        arrived[name]()
    begin("gains", "kr", "qr", "v", "att", "x_t")
    old = ref["x_cont"][...].astype(F32)
    _, unit_in, inverse_in, inverse_out = mix(old, ref["sums"][...], rate_one[...])
    d_one = both(ref["d_mine"][...], d_other[...])
    d_one = d_one + (1.0 - rate_two[...]) * ref["dmix_two"][...]
    dmix = norm_back(d_one, ref["one"][...], inverse_out)
    residual_ref[...] = dmix * (1.0 - rate_one[...])
    go.start(residual_ref, residual_far)
    att_grad = jnp.sum(dmix * (unit_in - old), axis=0, keepdims=True)
    d_attn = norm_back(dmix * rate_one[...], unit_in, inverse_in).astype(BF)
    arrived["wo"]()
    d_att[...] = dot_nt(d_attn, ref["wo"][...]).astype(BF)

    gains = ref["gains"]
    width = scale_ref.shape[1]
    arrived["gains"]()
    for i in range(D // width):
        gains[2 + i : 3 + i] = att_grad[:, i * width : (i + 1) * width]

    def raw_back(grad, unit, inverse, scale):
        scaled = grad * scale
        back = inverse * (scaled - unit * head_sums(scaled * unit))
        return back.astype(BF), jnp.sum(grad * unit, axis=0, keepdims=True)

    for name in ("kr", "qr", "v"):
        arrived[name]()
    for start in range(0, width, PAIR):
        cols = slice(start, start + PAIR)
        scale = scale_ref[:, cols]
        q_unit, q_inverse = unit_heads(ref["qr"][:, cols])
        k_unit, k_inverse = unit_heads(ref["kr"][:, cols])
        queries = halves((q_unit * scale).astype(BF))
        keys = (k_unit * scale).astype(BF)
        grads = halves(d_att[:, cols])
        probs = weights_of(queries, keys, P_SIZE)
        d_probs = dot_nt(grads, ref["v"][:, cols])
        delta = jnp.sum(d_probs * probs, axis=1, keepdims=True)
        d_scores = (probs * (d_probs - delta)).astype(BF)
        d_query = 8.0 * merge(dot(d_scores, keys))
        d_keys = 8.0 * dot_tn(d_scores, queries)
        dv_ref[:, cols] = dot_tn(probs.astype(BF), grads).astype(BF)
        dq_ref[:, cols], by_query = raw_back(d_query, q_unit, q_inverse, scale)
        dk_ref[:, cols], by_key = raw_back(d_keys, k_unit, k_inverse, scale)
        gains[12:13, cols] = by_query + by_key
    for source, target in ((dq_ref, dq_far), (dk_ref, dk_far), (dv_ref, dv_far)):
        go.start(source, target)

    arrived["x_t"]()
    arrived["att"]()
    x_t = ref["x_t"]
    products = (
        (x_t[...], dv_ref),
        (x_t[...], dk_ref),
        (x_t[:, P_SIZE:], dq_ref),
        (d_attn.T, ref["att"]),
    )
    gains_out[...] = gains[...]
    if split:
        far, outs = outs, (send_ref, keep_ref)

        def done(rows):
            for source, target in zip(outs, far):
                go.start(source.at[rows], target.at[rows])

        for out in outs:
            out[2 * D :] = gains[...].astype(BF)
        done(slice(2 * D, 2 * D + GAINS))
        give(split, info, products, outs, done)
    else:
        give(split, info, products, outs)
    go.wait()


def attention_back(line, split, info, passed, d_other, rate_two, rate_one, scale, ins):
    width = scale.shape[1]
    rows = ins["v"].shape[0]
    outs = [distant(2 * D + GAINS, width, BF)] * 2 if split else [shape(D, width, BF)] * 4
    first = len(outs)
    outs += [distant(L, width, BF), distant(rows, width, BF), distant(rows, width, BF)]
    outs += [distant(L, D, F32), shape(GAINS, width, F32), shape(*passed.shape, BF)]
    scratch = []
    for name, kind in BACK_INPUTS:
        scratch.append(vmem(L if name == "x_cont" else ins[name].shape[0], ins[name].shape[1], kind))
    scratch += [vmem(L, width, BF), vmem(L, width, BF), vmem(rows, width, BF), vmem(rows, width, BF)]
    scratch += [vmem(L, D, F32)] + [vmem(2 * D + GAINS if split else GAINS, width, BF)] * 2
    scratch += [sems(len(BACK_INPUTS)), sems(14)]
    flops = 20 * L * rows * width + 4 * (rows + L) * D * width + 4 * L * D * width
    return line.call(
        functools.partial(attention_back_kernel, split),
        outs,
        (info, passed, d_other, rate_two, rate_one, scale, *(ins[name] for name, _ in BACK_INPUTS)),
        flops=flops,
        scratch=scratch,
        vmem=44,
        smem=1,
        away=range(6, 6 + len(BACK_INPUTS)),
        loose=(1,),
        sent=(*range(2 if split else 0), first, first + 1, first + 2, first + 3, first + 5),
        aliases={1: first + 5},
    )


def fold_core_kernel(info, keep, got, *outs):
    size = D // 16
    total = (keep[...].astype(F32) + got[...].astype(F32)).astype(BF)
    for m in range(4):
        start = m * 8 * size
        blocks = [total[start + j * size : start + (j + 1) * size] for j in range(8)]
        send, kept = outs[:2] if m < 2 else outs[2:]
        split_blocks(blocks, info[PLACE_X] == 0, send, kept, m % 2 * 4 * size)
    for ref in outs[:2]:
        ref[8 * size :] = total[32 * size :]


def fold_kernel(matrices, count, bit, info, keep, got, send, kept):
    size = D // 16
    low = info[PLACE_FAR] // bit % 2 == 0
    total = (keep[...].astype(F32) + got[...].astype(F32)).astype(BF)
    half = count // 2
    for m in range(matrices):
        first = total[m * count * size : (m * count + half) * size]
        second = total[(m * count + half) * size : (m + 1) * count * size]
        rows = slice(m * half * size, (m + 1) * half * size)
        send[rows] = jnp.where(low, second, first)
        kept[rows] = jnp.where(low, first, second)
    if keep.shape[0] > matrices * count * size:
        for ref in (send, kept):
            ref[matrices * half * size :] = total[matrices * count * size :]


def finish_first_kernel(tokens, keep, got, *outs):
    value, key, mlp, att, up, gate, head, loss, factor_ref = outs
    size = value.shape[0]
    total = keep[...].astype(F32) + got[...].astype(F32)
    gains = total[2 * size :]
    factor = tokens / (gains[13:14, 2:3] + gains[13:14, 3:4])
    factor_ref[...] = factor
    loss[...] = factor * (gains[13:14, 0:1] + gains[13:14, 1:2])
    gains = gains * factor
    width = gains.shape[1]
    place = 0
    for ref in (mlp, att, up, gate, head):
        for start in range(0, ref.shape[1], width):
            ref[:, start : start + width] = gains[place : place + 1]
            place += 1
    value[...] = total[:size] * factor
    key[...] = total[size : 2 * size] * factor


def finish_second_kernel(factor, keep, got, query, out):
    size = query.shape[0]
    total = (keep[...].astype(F32) + got[...].astype(F32)) * factor[...]
    query[...] = total[:size]
    out[...] = total[size:]


def fold_units_kernel(info, keep, got, send_ref, keep_ref):
    size = keep.shape[0] // 6
    total = (keep[...].astype(F32) + got[...].astype(F32)).astype(BF)
    blocks = [total[j * size : (j + 1) * size] for j in range(6)]
    split_blocks(blocks, info[PLACE_X] == 0, send_ref, keep_ref, 0)


def finish_units_kernel(factor, keep, got, *results):
    total = (keep[...].astype(F32) + got[...].astype(F32)) * factor[...]
    size = total.shape[0] // 3
    for m, result in enumerate(results):
        result[...] = total[m * size : (m + 1) * size]


def rows_kernel(info, dq, dk, dv, wq_far, wk_far, wv_far, send_ref, keep_ref, wq, wk, wv, in_sems):
    come = Copies(in_sems)
    for source, target in ((wk_far, wk), (wv_far, wv), (wq_far, wq)):
        come.start(source, target)
    half = send_ref.shape[0]
    come.copies[0].wait()
    prompt = dot_nt(dk[...], wk[...])
    come.copies[1].wait()
    prompt = prompt + dot_nt(dv[...], wv[...])
    come.copies[2].wait()
    top = prompt[:half].astype(BF)
    low = jnp.concatenate(
        [prompt[half:P_SIZE], prompt[P_SIZE:] + dot_nt(dq[...], wq[...])], 0
    ).astype(BF)
    first = info[SIDE] == 0
    send_ref[...] = jnp.where(first, low, top)
    keep_ref[...] = jnp.where(first, top, low)


def share_kernel(info, keep, got, residual, kept_ref, sent_ref):
    half = keep.shape[0]
    total = keep[...].astype(F32) + got[...].astype(F32)
    row = lax.broadcasted_iota(jnp.int32, (half, 1), 0) + info[SIDE] * half
    away = (row < P_SIZE) & (info[OWN] == 0)
    sent_ref[...] = jnp.where(away, total, 0.0).astype(BF)
    kept_ref[...] = jnp.where(away, 0.0, total)
    kept_ref[half - L :] += jnp.where(info[SIDE] == 1, residual[...], 0.0)


def last_share_kernel(kept, got, factor, result):
    result[...] = (kept[...] + got[...].astype(F32)) * factor[...]


def last_mix_kernel(one, rate, out, *refs):
    parts, result = refs[:-1], refs[-1]
    count = len(parts) // 2
    size = P_SIZE // count
    for i in range(count):
        rows = slice(i * size, (i + 1) * size)
        result[rows] = mix(one[rows], both(parts[i][...], parts[count + i][...]), rate[...])[0]
    result[P_SIZE:] = out[...]


def local(
    hidden_in,
    query_weight,
    key_weight,
    value_weight,
    out_weight,
    up_weight,
    gate_weight,
    down_weight,
    head_scale,
    attention_rate,
    up_scale,
    gate_scale,
    swiglu_rate,
    teacher,
    valid_mask,
    group_ids,
):
    count_dp = lax.axis_size("dp")
    far = count_dp // 4
    split = far == 4
    me = lax.axis_index("dp")
    rows = hidden_in.shape[0]
    width = query_weight.shape[1]
    units = up_weight.shape[1]
    scale = head_scale.reshape(1, width)
    rate_one = attention_rate.reshape(1, D)
    rate_two = swiglu_rate.reshape(1, D)
    own = (group_ids[0] == me).astype(jnp.int32)
    info = jnp.stack([own, me % 2, me // 2 % 2, me // 4, lax.axis_index("tensor")])
    info = info.astype(jnp.int32)
    qkvo = (query_weight, key_weight, value_weight, out_weight)
    ffn_weights = (
        up_weight,
        gate_weight,
        down_weight,
        up_scale.reshape(1, units),
        gate_scale.reshape(1, units),
    )

    line = Line()

    other_x = swap(hidden_in, "dp", 1)
    a_mine, att, x_seen, values, query_raw, key_raw, *qkvo_near = cont_attention(
        line, info, hidden_in, other_x, qkvo, scale
    )
    a_other = swap(a_mine, "tensor", 1)
    p_mine, *ffn_near = prompt_attention(line, hidden_in, qkvo_near, scale, ffn_weights[:3])
    ffn_near = (*ffn_near, *ffn_weights[3:])
    m_mine, one_low, up_val, gate_val, one_near, attn_sums, one = ffn(
        line, a_mine, a_other, hidden_in, rate_one, ffn_near
    )
    m_other = swap(m_mine, "tensor", 1)
    x_seen_t = turn(line, x_seen)
    d_mine, d_ffn, out, dmix_two, gains = ffn_back(
        line,
        m_mine,
        m_other,
        one_near,
        rate_two,
        teacher,
        valid_mask.reshape(1, L),
        up_val,
        gate_val,
        ffn_near,
        width,
    )
    total_cont = count_dp * valid_mask.shape[0]
    mine = D // count_dp
    usual = group_ids[0] >= 0
    half_rows = shape(rows // 2, D, BF)

    d_other = swap(d_mine, "tensor", 1)
    if split:
        ones = [one_low]
        bit = 4
        while bit < count_dp:
            ones += [swap(part, "dp", bit) for part in ones]
            bit *= 2
        ones, ones_t = collect(line, info, ones)
    *first, d_query, d_key, d_value, residual, gains, p_mine = attention_back(
        line,
        split,
        info,
        p_mine,
        d_other,
        rate_two,
        rate_one,
        scale,
        {
            "d_mine": d_mine,
            "dmix_two": dmix_two,
            "one": one,
            "sums": attn_sums,
            "x_cont": hidden_in,
            "wo": out_weight,
            "kr": key_raw,
            "qr": query_raw,
            "v": values,
            "gains": gains,
            "x_t": x_seen_t,
            "att": att,
        },
    )

    p_other = swap(p_mine, "tensor", 1)

    def fold(line, send, keep, count, bit):
        more = keep.shape[0] - 2 * count * mine
        return line.call(
            functools.partial(fold_kernel, 2, count, bit),
            [shape(count * mine + more, width, BF)] * 2,
            (info, keep, send),
            smem=1,
        )

    def rows_step(info, before, first, d_query, d_key, d_value, ones):
        inner = Line(before)
        if split:
            got = swap(first[0], "dp", 1)
        rows_pair = inner.call(
            rows_kernel,
            (half_rows, half_rows),
            (info, d_query, d_key, d_value, query_weight, key_weight, value_weight),
            flops=6 * rows * D * width,
            scratch=[vmem(D, width, BF)] * 3 + [sems(3)],
            vmem=22,
            smem=1,
            away=(4, 5, 6),
        )
        if not split:
            return first, rows_pair, (), inner.last
        send_a, keep_a, send_b, keep_b = inner.call(
            fold_core_kernel,
            [shape(D // 2 + GAINS, width, BF)] * 2 + [shape(D // 2, width, BF)] * 2,
            (info, first[1], got),
            smem=1,
        )
        got_a = swap(send_a, "dp", 2)
        factors = unit_factors(inner, ones, ffn_weights)
        send_a, keep_a = fold(inner, got_a, keep_a, 4, 2)
        return (send_a, keep_a, send_b, keep_b), rows_pair, factors, inner.last

    if not split:
        ones = one_low
    first, (rows_sent, kept), factors, line.last = section(
        usual, rows_step, info, line.last, first, d_query, d_key, d_value, ones
    )
    share = swap(rows_sent, "tensor", 1)
    if split:
        send_a, keep_a, send_b, keep_b = first
        got_a, got_b = swap(send_a, "dp", 8), swap(send_b, "dp", 2)
        d_ffns = [d_ffn] + [swap(d_ffn, "dp", 4 * k) for k in range(1, far)]
        u_send, u_keep = ffn_grad(line, info, d_ffns, down_weight, ones_t, factors)
    else:
        u_send = u_keep = None
    one_p, *mp_mine = prompt_ffn(line, p_mine, p_other, hidden_in, rate_one, ffn_weights)
    mp_other = [swap(part, "tensor", 1) for part in mp_mine]
    if split:
        send_a, keep_a = fold(line, got_a, keep_a, 2, 1)
        got_a = swap(send_a, "dp", 4)

    def share_step(info, before, share_keep, share, residual, u_send, u_keep):
        inner = Line(before)
        if split:
            got = swap(u_send, "dp", 1)
        kept, sent = inner.call(
            share_kernel,
            (distant(rows // 2, D, F32), half_rows),
            (info, share_keep, share, residual),
            smem=1,
        )
        if split:
            u_send, u_keep = inner.call(
                fold_units_kernel, (shape(3 * mine, units, BF),) * 2, (info, u_keep, got), smem=1
            )
        return kept, sent, u_send, u_keep, inner.last

    kept, sent, u_send, u_keep, line.last = section(
        usual, share_step, info, line.last, kept, share, residual, u_send, u_keep
    )
    share = swap(sent, "dp", 1)
    if split:
        u_got = swap(u_send, "dp", 2)
        send_b, keep_b = fold(line, got_b, keep_b, 4, 2)
        got_b = swap(send_b, "dp", 8)
    if split:
        value_grad, key_grad, mlp, att_rate, up_g, gate_g, head, loss, factor = line.call(
            functools.partial(finish_first_kernel, total_cont),
            [distant(mine, width, F32)] * 2
            + [shape(1, n, F32) for n in (D, D, units, units, width, 1, 1)],
            (keep_a, got_a),
        )
    else:
        total = sum_all(gains)
        factor = total_cont / (total[13:14, 2:3] + total[13:14, 3:4])
        loss = factor * (total[13:14, 0:1] + total[13:14, 1:2])
        flat = (total * factor).reshape(-1)
        mlp, att_rate, up_g, gate_g, head = (
            flat[start : start + size]
            for start, size in (
                (0, D),
                (D, D),
                (2 * D, units),
                (2 * D + units, units),
                (2 * D + 2 * units, width),
            )
        )

        def scattered(grad):
            grad = grad.astype(F32)
            return factor * lax.psum_scatter(grad, "dp", scatter_dimension=0, tiled=True)

        value_grad, key_grad, query_grad, out_grad = (scattered(grad) for grad in first)
        up_grad, gate_grad, down_grad = (
            scattered(grad) for grad in plain_unit_grads(one_low, d_ffn, ffn_weights)
        )
    grad_hidden = line.call(
        last_share_kernel, (distant(rows // 2, D, F32),), (kept, share, factor), held=(0,)
    )[0]
    if split:
        send_b, keep_b = fold(line, got_b, keep_b, 2, 1)
        got_b = swap(send_b, "dp", 4)
    hidden_out = line.call(
        last_mix_kernel,
        (distant(rows, D, F32),),
        (one_p, rate_two, out, *mp_mine, *mp_other),
        held=(0, 2),
    )[0]
    if split:
        query_grad, out_grad = line.call(
            finish_second_kernel, [distant(mine, width, F32)] * 2, (factor, keep_b, got_b)
        )
        up_grad, gate_grad, down_grad = line.call(
            finish_units_kernel, (distant(mine, units, F32),) * 3, (factor, u_keep, u_got)
        )
    return (
        hidden_out,
        loss[0, 0],
        grad_hidden,
        query_grad,
        key_grad,
        value_grad,
        out_grad.T,
        up_grad,
        gate_grad,
        down_grad.T,
        head.reshape(-1),
        att_rate.reshape(-1),
        up_g.reshape(-1),
        gate_g.reshape(-1),
        mlp.reshape(-1),
    )


def solution(mesh):
    placed = (
        P("dp", None),
        P(None, "tensor"),
        P(None, "tensor"),
        P(None, "tensor"),
        P("tensor", None),
        P(None, "tensor"),
        P(None, "tensor"),
        P("tensor", None),
        P("tensor"),
        P(),
        P("tensor"),
        P("tensor"),
        P(),
        P("dp", None),
        P("dp"),
        P("dp"),
    )
    return jax.shard_map(
        local,
        mesh=mesh,
        in_specs=placed,
        out_specs=(
            P("dp", None),
            P(),
            P(("dp", "tensor"), None),
            P("dp", "tensor"),
            P("dp", "tensor"),
            P("dp", "tensor"),
            P("tensor", "dp"),
            P("dp", "tensor"),
            P("dp", "tensor"),
            P("tensor", "dp"),
            P("tensor"),
            P(),
            P("tensor"),
            P("tensor"),
            P(),
        ),
        check_vma=False,
    )
```

```python
import functools
import math

import jax
import jax.numpy as jnp
from jax import lax
from jax.experimental import pallas as pl
from jax.experimental.pallas import tpu as pltpu
from jax.sharding import PartitionSpec as P

D = 1280
HD = 64
P_SIZE = 384
L = 128
PAIR = 2 * HD
EPS = 1e-06
ROOT = math.sqrt(D)
BF = jnp.bfloat16
F32 = jnp.float32
MIB = 2**20
GAINS = 16
OWN, CORE, PLACE_X, PLACE_FAR, SIDE = range(5)


def swap(value, axis, bit):
    count = lax.axis_size(axis)
    return lax.ppermute(value, axis, [(i, i ^ bit) for i in range(count)])


def sum_all(value):
    bit = 1
    while bit < lax.axis_size("dp"):
        value = value + swap(value, "dp", bit)
        bit *= 2
    return value


def dot(left, right):
    return jnp.dot(left, right, preferred_element_type=F32)


def dot_nt(left, right):
    return lax.dot_general(left, right, (((1,), (1,)), ((), ())), preferred_element_type=F32)


def dot_tn(left, right):
    return lax.dot_general(left, right, (((0,), (0,)), ((), ())), preferred_element_type=F32)


def inverse_norm(values):
    return lax.rsqrt(jnp.sum(values * values, axis=-1, keepdims=True) + EPS)


def norm_back(grad, unit, inverse):
    return inverse * (grad - unit * jnp.sum(grad * unit, axis=-1, keepdims=True))


def mix(old, sums, rate):
    inverse_in = inverse_norm(sums)
    unit_in = sums * inverse_in
    mixed = old + rate * (unit_in - old)
    inverse_out = inverse_norm(mixed)
    return mixed * inverse_out, unit_in, inverse_in, inverse_out


def both(mine, other):
    return mine.astype(F32) + other.astype(F32)


class Line:
    def __init__(self, last=None):
        self.last = last

    def call(
        self, kernel, outs, ins, *, flops=0, scratch=(), vmem=12, smem=0, away=(), held=(), loose=(), sent=(), aliases=()
    ):
        moved = sum(math.prod(v.shape) * v.dtype.itemsize for v in (*ins, *outs))
        count, results = len(ins), len(outs)
        places = [pltpu.SMEM] * smem + [pltpu.VMEM] * (count - smem)
        ins = list(ins)
        for i in (*loose, *away):
            places[i] = pl.ANY
        for i in (*held, *away):
            ins[i] = pltpu.with_memory_space_constraint(ins[i], pltpu.HBM)
        out_places = [pl.ANY if i in sent else pltpu.VMEM for i in range(results)] + [pl.ANY]
        if self.last is not None:
            places.append(pl.ANY)
            ins.append(pltpu.with_memory_space_constraint(self.last, pltpu.HBM))
        first = len(ins)

        def body(*refs):
            kernel(*refs[:count], *refs[first : first + results], *refs[first + results + 1 :])

        *done, self.last = pl.pallas_call(
            body,
            out_shape=(*outs, distant(8, 128, F32)),
            in_specs=[pl.BlockSpec(memory_space=place) for place in places],
            out_specs=tuple(pl.BlockSpec(memory_space=place) for place in out_places),
            scratch_shapes=list(scratch),
            input_output_aliases=dict(aliases),
            compiler_params=pltpu.CompilerParams(vmem_limit_bytes=vmem * MIB),
            cost_estimate=pl.CostEstimate(flops=flops, bytes_accessed=moved, transcendentals=0),
        )(*ins)
        return done


def section(usual, work, *ins):
    shapes = jax.eval_shape(work, *ins)
    return lax.cond(
        usual, work, lambda *_: jax.tree.map(lambda v: jnp.zeros(v.shape, v.dtype), shapes), *ins
    )


class Copies:
    def __init__(self, sems):
        self.sems, self.copies = sems, []

    def start(self, source, target):
        copy = pltpu.make_async_copy(source, target, self.sems.at[len(self.copies)])
        copy.start()
        self.copies.append(copy)
        return copy

    def wait(self):
        for copy in self.copies:
            copy.wait()


class Tiles:
    def __init__(self, come, groups, ahead=2):
        self.come, self.groups, self.ahead, self.going = come, groups, ahead, []
        for _ in range(ahead):
            self.more()

    def more(self):
        if len(self.going) < len(self.groups):
            group = self.groups[len(self.going)]
            self.going.append([self.come.start(source, target) for source, target in group])

    def wait(self, i):
        for copy in self.going[i]:
            copy.wait()
        self.more()


def distant(rows, cols, kind):
    return pltpu.HBM((rows, cols), kind)


def vmem(rows, cols, kind):
    return pltpu.VMEM((rows, cols), kind)


def sems(count):
    return pltpu.SemaphoreType.DMA((count,))


def near(rows, cols, kind):
    return pltpu.VMEM((rows, cols), kind)


def fetch(pairs, sems):
    copies = [pltpu.make_async_copy(a, b, sems.at[i]) for i, (a, b) in enumerate(pairs)]
    for copy in copies:
        copy.start()
    return copies


def shape(rows, cols, kind):
    return jax.ShapeDtypeStruct((rows, cols), kind)


def head_sums(values):
    rows = lax.broadcasted_iota(jnp.int32, (PAIR, PAIR), 0) // HD
    cols = lax.broadcasted_iota(jnp.int32, (PAIR, PAIR), 1) // HD
    ones = jnp.where(rows == cols, 1.0, 0.0).astype(BF)
    high = values.astype(BF)
    low = (values - high.astype(F32)).astype(BF)
    return dot(high, ones) + dot(low, ones)


def unit_heads(raw):
    inverse = lax.rsqrt(head_sums(raw * raw) + EPS)
    return raw * inverse, inverse


def halves(value):
    first = lax.broadcasted_iota(jnp.int32, value.shape, 1) < HD
    zero = jnp.zeros_like(value)
    return jnp.concatenate([jnp.where(first, value, zero), jnp.where(first, zero, value)], 0)


def merge(value):
    rows = value.shape[0] // 2
    first = lax.broadcasted_iota(jnp.int32, (rows, PAIR), 1) < HD
    return jnp.where(first, value[:rows], value[rows:])


def weights_of(queries, keys, offset):
    scores = 8.0 * dot_nt(queries, keys)
    rows = queries.shape[0] // 2
    row = lax.broadcasted_iota(jnp.int32, scores.shape, 0)
    row = jnp.where(row >= rows, row - rows, row)
    col = lax.broadcasted_iota(jnp.int32, scores.shape, 1)
    expo = jnp.where(col <= row + offset, jnp.exp(scores), 0.0)
    return expo * (1.0 / jnp.sum(expo, axis=1, keepdims=True))


def attention_body(x, offset, weights, scale_ref, refs, arrived, ready, keep=lambda *_: None):
    wq_ref, wk_ref, wv_ref, wo_ref = weights
    att_ref, part_ref, v_ref, qr_ref, kr_ref = refs
    arrived(0)
    kr_ref[...] = dot(x, wk_ref[...])
    ready(0)
    arrived(1)
    v_ref[...] = dot(x, wv_ref[...]).astype(BF)
    ready(1)
    arrived(2)
    qr_ref[...] = dot(x[offset:], wq_ref[...])
    ready(2)
    for start in range(0, wq_ref.shape[1], PAIR):
        cols = slice(start, start + PAIR)
        scale = scale_ref[:, cols]
        keys = (unit_heads(kr_ref[:, cols])[0] * scale).astype(BF)
        queries = (unit_heads(qr_ref[:, cols])[0] * scale).astype(BF)
        probs = weights_of(halves(queries), keys, offset).astype(BF)
        keep(start, cols, queries, keys, probs)
        att_ref[:, cols] = merge(dot(probs, v_ref[:, cols])).astype(BF)
    ready(3)
    arrived(3)
    part_ref[...] = dot(att_ref[...], wo_ref[...]).astype(BF)


def cont_kernel(info, hidden, other, wq, wk, wv, wo, scale, *refs):
    part, att_far, x_far, v_far, qr_far, kr_far, q_far, k_far, p_far = refs[:9]
    wq_near, wk_near, wv_near, wo_near = refs[9:13]
    own_x, other_x, x_ref, att, v_ref, qr, kr, q_ref, k_ref, p_ref, in_sems, out_sems = refs[13:]
    come, go = Copies(in_sems), Copies(out_sems)
    arrive = Tiles(
        come,
        (
            ((hidden, own_x), (other.at[:P_SIZE], other_x)),
            ((wk, wk_near),),
            ((wv, wv_near),),
            ((wq, wq_near),),
            ((wo, wo_near),),
        ),
    )
    arrive.wait(0)
    x_ref[:P_SIZE] = jnp.where(info[OWN] == 1, own_x[:P_SIZE], other_x[...])
    x_ref[P_SIZE:] = own_x[P_SIZE:]
    go.start(x_ref, x_far)
    results = ((kr, kr_far), (v_ref, v_far), (qr, qr_far), (att, att_far))

    def keep(start, cols, queries, keys, probs):
        rows = slice(2 * L * (start // PAIR), 2 * L * (start // PAIR + 1))
        q_ref[:, cols] = queries
        k_ref[:, cols] = keys
        p_ref[rows] = probs
        go.start(k_ref.at[:, cols], k_far.at[:, cols])
        go.start(p_ref.at[rows], p_far.at[rows])

    attention_body(
        x_ref[...],
        P_SIZE,
        (wq_near, wk_near, wv_near, wo_near),
        scale,
        (att, part, v_ref, qr, kr),
        lambda i: arrive.wait(1 + i),
        lambda i: go.start(*results[i]),
        keep,
    )
    go.start(q_ref, q_far)
    go.wait()


def cont_attention(line, info, hidden, other, weights, scale):
    rows, width = hidden.shape[0], scale.shape[1]
    outs = [
        shape(L, D, BF),
        distant(L, width, BF),
        distant(rows, D, BF),
        distant(rows, width, BF),
        distant(L, width, F32),
        distant(rows, width, F32),
        distant(L, width, BF),
        distant(rows, width, BF),
        distant(width // HD * L, rows, BF),
    ] + [near(*weight.shape, BF) for weight in weights]
    scratch = [
        vmem(rows, D, BF),
        vmem(P_SIZE, D, BF),
        vmem(rows, D, BF),
        vmem(L, width, BF),
        vmem(rows, width, BF),
        vmem(L, width, F32),
        vmem(rows, width, F32),
        vmem(L, width, BF),
        vmem(rows, width, BF),
        vmem(width // HD * L, rows, BF),
        sems(6),
        sems(6 + 2 * (width // PAIR)),
    ]
    flops = 4 * rows * D * width + 4 * L * D * width + 8 * L * rows * width
    return line.call(
        cont_kernel,
        outs,
        (info, hidden, other, *weights, scale),
        flops=flops,
        scratch=scratch,
        vmem=28,
        smem=1,
        away=(1, 3, 4, 5, 6),
        loose=(2,),
        sent=range(1, 9),
    )


def prompt_kernel(hidden, wq, wk, wv, wo, scale, up, gate, down, *refs):
    part, up_near, gate_near, down_near, x_ref, att, v_ref, qr, kr, in_sems = refs
    come = Copies(in_sems)
    come.start(hidden.at[:P_SIZE], x_ref)
    for source, target in ((up, up_near), (gate, gate_near), (down, down_near)):
        come.start(source, target)
    come.copies[0].wait()
    attention_body(
        x_ref[...],
        0,
        (wq, wk, wv, wo),
        scale,
        (att, part, v_ref, qr, kr),
        lambda i: None,
        lambda i: None,
    )
    for copy in come.copies[1:]:
        copy.wait()


def prompt_attention(line, hidden, weights, scale, later):
    width = scale.shape[1]
    scratch = [
        vmem(P_SIZE, D, BF),
        vmem(P_SIZE, width, BF),
        vmem(P_SIZE, width, BF),
        vmem(P_SIZE, width, F32),
        vmem(P_SIZE, width, F32),
        sems(4),
    ]
    outs = [shape(P_SIZE, D, BF)] + [near(*weight.shape, BF) for weight in later]
    flops = 8 * P_SIZE * D * width + 8 * P_SIZE * P_SIZE * width
    ins = (hidden, *weights, scale, *later)
    return line.call(
        prompt_kernel, outs, ins, flops=flops, scratch=scratch, vmem=13, away=(0, 6, 7, 8)
    )


def swiglu_of(up_val, gate_val, up_scale, gate_scale):
    half = (gate_scale * (0.5 * ROOT)) * gate_val
    more = jnp.tanh(half) + 1.0
    swish = half * more
    return (up_scale * up_val * swish).astype(BF), 0.5 * more, swish


def swiglu_back(d_inner, up_val, sigma, swish, up_scale, gate_scale):
    scaled = d_inner * up_scale
    d_arg = scaled * up_val * (sigma + swish * (1.0 - sigma))
    return (scaled * swish).astype(BF), d_arg, (d_arg * (gate_scale * ROOT)).astype(BF)


def unit_tiles(units, tile):
    return [slice(start, start + tile) for start in range(0, units, tile)]


def ffn_kernel(mine, other, hidden, rate, up_w, gate_w, down_w, up_s, gate_s, *refs):
    part, low_ref, up_ref, gate_ref, one_ref, sums_far, one_far = refs[:7]
    sums_ref, inner_ref, x_ref, in_sems, out_sems = refs[7:]
    come, go = Copies(in_sems), Copies(out_sems)
    come.start(hidden.at[P_SIZE:], x_ref)
    sums = both(mine[...], other[...])
    sums_ref[...] = sums
    go.start(sums_ref, sums_far)
    come.wait()
    one = mix(x_ref[...].astype(F32), sums, rate[...])[0]
    one_ref[...] = one
    go.start(one_ref, one_far)
    low = one.astype(BF)
    low_ref[...] = low
    for cols in unit_tiles(up_w.shape[1], 512):
        up_val, gate_val = dot(low, up_w[:, cols]), dot(low, gate_w[:, cols])
        up_ref[:, cols] = up_val
        gate_ref[:, cols] = gate_val
        inner_ref[:, cols] = swiglu_of(up_val, gate_val, up_s[:, cols], gate_s[:, cols])[0]
    part[...] = dot(inner_ref[...], down_w[...]).astype(BF)
    go.wait()


def ffn(line, mine, other, hidden, rate, weights):
    units = weights[0].shape[1]
    outs = [
        shape(L, D, BF),
        shape(L, D, BF),
        near(L, units, F32),
        near(L, units, F32),
        near(L, D, F32),
        distant(L, D, F32),
        distant(L, D, F32),
    ]
    scratch = [vmem(L, D, F32), vmem(L, units, BF), vmem(L, D, BF), sems(1), sems(2)]
    ins = (mine, other, hidden, rate, *weights)
    flops = 6 * L * D * units
    return line.call(
        ffn_kernel, outs, ins, flops=flops, scratch=scratch, away=(2,), sent=(5, 6)
    )


def prompt_ffn_kernel(mine, other, hidden, rate, up_far, gate_far, down_far, up_s, gate_s, *refs):
    one_ref, *parts, inner_ref, x_ref, up_w, gate_w, down_w, in_sems = refs
    tiles = unit_tiles(up_w.shape[1], 512)
    groups = [((hidden.at[:P_SIZE], x_ref),)]
    for cols in tiles:
        groups.append(
            (
                (up_far.at[:, cols], up_w.at[:, cols]),
                (gate_far.at[:, cols], gate_w.at[:, cols]),
                (down_far.at[cols], down_w.at[cols]),
            )
        )
    arrive = Tiles(Copies(in_sems), groups, 3)
    arrive.wait(0)
    one = mix(x_ref[...].astype(F32), both(mine[...], other[...]), rate[...])[0]
    one_ref[...] = one
    low = one.astype(BF)
    for i, cols in enumerate(tiles):
        arrive.wait(1 + i)
        up_val, gate_val = dot(low, up_w[:, cols]), dot(low, gate_w[:, cols])
        inner_ref[:, cols] = swiglu_of(up_val, gate_val, up_s[:, cols], gate_s[:, cols])[0]
    total = dot(inner_ref[...], down_w[...]).astype(BF)
    for i, part in enumerate(parts):
        part[...] = total[i * part.shape[0] : (i + 1) * part.shape[0]]


def weight_scratch(weights):
    return [vmem(*weight.shape, BF) for weight in weights[:3]]


def prompt_ffn(line, mine, other, hidden, rate, weights):
    units = weights[0].shape[1]
    scratch = [
        vmem(P_SIZE, units, BF),
        vmem(P_SIZE, D, BF),
        *weight_scratch(weights),
        sems(1 + 3 * units // 512),
    ]
    ins = (mine, other, hidden, rate, *weights)
    outs = (distant(P_SIZE, D, F32), shape(P_SIZE // 2, D, BF), shape(P_SIZE // 2, D, BF))
    flops = 6 * P_SIZE * D * units
    return line.call(
        prompt_ffn_kernel,
        outs,
        ins,
        flops=flops,
        scratch=scratch,
        vmem=38,
        away=(2, 4, 5, 6),
        held=(0, 1),
    )


def ffn_back_kernel(mine, other, one, rate, teacher, valid, up_v, gate_v, *refs):
    up_w, gate_w, down_w, up_s, gate_s = refs[:5]
    part, low_ref, out_ref, dmix_ref, gains, d_up_ref, d_gate_ref = refs[5:]
    tiles = unit_tiles(up_w.shape[1], 512)
    row = lax.broadcasted_iota(jnp.int32, (L, L), 0)
    col = lax.broadcasted_iota(jnp.int32, (L, L), 1)
    counted = jnp.sum(jnp.where(row == col, valid[...].astype(F32), 0.0), axis=1, keepdims=True)
    old = one[...]
    out, unit, inverse_in, inverse_out = mix(old, both(mine[...], other[...]), rate[...])
    out_ref[...] = out
    diff = out - teacher[...].astype(F32)
    weighted = counted * diff
    by_row = jnp.sum(weighted * diff, axis=1, keepdims=True)
    dmix = norm_back(2.0 * weighted, out, inverse_out)
    dmix_ref[...] = dmix
    low = norm_back(dmix * rate[...], unit, inverse_in).astype(BF)
    low_ref[...] = low

    width = gains.shape[1]
    gains[...] = jnp.zeros_like(gains)

    def put(place, value):
        for start in range(0, value.shape[1], width):
            gains[place : place + 1] = value[:, start : start + width]
            place += 1

    put(0, jnp.sum(dmix * (unit - old), axis=0, keepdims=True))
    lane = lax.broadcasted_iota(jnp.int32, (1, width), 1)
    last = jnp.zeros((1, width), F32)
    for i, value in enumerate((by_row, counted)):
        value = jnp.sum(value, axis=0, keepdims=True)
        high = value.astype(BF).astype(F32)
        last = jnp.where(lane == 2 * i, high, last)
        last = jnp.where(lane == 2 * i + 1, value - high, last)
    put(13, last)
    for cols in tiles:
        d_inner = dot_nt(low, down_w[cols])
        up_val, gate_val = up_v[:, cols], gate_v[:, cols]
        _, sigma, swish = swiglu_of(up_val, gate_val, up_s[:, cols], gate_s[:, cols])
        d_up, d_arg, d_gate = swiglu_back(
            d_inner, up_val, sigma, swish, up_s[:, cols], gate_s[:, cols]
        )
        d_up_ref[:, cols] = d_up
        d_gate_ref[:, cols] = d_gate
        for place, value in ((4, d_inner * up_val * swish), (8, d_arg * ROOT * gate_val)):
            total = jnp.sum(value, axis=0, keepdims=True)
            done = cols.start
            while done < cols.stop:
                step = min(cols.stop, (done // width + 1) * width) - done
                left, at = done - cols.start, done % width
                gains[place + done // width : place + done // width + 1, at : at + step] = total[
                    :, left : left + step
                ]
                done += step
    total = dot_nt(d_up_ref[...], up_w[...]) + dot_nt(d_gate_ref[...], gate_w[...])
    part[...] = total.astype(BF)


def ffn_back(line, mine, other, one, rate, teacher, valid, up_val, gate_val, weights, width):
    units = weights[0].shape[1]
    outs = (
        distant(L, D, BF),
        distant(L, D, BF),
        distant(L, D, F32),
        distant(L, D, F32),
        distant(GAINS, width, F32),
    )
    scratch = [vmem(L, units, BF), vmem(L, units, BF)]
    ins = (mine, other, one, rate, teacher, valid, up_val, gate_val, *weights)
    flops = 6 * L * D * units
    return line.call(ffn_back_kernel, outs, ins, flops=flops, scratch=scratch)


def split_blocks(blocks, first, send_ref, keep_ref, start):
    size = blocks[0].shape[0]
    for j in range(0, len(blocks), 2):
        rows = slice(start + j // 2 * size, start + (j // 2 + 1) * size)
        even, odd = blocks[j], blocks[j + 1]
        send_ref[rows] = jnp.where(first, odd, even)
        keep_ref[rows] = jnp.where(first, even, odd)


def collect_kernel(far, info, *refs):
    parts, (ones_far, ones_t_far, ones, ones_t, in_sems, out_sems) = refs[:far], refs[far:]
    rows = parts[0].shape[0]
    come, go = Copies(in_sems), Copies(out_sems)
    for k, part in enumerate(parts):
        come.start(part, ones.at[pl.ds((info[PLACE_FAR] ^ k) * rows, rows)])
    come.wait()
    go.start(ones, ones_far)
    turn_part(far, info, ones, ones_t)
    go.start(ones_t, ones_t_far)
    go.wait()


def collect(line, info, parts):
    far, rows = len(parts), len(parts) * parts[0].shape[0]
    outs = (distant(rows, D, BF), distant(D // far, rows, BF))
    scratch = [vmem(rows, D, BF), vmem(D // far, rows, BF), sems(far), sems(2)]
    return line.call(
        functools.partial(collect_kernel, far),
        outs,
        (info, *parts),
        scratch=scratch,
        vmem=6,
        smem=1,
        loose=range(1, 1 + far),
        sent=(0, 1),
    )


def unit_factors_kernel(ones_far, up_far, gate_far, up_s, gate_s, *refs):
    far, (ones, up_w, gate_w), kept, (in_sems, out_sems) = refs[:3], refs[3:6], refs[6:9], refs[9:]
    go = Copies(out_sems)
    tiles = unit_tiles(up_w.shape[1], 512)
    groups = [((ones_far, ones),)]
    for cols in tiles:
        groups.append(
            ((up_far.at[:, cols], up_w.at[:, cols]), (gate_far.at[:, cols], gate_w.at[:, cols]))
        )
    arrive = Tiles(Copies(in_sems), groups, 3)
    arrive.wait(0)
    for i, cols in enumerate(tiles):
        arrive.wait(1 + i)
        up_scale, gate_scale = up_s[:, cols], gate_s[:, cols]
        up_val, gate_val = dot(ones[...], up_w[:, cols]), dot(ones[...], gate_w[:, cols])
        inner, sigma, swish = swiglu_of(up_val, gate_val, up_scale, gate_scale)
        kept[0][:, cols] = inner
        kept[1][:, cols] = (up_scale * swish).astype(BF)
        slope = sigma + swish * (1.0 - sigma)
        kept[2][:, cols] = (up_scale * (gate_scale * ROOT) * up_val * slope).astype(BF)
        for source, target in zip(kept, far):
            go.start(source.at[:, cols], target.at[:, cols])
    go.wait()


def turn_part(far, info, source, target):
    group = target.shape[0]
    for j in range(far):

        @pl.when(info[PLACE_FAR] == j)
        def _(j=j):
            target[...] = source[:, j * group : (j + 1) * group].T


def unit_factors(line, ones, weights):
    rows, units = ones.shape[0], weights[0].shape[1]
    outs = [distant(rows, units, BF)] * 3
    scratch = [vmem(rows, D, BF), vmem(D, units, BF), vmem(D, units, BF)]
    scratch += [vmem(rows, units, BF)] * 3 + [sems(1 + 2 * units // 512), sems(3 * units // 512)]
    return line.call(
        unit_factors_kernel,
        outs,
        (ones, weights[0], weights[1], weights[3], weights[4]),
        flops=4 * rows * D * units,
        scratch=scratch,
        vmem=36,
        away=(0, 1, 2),
        sent=(0, 1, 2),
    )


def ffn_grad_kernel(far, info, *refs):
    parts, (ones_t_far, down_far), refs = refs[:far], refs[far : far + 2], refs[far + 2 :]
    factors_far, (send, keep), refs = refs[:3], refs[3:5], refs[5:]
    ones_t, d_ffns, d_ffns_t, down_w, *factors, in_sems = refs
    rows = parts[0].shape[0]
    tiles = unit_tiles(down_w.shape[0], 512)
    first = [
        (part, d_ffns.at[pl.ds((info[PLACE_FAR] ^ k) * rows, rows)]) for k, part in enumerate(parts)
    ]
    groups = [[*first, (ones_t_far, ones_t)]]
    for cols in tiles:
        group = [(down_far.at[cols], down_w.at[cols])]
        group += [(a.at[:, cols], b.at[:, cols]) for a, b in zip(factors_far, factors)]
        groups.append(group)
    arrive = Tiles(Copies(in_sems), groups, 3)
    arrive.wait(0)
    turn_part(far, info, d_ffns, d_ffns_t)
    size = ones_t.shape[0] // 4
    for i, cols in enumerate(tiles):
        arrive.wait(1 + i)
        d_inner = dot_nt(d_ffns[...], down_w[cols])
        inner, to_up, to_gate = (factor[:, cols] for factor in factors)
        d_up = (d_inner * to_up.astype(F32)).astype(BF)
        d_gate = (d_inner * to_gate.astype(F32)).astype(BF)
        for k, (left, right) in enumerate(((ones_t, d_up), (ones_t, d_gate), (d_ffns_t, inner))):
            grad = dot(left[...], right).astype(BF)
            blocks = [grad[j * size : (j + 1) * size] for j in range(4)]
            split_blocks(blocks, info[CORE] == 0, send.at[:, cols], keep.at[:, cols], k * 2 * size)


def ffn_grad(line, info, parts, down_weight, ones_t, factors):
    far, units = len(parts), down_weight.shape[0]
    rows, group = far * parts[0].shape[0], D // far
    outs = [distant(3 * group // 2, units, BF)] * 2
    scratch = [vmem(group, rows, BF), vmem(rows, D, BF), vmem(group, rows, BF), vmem(units, D, BF)]
    scratch += [vmem(rows, units, BF)] * 3 + [sems(far + 1 + 4 * units // 512)]
    return line.call(
        functools.partial(ffn_grad_kernel, far),
        outs,
        (info, *parts, ones_t, down_weight, *factors),
        flops=2 * rows * (D + 3 * group) * units,
        scratch=scratch,
        vmem=36,
        smem=1,
        loose=range(1, 1 + far),
        away=range(1 + far, 6 + far),
    )


def plain_unit_grads(low, d_ffn, weights):
    up_w, gate_w, down_w, up_s, gate_s = weights
    up_val = dot(low, up_w)
    inner, sigma, swish = swiglu_of(up_val, dot(low, gate_w), up_s, gate_s)
    d_up, _, d_gate = swiglu_back(dot_nt(d_ffn, down_w), up_val, sigma, swish, up_s, gate_s)
    return dot_tn(low, d_up), dot_tn(low, d_gate), dot_tn(d_ffn, inner)


def turn_kernel(source, result):
    result[...] = source[...].T


def turn(line, value):
    rows, cols = value.shape
    value = pltpu.with_memory_space_constraint(value, pltpu.HBM)
    return line.call(turn_kernel, (distant(cols, rows, value.dtype),), (value,))[0]


def give(split, info, products, outs, done=lambda rows: None):
    for i, (left, right) in enumerate(products):
        grad = dot(left, right[...]).astype(BF)
        if split:
            size = D // 16
            blocks = [grad[j * size : (j + 1) * size] for j in range(16)]
            split_blocks(blocks, info[CORE] == 0, outs[0], outs[1], i * 8 * size)
            done(slice(i * 8 * size, (i + 1) * 8 * size))
        else:
            outs[i][...] = grad


BACK_INPUTS = (
    ("d_mine", BF),
    ("dmix_two", F32),
    ("one", F32),
    ("sums", F32),
    ("x_cont", BF),
    ("wo", BF),
    ("kr", F32),
    ("qr", F32),
    ("v", BF),
    ("queries", BF),
    ("keys", BF),
    ("probs", BF),
    ("gains", F32),
    ("x_t", BF),
    ("att", BF),
)


def attention_back_kernel(split, info, _, d_other, rate_two, rate_one, scale_ref, *refs):
    count = len(BACK_INPUTS)
    made = 2 if split else 4
    far, outs = refs[:count], refs[count : count + made]
    dq_far, dk_far, dv_far, residual_far, gains_out, _ = refs[count + made : count + made + 6]
    held, refs = refs[count + made + 6 : -9], refs[-9:]
    d_att, dq_ref, dk_ref, dv_ref, residual_ref, send_ref, keep_ref, in_sems, out_sems = refs
    come, go = Copies(in_sems), Copies(out_sems)
    ref = {}
    arrived = {}
    pairs = {}
    for (name, _), source, target in zip(BACK_INPUTS, far, held):
        ref[name] = target
        pairs[name] = (source.at[P_SIZE:] if name == "x_cont" else source, target)

    def begin(*names):
        for name in names:
            arrived[name] = come.start(*pairs[name]).wait

    begin("d_mine", "dmix_two", "one", "sums", "x_cont", "wo")

    for name in ("d_mine", "dmix_two", "one", "sums", "x_cont"):
        arrived[name]()
    begin("v", "probs", "queries", "keys", "kr", "qr", "gains", "att", "x_t")
    old = ref["x_cont"][...].astype(F32)
    _, unit_in, inverse_in, inverse_out = mix(old, ref["sums"][...], rate_one[...])
    d_one = both(ref["d_mine"][...], d_other[...])
    d_one = d_one + (1.0 - rate_two[...]) * ref["dmix_two"][...]
    dmix = norm_back(d_one, ref["one"][...], inverse_out)
    residual_ref[...] = dmix * (1.0 - rate_one[...])
    go.start(residual_ref, residual_far)
    att_grad = jnp.sum(dmix * (unit_in - old), axis=0, keepdims=True)
    d_attn = norm_back(dmix * rate_one[...], unit_in, inverse_in).astype(BF)
    arrived["wo"]()
    d_att[...] = dot_nt(d_attn, ref["wo"][...]).astype(BF)

    gains = ref["gains"]
    width = scale_ref.shape[1]
    arrived["gains"]()
    for i in range(D // width):
        gains[2 + i : 3 + i] = att_grad[:, i * width : (i + 1) * width]

    def raw_back(grad, unit, inverse, scale):
        scaled = grad * scale
        back = inverse * (scaled - unit * head_sums(scaled * unit))
        return back.astype(BF), jnp.sum(grad * unit, axis=0, keepdims=True)

    for name in ("v", "probs", "queries", "keys", "kr", "qr"):
        arrived[name]()
    pairs = [slice(start, start + PAIR) for start in range(0, width, PAIR)]
    probs = [ref["probs"][2 * L * i : 2 * L * (i + 1)] for i in range(len(pairs))]
    grads = [halves(d_att[:, cols]) for cols in pairs]
    d_probs = [dot_nt(grad, ref["v"][:, cols]) for grad, cols in zip(grads, pairs)]
    d_scores = []
    for prob, d_prob in zip(probs, d_probs):
        prob = prob.astype(F32)
        delta = jnp.sum(d_prob * prob, axis=1, keepdims=True)
        d_scores.append((prob * (d_prob - delta)).astype(BF))
    for prob, grad, cols in zip(probs, grads, pairs):
        dv_ref[:, cols] = dot_tn(prob, grad).astype(BF)
    for d_score, cols in zip(d_scores, pairs):
        scale = scale_ref[:, cols]
        q_unit, q_inverse = unit_heads(ref["qr"][:, cols])
        k_unit, k_inverse = unit_heads(ref["kr"][:, cols])
        d_query = 8.0 * merge(dot(d_score, ref["keys"][:, cols]))
        d_keys = 8.0 * dot_tn(d_score, halves(ref["queries"][:, cols]))
        dq_ref[:, cols], by_query = raw_back(d_query, q_unit, q_inverse, scale)
        dk_ref[:, cols], by_key = raw_back(d_keys, k_unit, k_inverse, scale)
        gains[12:13, cols] = by_query + by_key
    for source, target in ((dq_ref, dq_far), (dk_ref, dk_far), (dv_ref, dv_far)):
        go.start(source, target)

    arrived["x_t"]()
    arrived["att"]()
    x_t = ref["x_t"]
    products = (
        (x_t[...], dv_ref),
        (x_t[...], dk_ref),
        (x_t[:, P_SIZE:], dq_ref),
        (d_attn.T, ref["att"]),
    )
    gains_out[...] = gains[...]
    if split:
        far, outs = outs, (send_ref, keep_ref)

        def done(rows):
            for source, target in zip(outs, far):
                go.start(source.at[rows], target.at[rows])

        for out in outs:
            out[2 * D :] = gains[...].astype(BF)
        done(slice(2 * D, 2 * D + GAINS))
        give(split, info, products, outs, done)
    else:
        give(split, info, products, outs)
    go.wait()


def attention_back(line, split, info, passed, d_other, rate_two, rate_one, scale, ins):
    width = scale.shape[1]
    rows = ins["v"].shape[0]
    outs = [distant(2 * D + GAINS, width, BF)] * 2 if split else [shape(D, width, BF)] * 4
    first = len(outs)
    outs += [distant(L, width, BF), distant(rows, width, BF), distant(rows, width, BF)]
    outs += [distant(L, D, F32), shape(GAINS, width, F32), shape(*passed.shape, BF)]
    scratch = []
    for name, kind in BACK_INPUTS:
        scratch.append(vmem(L if name == "x_cont" else ins[name].shape[0], ins[name].shape[1], kind))
    scratch += [vmem(L, width, BF), vmem(L, width, BF), vmem(rows, width, BF), vmem(rows, width, BF)]
    scratch += [vmem(L, D, F32)] + [vmem(2 * D + GAINS if split else GAINS, width, BF)] * 2
    scratch += [sems(len(BACK_INPUTS)), sems(14)]
    flops = 20 * L * rows * width + 4 * (rows + L) * D * width + 4 * L * D * width
    return line.call(
        functools.partial(attention_back_kernel, split),
        outs,
        (info, passed, d_other, rate_two, rate_one, scale, *(ins[name] for name, _ in BACK_INPUTS)),
        flops=flops,
        scratch=scratch,
        vmem=50,
        smem=1,
        away=range(6, 6 + len(BACK_INPUTS)),
        loose=(1,),
        sent=(*range(2 if split else 0), first, first + 1, first + 2, first + 3, first + 5),
        aliases={1: first + 5},
    )


def fold_core_kernel(info, keep, got, *outs):
    size = D // 16
    total = (keep[...].astype(F32) + got[...].astype(F32)).astype(BF)
    for m in range(4):
        start = m * 8 * size
        blocks = [total[start + j * size : start + (j + 1) * size] for j in range(8)]
        send, kept = outs[:2] if m < 2 else outs[2:]
        split_blocks(blocks, info[PLACE_X] == 0, send, kept, m % 2 * 4 * size)
    for ref in outs[:2]:
        ref[8 * size :] = total[32 * size :]


def fold_kernel(matrices, count, bit, info, keep, got, send, kept):
    size = D // 16
    low = info[PLACE_FAR] // bit % 2 == 0
    total = (keep[...].astype(F32) + got[...].astype(F32)).astype(BF)
    half = count // 2
    for m in range(matrices):
        first = total[m * count * size : (m * count + half) * size]
        second = total[(m * count + half) * size : (m + 1) * count * size]
        rows = slice(m * half * size, (m + 1) * half * size)
        send[rows] = jnp.where(low, second, first)
        kept[rows] = jnp.where(low, first, second)
    if keep.shape[0] > matrices * count * size:
        for ref in (send, kept):
            ref[matrices * half * size :] = total[matrices * count * size :]


def finish_first_kernel(tokens, keep, got, *outs):
    value, key, mlp, att, up, gate, head, loss, factor_ref = outs
    size = value.shape[0]
    total = keep[...].astype(F32) + got[...].astype(F32)
    gains = total[2 * size :]
    factor = tokens / (gains[13:14, 2:3] + gains[13:14, 3:4])
    factor_ref[...] = factor
    loss[...] = factor * (gains[13:14, 0:1] + gains[13:14, 1:2])
    gains = gains * factor
    width = gains.shape[1]
    place = 0
    for ref in (mlp, att, up, gate, head):
        for start in range(0, ref.shape[1], width):
            ref[:, start : start + width] = gains[place : place + 1]
            place += 1
    value[...] = total[:size] * factor
    key[...] = total[size : 2 * size] * factor


def fold_units_kernel(info, keep, got, send_ref, keep_ref):
    size = keep.shape[0] // 6
    total = (keep[...].astype(F32) + got[...].astype(F32)).astype(BF)
    blocks = [total[j * size : (j + 1) * size] for j in range(6)]
    split_blocks(blocks, info[PLACE_X] == 0, send_ref, keep_ref, 0)


def finish_rest_kernel(factor, keep, got, u_keep, u_got, query, out, *results):
    size = query.shape[0]
    total = (keep[...].astype(F32) + got[...].astype(F32)) * factor[...]
    query[...] = total[:size]
    out[...] = total[size:]
    total = (u_keep[...].astype(F32) + u_got[...].astype(F32)) * factor[...]
    size = total.shape[0] // 3
    for m, result in enumerate(results):
        result[...] = total[m * size : (m + 1) * size]


def rows_kernel(info, dq, dk, dv, wq_far, wk_far, wv_far, send_ref, keep_ref, wq, wk, wv, in_sems):
    come = Copies(in_sems)
    for source, target in ((wk_far, wk), (wv_far, wv), (wq_far, wq)):
        come.start(source, target)
    half = send_ref.shape[0]
    come.copies[0].wait()
    prompt = dot_nt(dk[...], wk[...])
    come.copies[1].wait()
    prompt = prompt + dot_nt(dv[...], wv[...])
    come.copies[2].wait()
    top = prompt[:half].astype(BF)
    low = jnp.concatenate(
        [prompt[half:P_SIZE], prompt[P_SIZE:] + dot_nt(dq[...], wq[...])], 0
    ).astype(BF)
    first = info[SIDE] == 0
    send_ref[...] = jnp.where(first, low, top)
    keep_ref[...] = jnp.where(first, top, low)


def share_kernel(info, keep, got, residual, kept_ref, sent_ref):
    half = keep.shape[0]
    total = keep[...].astype(F32) + got[...].astype(F32)
    row = lax.broadcasted_iota(jnp.int32, (half, 1), 0) + info[SIDE] * half
    away = (row < P_SIZE) & (info[OWN] == 0)
    sent_ref[...] = jnp.where(away, total, 0.0).astype(BF)
    kept_ref[...] = jnp.where(away, 0.0, total)
    kept_ref[half - L :] += jnp.where(info[SIDE] == 1, residual[...], 0.0)


def last_share_kernel(kept, got, factor, result):
    result[...] = (kept[...] + got[...].astype(F32)) * factor[...]


def last_mix_kernel(one_far, rate, out_far, *refs):
    *parts, result_far, one, result, in_sems, out_sems = refs
    come, go = Copies(in_sems), Copies(out_sems)
    count = len(parts) // 2
    size = P_SIZE // count
    slices = [slice(i * size, (i + 1) * size) for i in range(count)]
    for rows in slices:
        come.start(one_far.at[rows], one.at[rows])
    come.start(out_far, result.at[P_SIZE:])
    for i, rows in enumerate(slices):
        come.copies[i].wait()
        result[rows] = mix(one[rows], both(parts[i][...], parts[count + i][...]), rate[...])[0]
        go.start(result.at[rows], result_far.at[rows])
    come.copies[-1].wait()
    go.start(result.at[P_SIZE:], result_far.at[P_SIZE:])
    go.wait()


def local(
    hidden_in,
    query_weight,
    key_weight,
    value_weight,
    out_weight,
    up_weight,
    gate_weight,
    down_weight,
    head_scale,
    attention_rate,
    up_scale,
    gate_scale,
    swiglu_rate,
    teacher,
    valid_mask,
    group_ids,
):
    count_dp = lax.axis_size("dp")
    far = count_dp // 4
    split = far == 4
    me = lax.axis_index("dp")
    rows = hidden_in.shape[0]
    width = query_weight.shape[1]
    units = up_weight.shape[1]
    scale = head_scale.reshape(1, width)
    rate_one = attention_rate.reshape(1, D)
    rate_two = swiglu_rate.reshape(1, D)
    own = (group_ids[0] == me).astype(jnp.int32)
    info = jnp.stack([own, me % 2, me // 2 % 2, me // 4, lax.axis_index("tensor")])
    info = info.astype(jnp.int32)
    qkvo = (query_weight, key_weight, value_weight, out_weight)
    ffn_weights = (
        up_weight,
        gate_weight,
        down_weight,
        up_scale.reshape(1, units),
        gate_scale.reshape(1, units),
    )

    line = Line()

    other_x = swap(hidden_in, "dp", 1)
    a_mine, att, x_seen, values, query_raw, key_raw, queries, keys, probs, *qkvo_near = cont_attention(
        line, info, hidden_in, other_x, qkvo, scale
    )
    a_other = swap(a_mine, "tensor", 1)
    p_mine, *ffn_near = prompt_attention(line, hidden_in, qkvo_near, scale, ffn_weights[:3])
    ffn_near = (*ffn_near, *ffn_weights[3:])
    m_mine, one_low, up_val, gate_val, one_near, attn_sums, one = ffn(
        line, a_mine, a_other, hidden_in, rate_one, ffn_near
    )
    m_other = swap(m_mine, "tensor", 1)
    x_seen_t = turn(line, x_seen)
    d_mine, d_ffn, out, dmix_two, gains = ffn_back(
        line,
        m_mine,
        m_other,
        one_near,
        rate_two,
        teacher,
        valid_mask.reshape(1, L),
        up_val,
        gate_val,
        ffn_near,
        width,
    )
    total_cont = count_dp * valid_mask.shape[0]
    mine = D // count_dp
    usual = group_ids[0] >= 0
    half_rows = shape(rows // 2, D, BF)

    d_other = swap(d_mine, "tensor", 1)
    if split:
        ones = [one_low]
        bit = 4
        while bit < count_dp:
            ones += [swap(part, "dp", bit) for part in ones]
            bit *= 2
        ones, ones_t = collect(line, info, ones)
    *first, d_query, d_key, d_value, residual, gains, p_mine = attention_back(
        line,
        split,
        info,
        p_mine,
        d_other,
        rate_two,
        rate_one,
        scale,
        {
            "d_mine": d_mine,
            "dmix_two": dmix_two,
            "one": one,
            "sums": attn_sums,
            "x_cont": hidden_in,
            "wo": out_weight,
            "kr": key_raw,
            "qr": query_raw,
            "v": values,
            "queries": queries,
            "keys": keys,
            "probs": probs,
            "gains": gains,
            "x_t": x_seen_t,
            "att": att,
        },
    )

    p_other = swap(p_mine, "tensor", 1)

    def fold(line, send, keep, count, bit, before=()):
        more = keep.shape[0] - 2 * count * mine

        def kernel(info, keep, send, *refs):
            fold_kernel(2, count, bit, info, keep, send, *refs[len(before) :])

        return line.call(
            kernel,
            [shape(count * mine + more, width, BF)] * 2,
            (info, keep, send, *before),
            smem=1,
            loose=range(3, 3 + len(before)),
        )

    def rows_step(info, before, first, d_query, d_key, d_value, ones):
        inner = Line(before)
        if split:
            got = swap(first[0], "dp", 1)
        rows_pair = inner.call(
            rows_kernel,
            (half_rows, half_rows),
            (info, d_query, d_key, d_value, query_weight, key_weight, value_weight),
            flops=6 * rows * D * width,
            scratch=[vmem(D, width, BF)] * 3 + [sems(3)],
            vmem=22,
            smem=1,
            away=(4, 5, 6),
        )
        if not split:
            return first, rows_pair, (), inner.last
        send_a, keep_a, send_b, keep_b = inner.call(
            fold_core_kernel,
            [shape(D // 2 + GAINS, width, BF)] * 2 + [shape(D // 2, width, BF)] * 2,
            (info, first[1], got),
            smem=1,
        )
        got_a = swap(send_a, "dp", 2)
        factors = unit_factors(inner, ones, ffn_weights)
        send_a, keep_a = fold(inner, got_a, keep_a, 4, 2)
        return (send_a, keep_a, send_b, keep_b), rows_pair, factors, inner.last

    if not split:
        ones = one_low
    first, (rows_sent, kept), factors, line.last = section(
        usual, rows_step, info, line.last, first, d_query, d_key, d_value, ones
    )
    share = swap(rows_sent, "tensor", 1)
    if split:
        send_a, keep_a, send_b, keep_b = first
        got_b = swap(send_b, "dp", 2)
        d_ffns = [d_ffn] + [swap(d_ffn, "dp", 4 * k) for k in range(1, far)]
        u_send, u_keep = ffn_grad(line, info, d_ffns, down_weight, ones_t, factors)
    else:
        u_send = u_keep = send_a = keep_a = None

    def middle_step(info, before, p_mine, p_other, share_keep, share, residual, u_send, u_keep, send_a, keep_a):
        inner = Line(before)
        if split:
            u_got, got_a = swap(u_send, "dp", 1), swap(send_a, "dp", 8)
        kept, sent = inner.call(
            share_kernel,
            (distant(rows // 2, D, F32), half_rows),
            (info, share_keep, share, residual),
            smem=1,
        )
        share = swap(sent, "dp", 1)
        prompt = prompt_ffn(inner, p_mine, p_other, hidden_in, rate_one, ffn_weights)
        if split:
            u_send, u_keep = inner.call(
                fold_units_kernel,
                (shape(3 * mine, units, BF),) * 2,
                (info, u_keep, u_got),
                smem=1,
            )
            send_a, keep_a = fold(inner, got_a, keep_a, 2, 1)
        return kept, share, prompt, u_send, u_keep, send_a, keep_a, inner.last

    kept, share, (one_p, *mp_mine), u_send, u_keep, send_a, keep_a, line.last = section(
        usual,
        middle_step,
        info,
        line.last,
        p_mine,
        p_other,
        kept,
        share,
        residual,
        u_send,
        u_keep,
        send_a,
        keep_a,
    )
    mp_other = [swap(part, "tensor", 1) for part in mp_mine]
    if split:
        u_got = swap(u_send, "dp", 2)
        got_a = swap(send_a, "dp", 4)
        send_b, keep_b = fold(line, got_b, keep_b, 4, 2)
        got_b = swap(send_b, "dp", 8)
    if split:
        value_grad, key_grad, mlp, att_rate, up_g, gate_g, head, loss, factor = line.call(
            functools.partial(finish_first_kernel, total_cont),
            [distant(mine, width, F32)] * 2
            + [shape(1, n, F32) for n in (D, D, units, units, width, 1, 1)],
            (keep_a, got_a),
        )
    else:
        total = sum_all(gains)
        factor = total_cont / (total[13:14, 2:3] + total[13:14, 3:4])
        loss = factor * (total[13:14, 0:1] + total[13:14, 1:2])
        flat = (total * factor).reshape(-1)
        mlp, att_rate, up_g, gate_g, head = (
            flat[start : start + size]
            for start, size in (
                (0, D),
                (D, D),
                (2 * D, units),
                (2 * D + units, units),
                (2 * D + 2 * units, width),
            )
        )
        flat = [head, att_rate, up_g, gate_g, mlp]

        def scattered(grad):
            grad = grad.astype(F32)
            return factor * lax.psum_scatter(grad, "dp", scatter_dimension=0, tiled=True)

        value_grad, key_grad, query_grad, out_grad = (scattered(grad) for grad in first)
        up_grad, gate_grad, down_grad = (
            scattered(grad) for grad in plain_unit_grads(one_low, d_ffn, ffn_weights)
        )
    grad_hidden = line.call(
        last_share_kernel, (distant(rows // 2, D, F32),), (kept, share, factor), held=(0,)
    )[0]
    if split:
        flat = [value.reshape(-1) for value in (head, att_rate, up_g, gate_g, mlp)]
        send_b, keep_b = fold(line, got_b, keep_b, 2, 1, flat)
        got_b = swap(send_b, "dp", 4)
    hidden_out = line.call(
        last_mix_kernel,
        (distant(rows, D, F32),),
        (one_p, rate_two, out, *mp_mine, *mp_other),
        scratch=[vmem(P_SIZE, D, F32), vmem(P_SIZE + L, D, F32), sems(3), sems(3)],
        away=(0, 2),
        sent=(0,),
    )[0]
    if split:
        query_grad, out_grad, up_grad, gate_grad, down_grad = line.call(
            finish_rest_kernel,
            [distant(mine, width, F32)] * 2 + [distant(mine, units, F32)] * 3,
            (factor, keep_b, got_b, u_keep, u_got),
        )
    return (
        hidden_out,
        loss[0, 0],
        grad_hidden,
        query_grad,
        key_grad,
        value_grad,
        out_grad.T,
        up_grad,
        gate_grad,
        down_grad.T,
        *flat,
    )


def solution(mesh):
    placed = (
        P("dp", None),
        P(None, "tensor"),
        P(None, "tensor"),
        P(None, "tensor"),
        P("tensor", None),
        P(None, "tensor"),
        P(None, "tensor"),
        P("tensor", None),
        P("tensor"),
        P(),
        P("tensor"),
        P("tensor"),
        P(),
        P("dp", None),
        P("dp"),
        P("dp"),
    )
    return jax.shard_map(
        local,
        mesh=mesh,
        in_specs=placed,
        out_specs=(
            P("dp", None),
            P(),
            P(("dp", "tensor"), None),
            P("dp", "tensor"),
            P("dp", "tensor"),
            P("dp", "tensor"),
            P("tensor", "dp"),
            P("dp", "tensor"),
            P("dp", "tensor"),
            P("tensor", "dp"),
            P("tensor"),
            P(),
            P("tensor"),
            P("tensor"),
            P(),
        ),
        check_vma=False,
    )
```

```python
import functools
import math

import jax
import jax.numpy as jnp
from jax import lax
from jax.experimental import pallas as pl
from jax.experimental.pallas import tpu as pltpu
from jax.sharding import PartitionSpec as P

D = 1280
HD = 64
P_SIZE = 384
L = 128
PAIR = 2 * HD
EPS = 1e-06
ROOT = math.sqrt(D)
BF = jnp.bfloat16
F32 = jnp.float32
MIB = 2**20
GAINS = 16
OWN, CORE, PLACE_X, PLACE_FAR, SIDE = range(5)


def swap(value, axis, bit):
    count = lax.axis_size(axis)
    return lax.ppermute(value, axis, [(i, i ^ bit) for i in range(count)])


def sum_all(value):
    bit = 1
    while bit < lax.axis_size("dp"):
        value = value + swap(value, "dp", bit)
        bit *= 2
    return value


def dot(left, right):
    return jnp.dot(left, right, preferred_element_type=F32)


def dot_nt(left, right):
    return lax.dot_general(left, right, (((1,), (1,)), ((), ())), preferred_element_type=F32)


def dot_tn(left, right):
    return lax.dot_general(left, right, (((0,), (0,)), ((), ())), preferred_element_type=F32)


def inverse_norm(values):
    return lax.rsqrt(jnp.sum(values * values, axis=-1, keepdims=True) + EPS)


def norm_back(grad, unit, inverse):
    return inverse * (grad - unit * jnp.sum(grad * unit, axis=-1, keepdims=True))


def mix(old, sums, rate):
    inverse_in = inverse_norm(sums)
    unit_in = sums * inverse_in
    mixed = old + rate * (unit_in - old)
    inverse_out = inverse_norm(mixed)
    return mixed * inverse_out, unit_in, inverse_in, inverse_out


def both(mine, other):
    return mine.astype(F32) + other.astype(F32)


class Line:
    def __init__(self, last=None):
        self.last = last

    def call(
        self, kernel, outs, ins, *, flops=0, scratch=(), vmem=12, smem=0, away=(), held=(), loose=(), sent=(), aliases=()
    ):
        moved = sum(math.prod(v.shape) * v.dtype.itemsize for v in (*ins, *outs))
        count, results = len(ins), len(outs)
        places = [pltpu.SMEM] * smem + [pltpu.VMEM] * (count - smem)
        ins = list(ins)
        for i in (*loose, *away):
            places[i] = pl.ANY
        for i in (*held, *away):
            ins[i] = pltpu.with_memory_space_constraint(ins[i], pltpu.HBM)
        out_places = [pl.ANY if i in sent else pltpu.VMEM for i in range(results)] + [pl.ANY]
        if self.last is not None:
            places.append(pl.ANY)
            ins.append(pltpu.with_memory_space_constraint(self.last, pltpu.HBM))
        first = len(ins)

        def body(*refs):
            kernel(*refs[:count], *refs[first : first + results], *refs[first + results + 1 :])

        *done, self.last = pl.pallas_call(
            body,
            out_shape=(*outs, distant(8, 128, F32)),
            in_specs=[pl.BlockSpec(memory_space=place) for place in places],
            out_specs=tuple(pl.BlockSpec(memory_space=place) for place in out_places),
            scratch_shapes=list(scratch),
            input_output_aliases=dict(aliases),
            compiler_params=pltpu.CompilerParams(vmem_limit_bytes=vmem * MIB),
            cost_estimate=pl.CostEstimate(flops=flops, bytes_accessed=moved, transcendentals=0),
        )(*ins)
        return done


def section(usual, work, *ins):
    shapes = jax.eval_shape(work, *ins)
    return lax.cond(
        usual, work, lambda *_: jax.tree.map(lambda v: jnp.zeros(v.shape, v.dtype), shapes), *ins
    )


class Copies:
    def __init__(self, sems):
        self.sems, self.copies = sems, []

    def start(self, source, target):
        copy = pltpu.make_async_copy(source, target, self.sems.at[len(self.copies)])
        copy.start()
        self.copies.append(copy)
        return copy

    def wait(self):
        for copy in self.copies:
            copy.wait()


class Tiles:
    def __init__(self, come, groups, ahead=2):
        self.come, self.groups, self.ahead, self.going = come, groups, ahead, []
        for _ in range(ahead):
            self.more()

    def more(self):
        if len(self.going) < len(self.groups):
            group = self.groups[len(self.going)]
            self.going.append([self.come.start(source, target) for source, target in group])

    def wait(self, i):
        for copy in self.going[i]:
            copy.wait()
        self.more()


def distant(rows, cols, kind):
    return pltpu.HBM((rows, cols), kind)


def vmem(rows, cols, kind):
    return pltpu.VMEM((rows, cols), kind)


def sems(count):
    return pltpu.SemaphoreType.DMA((count,))


def near(rows, cols, kind):
    return pltpu.VMEM((rows, cols), kind)


def fetch(pairs, sems):
    copies = [pltpu.make_async_copy(a, b, sems.at[i]) for i, (a, b) in enumerate(pairs)]
    for copy in copies:
        copy.start()
    return copies


def shape(rows, cols, kind):
    return jax.ShapeDtypeStruct((rows, cols), kind)


def head_sums(values):
    rows = lax.broadcasted_iota(jnp.int32, (PAIR, PAIR), 0) // HD
    cols = lax.broadcasted_iota(jnp.int32, (PAIR, PAIR), 1) // HD
    ones = jnp.where(rows == cols, 1.0, 0.0).astype(BF)
    high = values.astype(BF)
    low = (values - high.astype(F32)).astype(BF)
    return dot(high, ones) + dot(low, ones)


def unit_heads(raw):
    inverse = lax.rsqrt(head_sums(raw * raw) + EPS)
    return raw * inverse, inverse


def halves(value):
    first = lax.broadcasted_iota(jnp.int32, value.shape, 1) < HD
    zero = jnp.zeros_like(value)
    return jnp.concatenate([jnp.where(first, value, zero), jnp.where(first, zero, value)], 0)


def merge(value):
    rows = value.shape[0] // 2
    first = lax.broadcasted_iota(jnp.int32, (rows, PAIR), 1) < HD
    return jnp.where(first, value[:rows], value[rows:])


def weights_of(queries, keys, offset):
    scores = 8.0 * dot_nt(queries, keys)
    rows = queries.shape[0] // 2
    row = lax.broadcasted_iota(jnp.int32, scores.shape, 0)
    row = jnp.where(row >= rows, row - rows, row)
    col = lax.broadcasted_iota(jnp.int32, scores.shape, 1)
    expo = jnp.where(col <= row + offset, jnp.exp(scores), 0.0)
    return expo * (1.0 / jnp.sum(expo, axis=1, keepdims=True))


def attention_body(x, offset, weights, scale_ref, refs, arrived, ready, keep=lambda *_: None):
    wq_ref, wk_ref, wv_ref, wo_ref = weights
    att_ref, part_ref, v_ref, qr_ref, kr_ref = refs
    arrived(0)
    kr_ref[...] = dot(x, wk_ref[...])
    ready(0)
    arrived(1)
    v_ref[...] = dot(x, wv_ref[...]).astype(BF)
    ready(1)
    arrived(2)
    qr_ref[...] = dot(x[offset:], wq_ref[...])
    ready(2)
    for start in range(0, wq_ref.shape[1], PAIR):
        cols = slice(start, start + PAIR)
        scale = scale_ref[:, cols]
        keys = (unit_heads(kr_ref[:, cols])[0] * scale).astype(BF)
        queries = (unit_heads(qr_ref[:, cols])[0] * scale).astype(BF)
        probs = weights_of(halves(queries), keys, offset).astype(BF)
        keep(start, cols, queries, keys, probs)
        att_ref[:, cols] = merge(dot(probs, v_ref[:, cols])).astype(BF)
    ready(3)
    arrived(3)
    part_ref[...] = dot(att_ref[...], wo_ref[...]).astype(BF)


def cont_kernel(info, hidden, other, wq, wk, wv, wo, scale, *refs):
    part, att_far, x_far, v_far, qr_far, kr_far, q_far, k_far, p_far = refs[:9]
    wq_near, wk_near, wv_near, wo_near = refs[9:13]
    own_x, other_x, x_ref, att, v_ref, qr, kr, q_ref, k_ref, p_ref, in_sems, out_sems = refs[13:]
    come, go = Copies(in_sems), Copies(out_sems)
    arrive = Tiles(
        come,
        (
            ((hidden, own_x), (other.at[:P_SIZE], other_x)),
            ((wk, wk_near),),
            ((wv, wv_near),),
            ((wq, wq_near),),
            ((wo, wo_near),),
        ),
    )
    arrive.wait(0)
    x_ref[:P_SIZE] = jnp.where(info[OWN] == 1, own_x[:P_SIZE], other_x[...])
    x_ref[P_SIZE:] = own_x[P_SIZE:]
    go.start(x_ref, x_far)
    results = ((kr, kr_far), (v_ref, v_far), (qr, qr_far), (att, att_far))

    def keep(start, cols, queries, keys, probs):
        rows = slice(2 * L * (start // PAIR), 2 * L * (start // PAIR + 1))
        q_ref[:, cols] = queries
        k_ref[:, cols] = keys
        p_ref[rows] = probs
        go.start(k_ref.at[:, cols], k_far.at[:, cols])
        go.start(p_ref.at[rows], p_far.at[rows])

    attention_body(
        x_ref[...],
        P_SIZE,
        (wq_near, wk_near, wv_near, wo_near),
        scale,
        (att, part, v_ref, qr, kr),
        lambda i: arrive.wait(1 + i),
        lambda i: go.start(*results[i]),
        keep,
    )
    go.start(q_ref, q_far)
    go.wait()


def cont_attention(line, info, hidden, other, weights, scale):
    rows, width = hidden.shape[0], scale.shape[1]
    outs = [
        shape(L, D, BF),
        distant(L, width, BF),
        distant(rows, D, BF),
        distant(rows, width, BF),
        distant(L, width, F32),
        distant(rows, width, F32),
        distant(L, width, BF),
        distant(rows, width, BF),
        distant(width // HD * L, rows, BF),
    ] + [near(*weight.shape, BF) for weight in weights]
    scratch = [
        vmem(rows, D, BF),
        vmem(P_SIZE, D, BF),
        vmem(rows, D, BF),
        vmem(L, width, BF),
        vmem(rows, width, BF),
        vmem(L, width, F32),
        vmem(rows, width, F32),
        vmem(L, width, BF),
        vmem(rows, width, BF),
        vmem(width // HD * L, rows, BF),
        sems(6),
        sems(6 + 2 * (width // PAIR)),
    ]
    flops = 4 * rows * D * width + 4 * L * D * width + 8 * L * rows * width
    return line.call(
        cont_kernel,
        outs,
        (info, hidden, other, *weights, scale),
        flops=flops,
        scratch=scratch,
        vmem=28,
        smem=1,
        away=(1, 3, 4, 5, 6),
        loose=(2,),
        sent=range(1, 9),
    )


def prompt_kernel(hidden, wq, wk, wv, wo, scale, up, gate, down, *refs):
    part, up_near, gate_near, down_near, x_ref, att, v_ref, qr, kr, in_sems = refs
    come = Copies(in_sems)
    come.start(hidden.at[:P_SIZE], x_ref)
    for source, target in ((up, up_near), (gate, gate_near), (down, down_near)):
        come.start(source, target)
    come.copies[0].wait()
    attention_body(
        x_ref[...],
        0,
        (wq, wk, wv, wo),
        scale,
        (att, part, v_ref, qr, kr),
        lambda i: None,
        lambda i: None,
    )
    for copy in come.copies[1:]:
        copy.wait()


def prompt_attention(line, hidden, weights, scale, later):
    width = scale.shape[1]
    scratch = [
        vmem(P_SIZE, D, BF),
        vmem(P_SIZE, width, BF),
        vmem(P_SIZE, width, BF),
        vmem(P_SIZE, width, F32),
        vmem(P_SIZE, width, F32),
        sems(4),
    ]
    outs = [shape(P_SIZE, D, BF)] + [near(*weight.shape, BF) for weight in later]
    flops = 8 * P_SIZE * D * width + 8 * P_SIZE * P_SIZE * width
    ins = (hidden, *weights, scale, *later)
    return line.call(
        prompt_kernel, outs, ins, flops=flops, scratch=scratch, vmem=13, away=(0, 6, 7, 8)
    )


def swiglu_of(up_val, gate_val, up_scale, gate_scale):
    half = (gate_scale * (0.5 * ROOT)) * gate_val
    more = jnp.tanh(half) + 1.0
    swish = half * more
    return (up_scale * up_val * swish).astype(BF), 0.5 * more, swish


def swiglu_back(d_inner, up_val, sigma, swish, up_scale, gate_scale):
    scaled = d_inner * up_scale
    d_arg = scaled * up_val * (sigma + swish * (1.0 - sigma))
    return (scaled * swish).astype(BF), d_arg, (d_arg * (gate_scale * ROOT)).astype(BF)


def unit_tiles(units, tile):
    return [slice(start, start + tile) for start in range(0, units, tile)]


def ffn_kernel(mine, other, hidden, rate, up_w, gate_w, down_w, up_s, gate_s, *refs):
    part, low_ref, up_ref, gate_ref, one_ref, sums_far, one_far = refs[:7]
    sums_ref, inner_ref, x_ref, in_sems, out_sems = refs[7:]
    come, go = Copies(in_sems), Copies(out_sems)
    come.start(hidden.at[P_SIZE:], x_ref)
    sums = both(mine[...], other[...])
    sums_ref[...] = sums
    go.start(sums_ref, sums_far)
    come.wait()
    one = mix(x_ref[...].astype(F32), sums, rate[...])[0]
    one_ref[...] = one
    go.start(one_ref, one_far)
    low = one.astype(BF)
    low_ref[...] = low
    for cols in unit_tiles(up_w.shape[1], 512):
        up_val, gate_val = dot(low, up_w[:, cols]), dot(low, gate_w[:, cols])
        up_ref[:, cols] = up_val
        gate_ref[:, cols] = gate_val
        inner_ref[:, cols] = swiglu_of(up_val, gate_val, up_s[:, cols], gate_s[:, cols])[0]
    part[...] = dot(inner_ref[...], down_w[...]).astype(BF)
    go.wait()


def ffn(line, mine, other, hidden, rate, weights):
    units = weights[0].shape[1]
    outs = [
        shape(L, D, BF),
        shape(L, D, BF),
        near(L, units, F32),
        near(L, units, F32),
        near(L, D, F32),
        distant(L, D, F32),
        distant(L, D, F32),
    ]
    scratch = [vmem(L, D, F32), vmem(L, units, BF), vmem(L, D, BF), sems(1), sems(2)]
    ins = (mine, other, hidden, rate, *weights)
    flops = 6 * L * D * units
    return line.call(
        ffn_kernel, outs, ins, flops=flops, scratch=scratch, away=(2,), sent=(5, 6)
    )


def prompt_ffn_kernel(mine_far, other_far, hidden, rate, up_far, gate_far, down_far, up_s, gate_s, *refs):
    one_ref, *parts, inner_ref, x_ref, mine, other, up_w, gate_w, down_w, in_sems = refs
    tiles = unit_tiles(up_w.shape[1], 512)
    groups = [((hidden.at[:P_SIZE], x_ref), (mine_far, mine), (other_far, other))]
    for cols in tiles:
        groups.append(
            (
                (up_far.at[:, cols], up_w.at[:, cols]),
                (gate_far.at[:, cols], gate_w.at[:, cols]),
                (down_far.at[cols], down_w.at[cols]),
            )
        )
    arrive = Tiles(Copies(in_sems), groups, 3)
    arrive.wait(0)
    one = mix(x_ref[...].astype(F32), both(mine[...], other[...]), rate[...])[0]
    one_ref[...] = one
    low = one.astype(BF)
    for i, cols in enumerate(tiles):
        arrive.wait(1 + i)
        up_val, gate_val = dot(low, up_w[:, cols]), dot(low, gate_w[:, cols])
        inner_ref[:, cols] = swiglu_of(up_val, gate_val, up_s[:, cols], gate_s[:, cols])[0]
    total = dot(inner_ref[...], down_w[...]).astype(BF)
    for i, part in enumerate(parts):
        part[...] = total[i * part.shape[0] : (i + 1) * part.shape[0]]


def weight_scratch(weights):
    return [vmem(*weight.shape, BF) for weight in weights[:3]]


def prompt_ffn(line, mine, other, hidden, rate, weights):
    units = weights[0].shape[1]
    scratch = [
        vmem(P_SIZE, units, BF),
        *[vmem(P_SIZE, D, BF)] * 3,
        *weight_scratch(weights),
        sems(3 + 3 * units // 512),
    ]
    ins = (mine, other, hidden, rate, *weights)
    outs = (distant(P_SIZE, D, F32), shape(P_SIZE // 2, D, BF), shape(P_SIZE // 2, D, BF))
    flops = 6 * P_SIZE * D * units
    return line.call(
        prompt_ffn_kernel,
        outs,
        ins,
        flops=flops,
        scratch=scratch,
        vmem=42,
        away=(0, 1, 2, 4, 5, 6),
    )


def ffn_back_kernel(mine, other, one, rate, teacher, valid, up_v, gate_v, *refs):
    up_w, gate_w, down_w, up_s, gate_s = refs[:5]
    part, low_ref, out_ref, dmix_ref, gains, d_up_ref, d_gate_ref = refs[5:]
    tiles = unit_tiles(up_w.shape[1], 512)
    row = lax.broadcasted_iota(jnp.int32, (L, L), 0)
    col = lax.broadcasted_iota(jnp.int32, (L, L), 1)
    counted = jnp.sum(jnp.where(row == col, valid[...].astype(F32), 0.0), axis=1, keepdims=True)
    old = one[...]
    out, unit, inverse_in, inverse_out = mix(old, both(mine[...], other[...]), rate[...])
    out_ref[...] = out
    diff = out - teacher[...].astype(F32)
    weighted = counted * diff
    by_row = jnp.sum(weighted * diff, axis=1, keepdims=True)
    dmix = norm_back(2.0 * weighted, out, inverse_out)
    dmix_ref[...] = dmix
    low = norm_back(dmix * rate[...], unit, inverse_in).astype(BF)
    low_ref[...] = low

    width = gains.shape[1]
    gains[...] = jnp.zeros_like(gains)

    def put(place, value):
        for start in range(0, value.shape[1], width):
            gains[place : place + 1] = value[:, start : start + width]
            place += 1

    put(0, jnp.sum(dmix * (unit - old), axis=0, keepdims=True))
    lane = lax.broadcasted_iota(jnp.int32, (1, width), 1)
    last = jnp.zeros((1, width), F32)
    for i, value in enumerate((by_row, counted)):
        value = jnp.sum(value, axis=0, keepdims=True)
        high = value.astype(BF).astype(F32)
        last = jnp.where(lane == 2 * i, high, last)
        last = jnp.where(lane == 2 * i + 1, value - high, last)
    put(13, last)
    for cols in tiles:
        d_inner = dot_nt(low, down_w[cols])
        up_val, gate_val = up_v[:, cols], gate_v[:, cols]
        _, sigma, swish = swiglu_of(up_val, gate_val, up_s[:, cols], gate_s[:, cols])
        d_up, d_arg, d_gate = swiglu_back(
            d_inner, up_val, sigma, swish, up_s[:, cols], gate_s[:, cols]
        )
        d_up_ref[:, cols] = d_up
        d_gate_ref[:, cols] = d_gate
        for place, value in ((4, d_inner * up_val * swish), (8, d_arg * ROOT * gate_val)):
            total = jnp.sum(value, axis=0, keepdims=True)
            done = cols.start
            while done < cols.stop:
                step = min(cols.stop, (done // width + 1) * width) - done
                left, at = done - cols.start, done % width
                gains[place + done // width : place + done // width + 1, at : at + step] = total[
                    :, left : left + step
                ]
                done += step
    total = dot_nt(d_up_ref[...], up_w[...]) + dot_nt(d_gate_ref[...], gate_w[...])
    part[...] = total.astype(BF)


def ffn_back(line, mine, other, one, rate, teacher, valid, up_val, gate_val, weights, width):
    units = weights[0].shape[1]
    outs = (
        distant(L, D, BF),
        distant(L, D, BF),
        distant(L, D, F32),
        distant(L, D, F32),
        distant(GAINS, width, F32),
    )
    scratch = [vmem(L, units, BF), vmem(L, units, BF)]
    ins = (mine, other, one, rate, teacher, valid, up_val, gate_val, *weights)
    flops = 6 * L * D * units
    return line.call(ffn_back_kernel, outs, ins, flops=flops, scratch=scratch)


def split_blocks(blocks, first, send_ref, keep_ref, start):
    size = blocks[0].shape[0]
    for j in range(0, len(blocks), 2):
        rows = slice(start + j // 2 * size, start + (j // 2 + 1) * size)
        even, odd = blocks[j], blocks[j + 1]
        send_ref[rows] = jnp.where(first, odd, even)
        keep_ref[rows] = jnp.where(first, even, odd)


def collect_kernel(far, info, *refs):
    parts, (ones_far, ones_t_far, ones, ones_t, in_sems, out_sems) = refs[:far], refs[far:]
    rows = parts[0].shape[0]
    come, go = Copies(in_sems), Copies(out_sems)
    for k, part in enumerate(parts):
        come.start(part, ones.at[pl.ds((info[PLACE_FAR] ^ k) * rows, rows)])
    come.wait()
    go.start(ones, ones_far)
    turn_part(far, info, ones, ones_t)
    go.start(ones_t, ones_t_far)
    go.wait()


def collect(line, info, parts):
    far, rows = len(parts), len(parts) * parts[0].shape[0]
    outs = (distant(rows, D, BF), distant(D // far, rows, BF))
    scratch = [vmem(rows, D, BF), vmem(D // far, rows, BF), sems(far), sems(2)]
    return line.call(
        functools.partial(collect_kernel, far),
        outs,
        (info, *parts),
        scratch=scratch,
        vmem=6,
        smem=1,
        loose=range(1, 1 + far),
        sent=(0, 1),
    )


def unit_factors_kernel(ones_far, up_far, gate_far, up_s, gate_s, *refs):
    far, (ones, up_w, gate_w), kept, (in_sems, out_sems) = refs[:3], refs[3:6], refs[6:9], refs[9:]
    go = Copies(out_sems)
    tiles = unit_tiles(up_w.shape[1], 512)
    groups = [((ones_far, ones),)]
    for cols in tiles:
        groups.append(
            ((up_far.at[:, cols], up_w.at[:, cols]), (gate_far.at[:, cols], gate_w.at[:, cols]))
        )
    arrive = Tiles(Copies(in_sems), groups, 3)
    arrive.wait(0)
    for i, cols in enumerate(tiles):
        arrive.wait(1 + i)
        up_scale, gate_scale = up_s[:, cols], gate_s[:, cols]
        up_val, gate_val = dot(ones[...], up_w[:, cols]), dot(ones[...], gate_w[:, cols])
        inner, sigma, swish = swiglu_of(up_val, gate_val, up_scale, gate_scale)
        kept[0][:, cols] = inner
        kept[1][:, cols] = (up_scale * swish).astype(BF)
        slope = sigma + swish * (1.0 - sigma)
        kept[2][:, cols] = (up_scale * (gate_scale * ROOT) * up_val * slope).astype(BF)
        for source, target in zip(kept, far):
            go.start(source.at[:, cols], target.at[:, cols])
    go.wait()


def turn_part(far, info, source, target):
    group = target.shape[0]
    for j in range(far):

        @pl.when(info[PLACE_FAR] == j)
        def _(j=j):
            target[...] = source[:, j * group : (j + 1) * group].T


def unit_factors(line, ones, weights):
    rows, units = ones.shape[0], weights[0].shape[1]
    outs = [distant(rows, units, BF)] * 3
    scratch = [vmem(rows, D, BF), vmem(D, units, BF), vmem(D, units, BF)]
    scratch += [vmem(rows, units, BF)] * 3 + [sems(1 + 2 * units // 512), sems(3 * units // 512)]
    return line.call(
        unit_factors_kernel,
        outs,
        (ones, weights[0], weights[1], weights[3], weights[4]),
        flops=4 * rows * D * units,
        scratch=scratch,
        vmem=36,
        away=(0, 1, 2),
        sent=(0, 1, 2),
    )


def ffn_grad_kernel(far, info, *refs):
    parts, (ones_t_far, down_far), refs = refs[:far], refs[far : far + 2], refs[far + 2 :]
    factors_far, (send, keep), refs = refs[:3], refs[3:5], refs[5:]
    ones_t, d_ffns, d_ffns_t, down_w, *factors, in_sems = refs
    rows = parts[0].shape[0]
    tiles = unit_tiles(down_w.shape[0], 512)
    first = [
        (part, d_ffns.at[pl.ds((info[PLACE_FAR] ^ k) * rows, rows)]) for k, part in enumerate(parts)
    ]
    groups = [[*first, (ones_t_far, ones_t)]]
    for cols in tiles:
        group = [(down_far.at[cols], down_w.at[cols])]
        group += [(a.at[:, cols], b.at[:, cols]) for a, b in zip(factors_far, factors)]
        groups.append(group)
    arrive = Tiles(Copies(in_sems), groups, 3)
    arrive.wait(0)
    turn_part(far, info, d_ffns, d_ffns_t)
    size = ones_t.shape[0] // 4
    for i, cols in enumerate(tiles):
        arrive.wait(1 + i)
        d_inner = dot_nt(d_ffns[...], down_w[cols])
        inner, to_up, to_gate = (factor[:, cols] for factor in factors)
        d_up = (d_inner * to_up.astype(F32)).astype(BF)
        d_gate = (d_inner * to_gate.astype(F32)).astype(BF)
        for k, (left, right) in enumerate(((ones_t, d_up), (ones_t, d_gate), (d_ffns_t, inner))):
            grad = dot(left[...], right).astype(BF)
            blocks = [grad[j * size : (j + 1) * size] for j in range(4)]
            split_blocks(blocks, info[CORE] == 0, send.at[:, cols], keep.at[:, cols], k * 2 * size)


def ffn_grad(line, info, parts, down_weight, ones_t, factors):
    far, units = len(parts), down_weight.shape[0]
    rows, group = far * parts[0].shape[0], D // far
    outs = [distant(3 * group // 2, units, BF)] * 2
    scratch = [vmem(group, rows, BF), vmem(rows, D, BF), vmem(group, rows, BF), vmem(units, D, BF)]
    scratch += [vmem(rows, units, BF)] * 3 + [sems(far + 1 + 4 * units // 512)]
    return line.call(
        functools.partial(ffn_grad_kernel, far),
        outs,
        (info, *parts, ones_t, down_weight, *factors),
        flops=2 * rows * (D + 3 * group) * units,
        scratch=scratch,
        vmem=36,
        smem=1,
        loose=range(1, 1 + far),
        away=range(1 + far, 6 + far),
    )


def plain_unit_grads(low, d_ffn, weights):
    up_w, gate_w, down_w, up_s, gate_s = weights
    up_val = dot(low, up_w)
    inner, sigma, swish = swiglu_of(up_val, dot(low, gate_w), up_s, gate_s)
    d_up, _, d_gate = swiglu_back(dot_nt(d_ffn, down_w), up_val, sigma, swish, up_s, gate_s)
    return dot_tn(low, d_up), dot_tn(low, d_gate), dot_tn(d_ffn, inner)


def turn_kernel(source, result):
    result[...] = source[...].T


def turn(line, value):
    rows, cols = value.shape
    value = pltpu.with_memory_space_constraint(value, pltpu.HBM)
    return line.call(turn_kernel, (distant(cols, rows, value.dtype),), (value,))[0]


def give(split, info, products, outs, done=lambda rows: None):
    for i, (left, right) in enumerate(products):
        grad = dot(left, right[...]).astype(BF)
        if split:
            size = D // 16
            blocks = [grad[j * size : (j + 1) * size] for j in range(16)]
            split_blocks(blocks, info[CORE] == 0, outs[0], outs[1], i * 8 * size)
            done(slice(i * 8 * size, (i + 1) * 8 * size))
        else:
            outs[i][...] = grad


BACK_INPUTS = (
    ("d_mine", BF),
    ("dmix_two", F32),
    ("one", F32),
    ("sums", F32),
    ("x_cont", BF),
    ("wo", BF),
    ("kr", F32),
    ("qr", F32),
    ("v", BF),
    ("queries", BF),
    ("keys", BF),
    ("probs", BF),
    ("gains", F32),
    ("x_t", BF),
    ("att", BF),
)


def attention_back_kernel(split, info, _, d_other, rate_two, rate_one, scale_ref, *refs):
    count = len(BACK_INPUTS)
    made = 2 if split else 4
    far, outs = refs[:count], refs[count : count + made]
    dq_far, dk_far, dv_far, residual_far, gains_out, _ = refs[count + made : count + made + 6]
    held, refs = refs[count + made + 6 : -9], refs[-9:]
    d_att, dq_ref, dk_ref, dv_ref, residual_ref, send_ref, keep_ref, in_sems, out_sems = refs
    come, go = Copies(in_sems), Copies(out_sems)
    ref = {}
    arrived = {}
    pairs = {}
    for (name, _), source, target in zip(BACK_INPUTS, far, held):
        ref[name] = target
        pairs[name] = (source.at[P_SIZE:] if name == "x_cont" else source, target)

    def begin(*names):
        for name in names:
            arrived[name] = come.start(*pairs[name]).wait

    begin("d_mine", "dmix_two", "one", "sums", "x_cont", "wo")

    for name in ("d_mine", "dmix_two", "one", "sums", "x_cont"):
        arrived[name]()
    begin("v", "probs", "queries", "keys", "kr", "qr", "gains", "att", "x_t")
    old = ref["x_cont"][...].astype(F32)
    _, unit_in, inverse_in, inverse_out = mix(old, ref["sums"][...], rate_one[...])
    d_one = both(ref["d_mine"][...], d_other[...])
    d_one = d_one + (1.0 - rate_two[...]) * ref["dmix_two"][...]
    dmix = norm_back(d_one, ref["one"][...], inverse_out)
    residual_ref[...] = dmix * (1.0 - rate_one[...])
    go.start(residual_ref, residual_far)
    att_grad = jnp.sum(dmix * (unit_in - old), axis=0, keepdims=True)
    d_attn = norm_back(dmix * rate_one[...], unit_in, inverse_in).astype(BF)
    arrived["wo"]()
    d_att[...] = dot_nt(d_attn, ref["wo"][...]).astype(BF)

    gains = ref["gains"]
    width = scale_ref.shape[1]
    arrived["gains"]()
    for i in range(D // width):
        gains[2 + i : 3 + i] = att_grad[:, i * width : (i + 1) * width]

    def raw_back(grad, unit, inverse, scale):
        scaled = grad * scale
        back = inverse * (scaled - unit * head_sums(scaled * unit))
        return back.astype(BF), jnp.sum(grad * unit, axis=0, keepdims=True)

    for name in ("v", "probs", "queries", "keys", "kr", "qr"):
        arrived[name]()
    pairs = [slice(start, start + PAIR) for start in range(0, width, PAIR)]
    probs = [ref["probs"][2 * L * i : 2 * L * (i + 1)] for i in range(len(pairs))]
    grads = [halves(d_att[:, cols]) for cols in pairs]
    d_probs = [dot_nt(grad, ref["v"][:, cols]) for grad, cols in zip(grads, pairs)]
    d_scores = []
    for prob, d_prob in zip(probs, d_probs):
        prob = prob.astype(F32)
        delta = jnp.sum(d_prob * prob, axis=1, keepdims=True)
        d_scores.append((prob * (d_prob - delta)).astype(BF))
    for prob, grad, cols in zip(probs, grads, pairs):
        dv_ref[:, cols] = dot_tn(prob, grad).astype(BF)
    for d_score, cols in zip(d_scores, pairs):
        scale = scale_ref[:, cols]
        q_unit, q_inverse = unit_heads(ref["qr"][:, cols])
        k_unit, k_inverse = unit_heads(ref["kr"][:, cols])
        d_query = 8.0 * merge(dot(d_score, ref["keys"][:, cols]))
        d_keys = 8.0 * dot_tn(d_score, halves(ref["queries"][:, cols]))
        dq_ref[:, cols], by_query = raw_back(d_query, q_unit, q_inverse, scale)
        dk_ref[:, cols], by_key = raw_back(d_keys, k_unit, k_inverse, scale)
        gains[12:13, cols] = by_query + by_key
    for source, target in ((dq_ref, dq_far), (dk_ref, dk_far), (dv_ref, dv_far)):
        go.start(source, target)

    arrived["x_t"]()
    arrived["att"]()
    x_t = ref["x_t"]
    products = (
        (x_t[...], dv_ref),
        (x_t[...], dk_ref),
        (x_t[:, P_SIZE:], dq_ref),
        (d_attn.T, ref["att"]),
    )
    gains_out[...] = gains[...]
    if split:
        far, outs = outs, (send_ref, keep_ref)

        def done(rows):
            for source, target in zip(outs, far):
                go.start(source.at[rows], target.at[rows])

        for out in outs:
            out[2 * D :] = gains[...].astype(BF)
        done(slice(2 * D, 2 * D + GAINS))
        give(split, info, products, outs, done)
    else:
        give(split, info, products, outs)
    go.wait()


def attention_back(line, split, info, passed, d_other, rate_two, rate_one, scale, ins):
    width = scale.shape[1]
    rows = ins["v"].shape[0]
    outs = [distant(2 * D + GAINS, width, BF)] * 2 if split else [shape(D, width, BF)] * 4
    first = len(outs)
    outs += [distant(L, width, BF), distant(rows, width, BF), distant(rows, width, BF)]
    outs += [distant(L, D, F32), shape(GAINS, width, F32), shape(*passed.shape, BF)]
    scratch = []
    for name, kind in BACK_INPUTS:
        scratch.append(vmem(L if name == "x_cont" else ins[name].shape[0], ins[name].shape[1], kind))
    scratch += [vmem(L, width, BF), vmem(L, width, BF), vmem(rows, width, BF), vmem(rows, width, BF)]
    scratch += [vmem(L, D, F32)] + [vmem(2 * D + GAINS if split else GAINS, width, BF)] * 2
    scratch += [sems(len(BACK_INPUTS)), sems(14)]
    flops = 20 * L * rows * width + 4 * (rows + L) * D * width + 4 * L * D * width
    return line.call(
        functools.partial(attention_back_kernel, split),
        outs,
        (info, passed, d_other, rate_two, rate_one, scale, *(ins[name] for name, _ in BACK_INPUTS)),
        flops=flops,
        scratch=scratch,
        vmem=50,
        smem=1,
        away=range(6, 6 + len(BACK_INPUTS)),
        loose=(1,),
        sent=(*range(2 if split else 0), first, first + 1, first + 2, first + 3, first + 5),
        aliases={1: first + 5},
    )


def fold_core_kernel(info, keep, got, *outs):
    size = D // 16
    total = (keep[...].astype(F32) + got[...].astype(F32)).astype(BF)
    for m in range(4):
        start = m * 8 * size
        blocks = [total[start + j * size : start + (j + 1) * size] for j in range(8)]
        send, kept = outs[:2] if m < 2 else outs[2:]
        split_blocks(blocks, info[PLACE_X] == 0, send, kept, m % 2 * 4 * size)
    for ref in outs[:2]:
        ref[8 * size :] = total[32 * size :]


def fold_kernel(matrices, count, bit, info, keep, got, send, kept):
    size = D // 16
    low = info[PLACE_FAR] // bit % 2 == 0
    total = (keep[...].astype(F32) + got[...].astype(F32)).astype(BF)
    half = count // 2
    for m in range(matrices):
        first = total[m * count * size : (m * count + half) * size]
        second = total[(m * count + half) * size : (m + 1) * count * size]
        rows = slice(m * half * size, (m + 1) * half * size)
        send[rows] = jnp.where(low, second, first)
        kept[rows] = jnp.where(low, first, second)
    if keep.shape[0] > matrices * count * size:
        for ref in (send, kept):
            ref[matrices * half * size :] = total[matrices * count * size :]


def finish_first_kernel(tokens, keep, got, *outs):
    value, key, mlp, att, up, gate, head, loss, factor_ref = outs
    size = value.shape[0]
    total = keep[...].astype(F32) + got[...].astype(F32)
    gains = total[2 * size :]
    factor = tokens / (gains[13:14, 2:3] + gains[13:14, 3:4])
    factor_ref[...] = factor
    loss[...] = factor * (gains[13:14, 0:1] + gains[13:14, 1:2])
    gains = gains * factor
    width = gains.shape[1]
    place = 0
    for ref in (mlp, att, up, gate, head):
        for start in range(0, ref.shape[1], width):
            ref[:, start : start + width] = gains[place : place + 1]
            place += 1
    value[...] = total[:size] * factor
    key[...] = total[size : 2 * size] * factor


def fold_units_kernel(info, keep, got, send_ref, keep_ref):
    size = keep.shape[0] // 6
    total = (keep[...].astype(F32) + got[...].astype(F32)).astype(BF)
    blocks = [total[j * size : (j + 1) * size] for j in range(6)]
    split_blocks(blocks, info[PLACE_X] == 0, send_ref, keep_ref, 0)


def finish_rest_kernel(factor, keep, got, u_keep, u_got, query, out, *results):
    size = query.shape[0]
    total = (keep[...].astype(F32) + got[...].astype(F32)) * factor[...]
    query[...] = total[:size]
    out[...] = total[size:]
    total = (u_keep[...].astype(F32) + u_got[...].astype(F32)) * factor[...]
    size = total.shape[0] // 3
    for m, result in enumerate(results):
        result[...] = total[m * size : (m + 1) * size]


def rows_kernel(info, dq_far, dk_far, dv_far, wq_far, wk_far, wv_far, send_ref, keep_ref, *refs):
    wq, wk, wv, dq, dk, dv, in_sems = refs
    groups = (
        ((dk_far, dk), (wk_far, wk)),
        ((dv_far, dv), (wv_far, wv)),
        ((dq_far, dq), (wq_far, wq)),
    )
    arrive = Tiles(Copies(in_sems), groups)
    half = send_ref.shape[0]
    arrive.wait(0)
    prompt = dot_nt(dk[...], wk[...])
    arrive.wait(1)
    prompt = prompt + dot_nt(dv[...], wv[...])
    arrive.wait(2)
    top = prompt[:half].astype(BF)
    low = jnp.concatenate(
        [prompt[half:P_SIZE], prompt[P_SIZE:] + dot_nt(dq[...], wq[...])], 0
    ).astype(BF)
    first = info[SIDE] == 0
    send_ref[...] = jnp.where(first, low, top)
    keep_ref[...] = jnp.where(first, top, low)


def share_kernel(info, keep, got, residual, kept_ref, sent_ref):
    half = keep.shape[0]
    total = keep[...].astype(F32) + got[...].astype(F32)
    row = lax.broadcasted_iota(jnp.int32, (half, 1), 0) + info[SIDE] * half
    away = (row < P_SIZE) & (info[OWN] == 0)
    sent_ref[...] = jnp.where(away, total, 0.0).astype(BF)
    kept_ref[...] = jnp.where(away, 0.0, total)
    kept_ref[half - L :] += jnp.where(info[SIDE] == 1, residual[...], 0.0)


def last_share_kernel(kept, got, factor, result):
    result[...] = (kept[...] + got[...].astype(F32)) * factor[...]


def last_mix_kernel(one_far, rate, out_far, *refs):
    *parts, result_far, one, result, in_sems, out_sems = refs
    come, go = Copies(in_sems), Copies(out_sems)
    count = len(parts) // 2
    size = P_SIZE // count
    slices = [slice(i * size, (i + 1) * size) for i in range(count)]
    for rows in slices:
        come.start(one_far.at[rows], one.at[rows])
    come.start(out_far, result.at[P_SIZE:])
    for i, rows in enumerate(slices):
        come.copies[i].wait()
        result[rows] = mix(one[rows], both(parts[i][...], parts[count + i][...]), rate[...])[0]
        go.start(result.at[rows], result_far.at[rows])
    come.copies[-1].wait()
    go.start(result.at[P_SIZE:], result_far.at[P_SIZE:])
    go.wait()


def local(
    hidden_in,
    query_weight,
    key_weight,
    value_weight,
    out_weight,
    up_weight,
    gate_weight,
    down_weight,
    head_scale,
    attention_rate,
    up_scale,
    gate_scale,
    swiglu_rate,
    teacher,
    valid_mask,
    group_ids,
):
    count_dp = lax.axis_size("dp")
    far = count_dp // 4
    split = far == 4
    me = lax.axis_index("dp")
    rows = hidden_in.shape[0]
    width = query_weight.shape[1]
    units = up_weight.shape[1]
    scale = head_scale.reshape(1, width)
    rate_one = attention_rate.reshape(1, D)
    rate_two = swiglu_rate.reshape(1, D)
    own = (group_ids[0] == me).astype(jnp.int32)
    info = jnp.stack([own, me % 2, me // 2 % 2, me // 4, lax.axis_index("tensor")])
    info = info.astype(jnp.int32)
    qkvo = (query_weight, key_weight, value_weight, out_weight)
    ffn_weights = (
        up_weight,
        gate_weight,
        down_weight,
        up_scale.reshape(1, units),
        gate_scale.reshape(1, units),
    )

    line = Line()

    other_x = swap(hidden_in, "dp", 1)
    a_mine, att, x_seen, values, query_raw, key_raw, queries, keys, probs, *qkvo_near = cont_attention(
        line, info, hidden_in, other_x, qkvo, scale
    )
    a_other = swap(a_mine, "tensor", 1)
    p_mine, *ffn_near = prompt_attention(line, hidden_in, qkvo_near, scale, ffn_weights[:3])
    ffn_near = (*ffn_near, *ffn_weights[3:])
    m_mine, one_low, up_val, gate_val, one_near, attn_sums, one = ffn(
        line, a_mine, a_other, hidden_in, rate_one, ffn_near
    )
    m_other = swap(m_mine, "tensor", 1)
    x_seen_t = turn(line, x_seen)
    d_mine, d_ffn, out, dmix_two, gains = ffn_back(
        line,
        m_mine,
        m_other,
        one_near,
        rate_two,
        teacher,
        valid_mask.reshape(1, L),
        up_val,
        gate_val,
        ffn_near,
        width,
    )
    total_cont = count_dp * valid_mask.shape[0]
    mine = D // count_dp
    usual = group_ids[0] >= 0
    half_rows = shape(rows // 2, D, BF)

    d_other = swap(d_mine, "tensor", 1)
    if split:
        ones = [one_low]
        bit = 4
        while bit < count_dp:
            ones += [swap(part, "dp", bit) for part in ones]
            bit *= 2
        ones, ones_t = collect(line, info, ones)
    *first, d_query, d_key, d_value, residual, gains, p_mine = attention_back(
        line,
        split,
        info,
        p_mine,
        d_other,
        rate_two,
        rate_one,
        scale,
        {
            "d_mine": d_mine,
            "dmix_two": dmix_two,
            "one": one,
            "sums": attn_sums,
            "x_cont": hidden_in,
            "wo": out_weight,
            "kr": key_raw,
            "qr": query_raw,
            "v": values,
            "queries": queries,
            "keys": keys,
            "probs": probs,
            "gains": gains,
            "x_t": x_seen_t,
            "att": att,
        },
    )

    p_other = swap(p_mine, "tensor", 1)

    def fold(line, send, keep, count, bit, before=()):
        more = keep.shape[0] - 2 * count * mine

        def kernel(info, keep, send, *refs):
            fold_kernel(2, count, bit, info, keep, send, *refs[len(before) :])

        return line.call(
            kernel,
            [shape(count * mine + more, width, BF)] * 2,
            (info, keep, send, *before),
            smem=1,
            loose=range(3, 3 + len(before)),
        )

    def rows_step(info, before, first, d_query, d_key, d_value, ones):
        inner = Line(before)
        if split:
            got = swap(first[0], "dp", 1)
        rows_pair = inner.call(
            rows_kernel,
            (half_rows, half_rows),
            (info, d_query, d_key, d_value, query_weight, key_weight, value_weight),
            flops=6 * rows * D * width,
            scratch=[vmem(D, width, BF)] * 3
            + [vmem(L, width, BF)]
            + [vmem(rows, width, BF)] * 2
            + [sems(6)],
            vmem=24,
            smem=1,
            away=(1, 2, 3, 4, 5, 6),
        )
        if not split:
            return first, rows_pair, (), inner.last
        send_a, keep_a, send_b, keep_b = inner.call(
            fold_core_kernel,
            [shape(D // 2 + GAINS, width, BF)] * 2 + [shape(D // 2, width, BF)] * 2,
            (info, first[1], got),
            smem=1,
        )
        got_a = swap(send_a, "dp", 2)
        factors = unit_factors(inner, ones, ffn_weights)
        send_a, keep_a = fold(inner, got_a, keep_a, 4, 2)
        return (send_a, keep_a, send_b, keep_b), rows_pair, factors, inner.last

    if not split:
        ones = one_low
    first, (rows_sent, kept), factors, line.last = section(
        usual, rows_step, info, line.last, first, d_query, d_key, d_value, ones
    )
    share = swap(rows_sent, "tensor", 1)
    if split:
        send_a, keep_a, send_b, keep_b = first
        got_b = swap(send_b, "dp", 2)
        d_ffns = [d_ffn] + [swap(d_ffn, "dp", 4 * k) for k in range(1, far)]
        u_send, u_keep = ffn_grad(line, info, d_ffns, down_weight, ones_t, factors)
    else:
        u_send = u_keep = send_a = keep_a = None

    def middle_step(info, before, p_mine, p_other, share_keep, share, residual, u_send, u_keep, send_a, keep_a):
        inner = Line(before)
        if split:
            u_got, got_a = swap(u_send, "dp", 1), swap(send_a, "dp", 8)
        kept, sent = inner.call(
            share_kernel,
            (distant(rows // 2, D, F32), half_rows),
            (info, share_keep, share, residual),
            smem=1,
        )
        share = swap(sent, "dp", 1)
        prompt = prompt_ffn(inner, p_mine, p_other, hidden_in, rate_one, ffn_weights)
        if split:
            u_send, u_keep = inner.call(
                fold_units_kernel,
                (shape(3 * mine, units, BF),) * 2,
                (info, u_keep, u_got),
                smem=1,
            )
            send_a, keep_a = fold(inner, got_a, keep_a, 2, 1)
        return kept, share, prompt, u_send, u_keep, send_a, keep_a, inner.last

    kept, share, (one_p, *mp_mine), u_send, u_keep, send_a, keep_a, line.last = section(
        usual,
        middle_step,
        info,
        line.last,
        p_mine,
        p_other,
        kept,
        share,
        residual,
        u_send,
        u_keep,
        send_a,
        keep_a,
    )
    mp_other = [swap(part, "tensor", 1) for part in mp_mine]
    if split:
        u_got = swap(u_send, "dp", 2)
        got_a = swap(send_a, "dp", 4)
        send_b, keep_b = fold(line, got_b, keep_b, 4, 2)
        got_b = swap(send_b, "dp", 8)
    if split:
        value_grad, key_grad, mlp, att_rate, up_g, gate_g, head, loss, factor = line.call(
            functools.partial(finish_first_kernel, total_cont),
            [distant(mine, width, F32)] * 2
            + [shape(1, n, F32) for n in (D, D, units, units, width, 1, 1)],
            (keep_a, got_a),
        )
    else:
        total = sum_all(gains)
        factor = total_cont / (total[13:14, 2:3] + total[13:14, 3:4])
        loss = factor * (total[13:14, 0:1] + total[13:14, 1:2])
        flat = (total * factor).reshape(-1)
        mlp, att_rate, up_g, gate_g, head = (
            flat[start : start + size]
            for start, size in (
                (0, D),
                (D, D),
                (2 * D, units),
                (2 * D + units, units),
                (2 * D + 2 * units, width),
            )
        )
        flat = [head, att_rate, up_g, gate_g, mlp]

        def scattered(grad):
            grad = grad.astype(F32)
            return factor * lax.psum_scatter(grad, "dp", scatter_dimension=0, tiled=True)

        value_grad, key_grad, query_grad, out_grad = (scattered(grad) for grad in first)
        up_grad, gate_grad, down_grad = (
            scattered(grad) for grad in plain_unit_grads(one_low, d_ffn, ffn_weights)
        )
    grad_hidden = line.call(
        last_share_kernel, (distant(rows // 2, D, F32),), (kept, share, factor), held=(0,)
    )[0]
    if split:
        flat = [value.reshape(-1) for value in (head, att_rate, up_g, gate_g, mlp)]
        send_b, keep_b = fold(line, got_b, keep_b, 2, 1, flat)
        got_b = swap(send_b, "dp", 4)
    hidden_out = line.call(
        last_mix_kernel,
        (distant(rows, D, F32),),
        (one_p, rate_two, out, *mp_mine, *mp_other),
        scratch=[vmem(P_SIZE, D, F32), vmem(P_SIZE + L, D, F32), sems(3), sems(3)],
        away=(0, 2),
        sent=(0,),
    )[0]
    if split:
        query_grad, out_grad, up_grad, gate_grad, down_grad = line.call(
            finish_rest_kernel,
            [distant(mine, width, F32)] * 2 + [distant(mine, units, F32)] * 3,
            (factor, keep_b, got_b, u_keep, u_got),
        )
    return (
        hidden_out,
        loss[0, 0],
        grad_hidden,
        query_grad,
        key_grad,
        value_grad,
        out_grad.T,
        up_grad,
        gate_grad,
        down_grad.T,
        *flat,
    )


def solution(mesh):
    placed = (
        P("dp", None),
        P(None, "tensor"),
        P(None, "tensor"),
        P(None, "tensor"),
        P("tensor", None),
        P(None, "tensor"),
        P(None, "tensor"),
        P("tensor", None),
        P("tensor"),
        P(),
        P("tensor"),
        P("tensor"),
        P(),
        P("dp", None),
        P("dp"),
        P("dp"),
    )
    return jax.shard_map(
        local,
        mesh=mesh,
        in_specs=placed,
        out_specs=(
            P("dp", None),
            P(),
            P(("dp", "tensor"), None),
            P("dp", "tensor"),
            P("dp", "tensor"),
            P("dp", "tensor"),
            P("tensor", "dp"),
            P("dp", "tensor"),
            P("dp", "tensor"),
            P("tensor", "dp"),
            P("tensor"),
            P(),
            P("tensor"),
            P("tensor"),
            P(),
        ),
        check_vma=False,
    )
```
